32 devices in a mesh: grp: 8 (over y, x, core), lag: 4 (over z).
Axes of the slice: x: 2, y: 2, z: 4, core: 2. Of those that a mesh axis runs over, the one named last changes fastest.
Arguments:
- weights: bfloat16 [3, 16384, 256], P(None, 'lag'), may hold values from -0.125 to 0.125
- history: bfloat16 [128, 2048, 256], P(('grp', 'lag')), may hold values from -6 to 6
- send_patch: int32 [256, 2], P(('grp', 'lag')), may hold values from 0 to 3
- send_lag: int32 [256, 2], P(('grp', 'lag')), may hold values from 0 to 56
- send_class: int32 [256, 2], P(('grp', 'lag')), may hold values from 0 to 2
- recv_target: int32 [256, 2], P(('grp', 'lag')), may hold values from 0 to 3
- local_src: int32 [1536], P(('grp', 'lag')), may hold values from 0 to 3
- local_lag: int32 [1536], P(('grp', 'lag')), may hold values from 0 to 56
- local_class: int32 [1536], P(('grp', 'lag')), may hold values from 0 to 2
- local_target: int32 [1536], P(('grp', 'lag')), may hold values from 0 to 3
- inverse_blocks: bfloat16 [128, 256, 256], P(('grp', 'lag')), may hold values from -0.375 to 0.375
- incident: bfloat16 [128, 256, 256], P(('grp', 'lag')), may hold values from -6 to 6
Outputs:
- density: bfloat16 [128, 256, 256], P(('grp', 'lag'))
The draws below stay inside these ranges and needn't reach their ends.
All inputs are finite; a program needn't handle non-finite values.
Results may differ from the reference program's by a relative error of at most 0.0049.
Values may be sent and summed in bfloat16 or wider, within the bound.
No kernel may reach another device: no remote copies, remote signals or barrier semaphores. Data moves between devices by JAX's collectives and lax.ppermute only.
A program may use at most 256 MiB of HBM per device.

```python
import jax
import jax.numpy as jnp
from jax import lax

P_SIZE = 256
C = 256
M = 8
LAGS = 64
CLASSES = 3
PD = 4
CAP = 2
NLOC = 48
PATCHES = 128
N_GRP = 8
N_LAG = 4


def with_ends(values, rng, smallest, top_value):
    place = [jax.random.randint(jax.random.fold_in(rng, axis), (), 0, length) for axis, length in enumerate(values.shape)]
    main_axis = values.shape.index(max(values.shape))
    beside = place[:main_axis] + [(place[main_axis] + 1) % values.shape[main_axis]] + place[main_axis + 1:]
    return values.at[tuple(place)].set(smallest).at[tuple(beside)].set(top_value)


def levels(key, shape, cuts, smallest, top_value):
    gain, own = 1.0, jax.random.fold_in(key, 6)
    for position, blocks in cuts:
        heights = jnp.exp(jax.random.uniform(jax.random.fold_in(own, position), (blocks,), jnp.float32, smallest / len(cuts), top_value / len(cuts)))
        gain = gain * jnp.repeat(heights, shape[position] // blocks).reshape([-1 if axis == position else 1 for axis in range(len(shape))])
    return gain


def gaussian(own_key, dims, spread, reach, shards=(), kind=jnp.bfloat16):
    array = jax.random.normal(own_key, dims, jnp.float32) * spread
    if len(shards) > 0:
        array = levels(own_key, dims, shards, -0.22, 0.18) * array
    return jnp.clip(array, min=-reach, max=reach).astype(kind)


def setup_inputs(seed: int = 0) -> dict:
    keys = jax.random.split(jax.random.key(seed), 13)
    weights = gaussian(keys[0], (CLASSES, LAGS * P_SIZE, P_SIZE), (M * P_SIZE) ** -0.5, 0.125, ((1, 4),))
    history = gaussian(keys[1], (PATCHES, M * P_SIZE, C), 1.0, 6.0, ((0, 32),))
    send_patch = with_ends(jax.random.randint(keys[2], (N_GRP * N_LAG * N_GRP, CAP), 0, PD), jax.random.fold_in(keys[2], 1), 0, PD - 1).astype(jnp.int32)
    send_lag = with_ends(jax.random.randint(keys[3], (N_GRP * N_LAG * N_GRP, CAP), 0, LAGS - M + 1), jax.random.fold_in(keys[3], 1), 0, LAGS - M).astype(jnp.int32)
    send_class = with_ends(jax.random.randint(keys[4], (N_GRP * N_LAG * N_GRP, CAP), 0, CLASSES), jax.random.fold_in(keys[4], 1), 0, CLASSES - 1).astype(jnp.int32)
    recv_target = with_ends(jax.random.randint(keys[5], (N_GRP * N_LAG * N_GRP, CAP), 0, PD), jax.random.fold_in(keys[5], 1), 0, PD - 1).astype(jnp.int32)
    local_src = with_ends(jax.random.randint(keys[6], (N_GRP * N_LAG * NLOC,), 0, PD), jax.random.fold_in(keys[6], 1), 0, PD - 1).astype(jnp.int32)
    local_lag = with_ends(jax.random.randint(keys[7], (N_GRP * N_LAG * NLOC,), 0, LAGS - M + 1), jax.random.fold_in(keys[7], 1), 0, LAGS - M).astype(jnp.int32)
    local_class = with_ends(jax.random.randint(keys[8], (N_GRP * N_LAG * NLOC,), 0, CLASSES), jax.random.fold_in(keys[8], 1), 0, CLASSES - 1).astype(jnp.int32)
    local_target = with_ends(jax.random.randint(keys[9], (N_GRP * N_LAG * NLOC,), 0, PD), jax.random.fold_in(keys[9], 1), 0, PD - 1).astype(jnp.int32)
    inverse_blocks = gaussian(keys[10], (PATCHES, P_SIZE, P_SIZE), P_SIZE ** -0.5, 0.375, ((0, 32),))
    incident = gaussian(keys[11], (PATCHES, P_SIZE, C), 1.0, 6.0, ((0, 32),))
    return dict(weights=weights, history=history, send_patch=send_patch, send_lag=send_lag, send_class=send_class, recv_target=recv_target, local_src=local_src, local_lag=local_lag, local_class=local_class, local_target=local_target, inverse_blocks=inverse_blocks, incident=incident)


def pair_blocks(weights_full, hist_rows, classes, offsets):
    def window(klass, offset):
        return lax.dynamic_slice(weights_full, (klass, offset * P_SIZE, jnp.int32(0)), (1, M * P_SIZE, P_SIZE))[0]
    blocks = jax.vmap(window)(classes.astype(jnp.int32), offsets.astype(jnp.int32))
    return jnp.einsum("bkp,bkc->bpc", blocks, hist_rows, precision=lax.Precision.HIGHEST)


def reference(weights, history, send_patch, send_lag, send_class, recv_target, local_src, local_lag, local_class, local_target, inverse_blocks, incident):
    devices = N_GRP * N_LAG
    weights_full = weights.astype(jnp.float32)
    owner = jnp.arange(devices, dtype=jnp.int32)
    local_s = (owner[:, None] * PD + local_src.reshape(devices, NLOC)).astype(jnp.int32)
    local_o = local_lag.reshape(devices, NLOC).astype(jnp.int32)
    local_k = local_class.reshape(devices, NLOC).astype(jnp.int32)
    local_t = (owner[:, None] * PD + local_target.reshape(devices, NLOC)).astype(jnp.int32)
    sender = owner.reshape(N_GRP, N_LAG, 1, 1)
    peer_grp = jnp.arange(N_GRP, dtype=jnp.int32).reshape(1, 1, N_GRP, 1)
    lane_idx = jnp.arange(N_LAG, dtype=jnp.int32).reshape(1, N_LAG, 1, 1)
    remote_s = sender * PD + send_patch.reshape(N_GRP, N_LAG, N_GRP, CAP)
    remote_o = send_lag.reshape(N_GRP, N_LAG, N_GRP, CAP)
    remote_k = send_class.reshape(N_GRP, N_LAG, N_GRP, CAP)
    targets_back = jnp.transpose(recv_target.reshape(N_GRP, N_LAG, N_GRP, CAP), (2, 1, 0, 3))
    remote_t = (peer_grp * N_LAG + lane_idx) * PD + targets_back
    all_s = jnp.concatenate([local_s, remote_s.reshape(devices, N_GRP * CAP).astype(jnp.int32)], 1)
    all_o = jnp.concatenate([local_o, remote_o.reshape(devices, N_GRP * CAP).astype(jnp.int32)], 1)
    all_k = jnp.concatenate([local_k, remote_k.reshape(devices, N_GRP * CAP).astype(jnp.int32)], 1)
    all_t = jnp.concatenate([local_t, remote_t.reshape(devices, N_GRP * CAP).astype(jnp.int32)], 1)

    def advance(near_sum, inputs):
        sources, classes, offsets, targets = inputs
        hist_rows = history[sources].astype(jnp.float32)
        contrib = pair_blocks(weights_full, hist_rows, classes, offsets)
        return near_sum.at[targets].add(contrib), None

    near0 = jnp.zeros((history.shape[0], P_SIZE, C), jnp.float32)
    near_sum, _ = lax.scan(advance, near0, (all_s, all_k, all_o, all_t))
    residual = (incident.astype(jnp.float32) - near_sum).astype(jnp.bfloat16)
    density = jnp.einsum("tpq,tqc->tpc", inverse_blocks.astype(jnp.float32), residual.astype(jnp.float32), precision=lax.Precision.HIGHEST)
    return density.astype(jnp.bfloat16)
```

```python
import functools

import jax
import jax.numpy as jnp
from jax import lax
from jax.experimental import pallas as pl
from jax.experimental.pallas import tpu as pltpu
from jax.sharding import PartitionSpec as P

SMEM = pl.BlockSpec(memory_space=pltpu.SMEM)
VMEM = pl.BlockSpec(memory_space=pltpu.VMEM)
ANY = pl.BlockSpec(memory_space=pl.ANY)
MIB = 1 << 20


def matmul_cost(count, panels, height, excite, moved):
    return pl.CostEstimate(
        flops=2 * count * panels * height * excite, bytes_accessed=moved, transcendentals=0
    )


def local_kernel(klass, src_ref, lag_ref, class_ref, target_ref, table_ref, hist_ref, near_ref):
    panels = table_ref.shape[1]
    height = hist_ref.shape[2]
    near_ref[...] = jnp.zeros_like(near_ref)

    @pl.loop(0, src_ref.shape[0])
    def _(i):
        @pl.when(class_ref[i] == klass)
        def _():
            first = pl.multiple_of(lag_ref[i] * panels, panels)
            window = table_ref[pl.ds(first, height), :]
            near_ref[target_ref[i]] += jnp.dot(
                hist_ref[src_ref[i]], window, preferred_element_type=jnp.float32
            )


def local_sum(klass, src, lag, classes, target, table, hist_t):
    owned, excite, height = hist_t.shape
    panels = table.shape[1]
    return pl.pallas_call(
        functools.partial(local_kernel, klass),
        out_shape=jax.ShapeDtypeStruct((owned, excite, panels), jnp.float32),
        in_specs=[SMEM] * 4 + [VMEM] * 2,
        out_specs=VMEM,
        compiler_params=pltpu.CompilerParams(vmem_limit_bytes=32 * MIB),
        cost_estimate=matmul_cost(
            src.shape[0] // 3, panels, height, excite, 2 * (table.size + hist_t.size)
        ),
    )(src, lag, classes, target, table, hist_t)


def served_kernel(src_ref, lag_ref, class_ref, *refs):
    tables, (hist_ref, out_ref, held, sems) = refs[:-4], refs[-4:]
    count = src_ref.shape[0]
    panels = held.shape[2]
    height = held.shape[1]
    depth = held.shape[0]

    def fetch(i, slot, wait):
        first = pl.multiple_of(lag_ref[i] * panels, panels)
        for k, table in enumerate(tables):
            @pl.when(class_ref[i] == k)
            def _():
                copy = pltpu.make_async_copy(
                    table.at[pl.ds(first, height), :], held.at[slot], sems.at[slot]
                )
                if wait:
                    copy.wait()
                else:
                    copy.start()

    for i in range(min(depth - 1, count)):
        fetch(i, i, False)

    @pl.loop(0, count)
    def _(i):
        @pl.when(i + depth - 1 < count)
        def _():
            ahead = i + depth - 1
            fetch(ahead, lax.rem(ahead, depth), False)

        slot = lax.rem(i, depth)
        fetch(i, slot, True)
        out_ref[i] = jnp.dot(
            hist_ref[src_ref[i]], held[slot], preferred_element_type=jnp.float32
        ).astype(out_ref.dtype)


def served_products(src, lag, classes, tables, hist_t):
    owned, excite, height = hist_t.shape
    panels = tables[0].shape[1]
    count = src.shape[0]
    depth = 4
    return pl.pallas_call(
        served_kernel,
        out_shape=jax.ShapeDtypeStruct((count, excite, panels), jnp.bfloat16),
        in_specs=[SMEM] * 3 + [ANY] * len(tables) + [VMEM],
        out_specs=VMEM,
        scratch_shapes=[
            pltpu.VMEM((depth, height, panels), jnp.bfloat16),
            pltpu.SemaphoreType.DMA((depth,)),
        ],
        compiler_params=pltpu.CompilerParams(vmem_limit_bytes=32 * MIB),
        cost_estimate=matmul_cost(
            count, panels, height, excite, 2 * (count * height * panels + hist_t.size)
        ),
    )(src, lag, classes, *tables, hist_t)


def update_kernel(target_ref, *refs):
    nears, (recv_ref, inverse_ref, incident_ref, out_ref, total) = refs[:-5], refs[-5:]
    total[...] = sum(near[...] for near in nears)

    @pl.loop(0, target_ref.shape[0])
    def _(i):
        total[target_ref[i]] += recv_ref[i].astype(jnp.float32)

    for t in range(out_ref.shape[0]):
        residual = (incident_ref[t].astype(jnp.float32) - total[t].T).astype(jnp.bfloat16)
        out_ref[t] = jnp.dot(
            inverse_ref[t], residual, preferred_element_type=jnp.float32
        ).astype(out_ref.dtype)


def update(target, nears, recv, inverse, incident):
    return pl.pallas_call(
        update_kernel,
        out_shape=jax.ShapeDtypeStruct(incident.shape, jnp.bfloat16),
        in_specs=[SMEM] + [VMEM] * (len(nears) + 3),
        out_specs=VMEM,
        scratch_shapes=[pltpu.VMEM(nears[0].shape, jnp.float32)],
        compiler_params=pltpu.CompilerParams(vmem_limit_bytes=32 * MIB),
    )(target, *nears, recv, inverse, incident)


def per_device(
    weights,
    history,
    send_patch,
    send_lag,
    send_class,
    recv_target,
    local_src,
    local_lag,
    local_class,
    local_target,
    inverse_blocks,
    incident,
):
    classes, rows, panels = weights.shape
    peers, slots = send_patch.shape
    step = rows // peers
    piece = lax.dynamic_slice_in_dim(weights, lax.axis_index("grp") * step, step, 1)
    tables = [
        lax.all_gather(piece[k], ("lag", "grp"), axis=0, tiled=True) for k in range(classes)
    ]
    hist_t = jnp.swapaxes(history, 1, 2)
    served = served_products(
        send_patch.reshape(-1), send_lag.reshape(-1), send_class.reshape(-1), tables, hist_t
    )
    recv = lax.all_to_all(
        served.reshape(peers, slots, *served.shape[1:]), "grp", split_axis=0, concat_axis=0, tiled=True
    ).reshape(served.shape)
    nears = [
        local_sum(k, local_src, local_lag, local_class, local_target, tables[k], hist_t)
        for k in range(classes)
    ]
    return update(recv_target.reshape(-1), nears, recv, inverse_blocks, incident)


def solution(mesh):
    both = ("grp", "lag")
    return jax.shard_map(
        per_device,
        mesh=mesh,
        in_specs=(
            P(None, "lag", None),
            P(both, None, None),
            P(both, None),
            P(both, None),
            P(both, None),
            P(both, None),
            P(both),
            P(both),
            P(both),
            P(both),
            P(both, None, None),
            P(both, None, None),
        ),
        out_specs=P(both, None, None),
        check_vma=False,
    )
```

```python
import functools

import jax
import jax.numpy as jnp
from jax import lax
from jax.experimental import pallas as pl
from jax.experimental.pallas import tpu as pltpu
from jax.sharding import PartitionSpec as P

SMEM = pl.BlockSpec(memory_space=pltpu.SMEM)
VMEM = pl.BlockSpec(memory_space=pltpu.VMEM)
ANY = pl.BlockSpec(memory_space=pl.ANY)
MIB = 1 << 20


def add_pairs(shard, pairs, hist_ref, table, acc):
    src_ref, lag_ref, class_ref, dest_ref = pairs
    panels = table.shape[2]
    steps = hist_ref.shape[2] // panels
    lags = table.shape[1] // panels

    @pl.loop(0, src_ref.shape[0])
    def _(i):
        offset = lag_ref[i] - shard * lags
        first = jnp.maximum(offset, 0)
        count = jnp.minimum(offset + steps, lags) - first
        for n in range(1, min(steps, lags) + 1):
            @pl.when(count == n)
            def _():
                rows = pl.multiple_of(first * panels, panels)
                columns = pl.multiple_of((first - offset) * panels, panels)
                acc[dest_ref[i]] += jnp.dot(
                    hist_ref[src_ref[i], :, pl.ds(columns, n * panels)],
                    table[class_ref[i], pl.ds(rows, n * panels), :],
                    preferred_element_type=jnp.float32,
                )


def round_kernel(places, groups, begun, *refs):
    refs = list(refs)
    where = refs.pop(0)
    pairs = [[refs.pop(0) for _ in range(4)] for _ in range(groups)]
    hist_ref = refs.pop(0)
    pieces = [refs.pop(0) for _ in places]
    before = [refs.pop(0) for _ in range(groups if begun else 0)]
    outs = [refs.pop(0) for _ in range(groups)]
    table, sems, acc_sems = refs[:3]
    accs = refs[3:] or outs
    shard, group = where[0], where[1]

    copies = []
    for n, ((mask, first, height), piece) in enumerate(zip(places, pieces)):
        start = pl.multiple_of((group ^ mask) * height + first, 16)
        rows = piece.shape[1]
        copies.append(
            pltpu.make_async_copy(piece, table.at[:, pl.ds(start, rows), :], sems.at[n])
        )
    for n, (old, acc) in enumerate(zip(before, accs)):
        copies.append(pltpu.make_async_copy(old, acc, acc_sems.at[n]))
    for copy in copies:
        copy.start()
    if not begun:
        for acc in accs:
            acc[...] = jnp.zeros_like(acc)
    for copy in copies:
        copy.wait()
    for group_pairs, acc in zip(pairs, accs):
        add_pairs(shard, group_pairs, hist_ref, table, acc)
    for acc, out in zip(accs, outs):
        if acc is not out:
            out[...] = acc[...].astype(out.dtype)


def run_round(shard, group, pieces, height, pair_lists, hist_t, sums, counts, dtype=jnp.float32):
    owned, excite, depth = hist_t.shape
    classes, _, panels = pieces[0][2].shape
    rows = height * (pieces_total(pieces) // height)
    places = [(mask, first, height) for mask, first, _ in pieces]
    groups = len(pair_lists)
    shapes = [(count, excite, panels) for count in counts]
    wide = [pltpu.VMEM(s, jnp.float32) for s in shapes] if dtype != jnp.float32 else []
    pair_count = sum(lists[0].shape[0] for lists in pair_lists)
    moved = classes * rows * panels * 2 + hist_t.size * 2 + sum(8 * s[0] * s[1] * s[2] for s in shapes)
    return pl.pallas_call(
        functools.partial(round_kernel, places, groups, sums is not None),
        out_shape=[jax.ShapeDtypeStruct(s, dtype) for s in shapes],
        in_specs=[SMEM] * (1 + 4 * groups)
        + [VMEM]
        + [ANY] * (len(places) + (groups if sums is not None else 0)),
        out_specs=[VMEM] * groups,
        scratch_shapes=[
            pltpu.VMEM((classes, rows, panels), jnp.bfloat16),
            pltpu.SemaphoreType.DMA((len(places),)),
            pltpu.SemaphoreType.DMA((groups,)),
        ]
        + wide,
        compiler_params=pltpu.CompilerParams(vmem_limit_bytes=40 * MIB),
        cost_estimate=pl.CostEstimate(
            flops=2 * pair_count * panels * depth * excite // 3, bytes_accessed=moved, transcendentals=0
        ),
    )(
        jnp.stack([shard, group]).astype(jnp.int32),
        *[x for lists in pair_lists for x in lists],
        hist_t,
        *[piece for _, _, piece in pieces],
        *(sums if sums is not None else []),
    )


def pieces_total(pieces):
    return sum(piece.shape[1] for _, _, piece in pieces)


def update_kernel(target_ref, near_ref, recv_ref, inverse_ref, incident_ref, out_ref, total):
    total[...] = near_ref[...]

    @pl.loop(0, target_ref.shape[0])
    def _(i):
        total[target_ref[i]] += recv_ref[i].astype(jnp.float32)

    for t in range(out_ref.shape[0]):
        residual = (incident_ref[t].astype(jnp.float32) - total[t].T).astype(jnp.bfloat16)
        out_ref[t] = jnp.dot(
            inverse_ref[t], residual, preferred_element_type=jnp.float32
        ).astype(out_ref.dtype)


def update(target, near, recv, inverse, incident):
    return pl.pallas_call(
        update_kernel,
        out_shape=jax.ShapeDtypeStruct(incident.shape, jnp.bfloat16),
        in_specs=[SMEM] + [VMEM] * 4,
        out_specs=VMEM,
        scratch_shapes=[pltpu.VMEM(near.shape, jnp.float32)],
        compiler_params=pltpu.CompilerParams(vmem_limit_bytes=32 * MIB),
    )(target, near, recv, inverse, incident)


def swap(value, bit, peers):
    return lax.ppermute(value, "grp", [(i, i ^ bit) for i in range(peers)])


def spread(piece, peers):
    held = [(0, 0, piece)]
    bit = 8
    while bit < peers:
        held += [(mask ^ bit, first, swap(value, bit, peers)) for mask, first, value in held]
        bit *= 2
    found = []
    for mask, first, value in held:
        half = value.shape[1] // 2
        across = swap(value, 2, peers)
        along = swap(value, 4, peers)
        corner_a = swap(along[:, :half], 2, peers)
        corner_b = swap(across[:, half:], 4, peers)
        found += [
            (mask, first, value),
            (mask ^ 2, first, across),
            (mask ^ 4, first, along),
            (mask ^ 6, first, corner_a),
            (mask ^ 6, first + half, corner_b),
        ]
    return found + [(mask ^ 1, first, swap(value, 1, peers)) for mask, first, value in found]


def per_device(
    weights,
    history,
    send_patch,
    send_lag,
    send_class,
    recv_target,
    local_src,
    local_lag,
    local_class,
    local_target,
    inverse_blocks,
    incident,
):
    rows = weights.shape[1]
    owned = history.shape[0]
    peers, slots = send_patch.shape
    served_count = peers * slots
    height = rows // peers
    group = lax.axis_index("grp")
    lane = lax.axis_index("lag")
    lanes = lax.axis_size("lag")

    hist_t = jnp.swapaxes(history, 1, 2)
    served_pairs = (
        send_patch.reshape(-1),
        send_lag.reshape(-1),
        send_class.reshape(-1),
        jnp.arange(served_count, dtype=jnp.int32),
    )
    local_pairs = (local_src, local_lag, local_class, local_target)
    pairs = [served_pairs, local_pairs]
    counts = [served_count, owned]

    sums = run_round(lane, group * 0, [(0, 0, weights)], rows, pairs, hist_t, None, counts)
    piece = lax.dynamic_slice_in_dim(weights, group * height, height, 1)
    for step in range(1, lanes):
        piece = lax.ppermute(piece, "lag", [(i, (i - 1) % lanes) for i in range(lanes)])
        pieces = spread(piece, peers)
        shard = lax.rem(lane + step, lanes)
        if step < lanes - 1:
            sums = run_round(shard, group, pieces, height, pairs, hist_t, sums, counts)
    served = run_round(
        shard, group, pieces, height, pairs[:1], hist_t, sums[:1], counts[:1], jnp.bfloat16
    )[0]
    recv = lax.all_to_all(
        served.reshape(peers, slots, *served.shape[1:]), "grp", split_axis=0, concat_axis=0, tiled=True
    ).reshape(served.shape)
    near = run_round(shard, group, pieces, height, pairs[1:], hist_t, sums[1:], counts[1:])[0]
    return update(recv_target.reshape(-1), near, recv, inverse_blocks, incident)


def solution(mesh):
    both = ("grp", "lag")
    return jax.shard_map(
        per_device,
        mesh=mesh,
        in_specs=(
            P(None, "lag", None),
            P(both, None, None),
            P(both, None),
            P(both, None),
            P(both, None),
            P(both, None),
            P(both),
            P(both),
            P(both),
            P(both),
            P(both, None, None),
            P(both, None, None),
        ),
        out_specs=P(both, None, None),
        check_vma=False,
    )
```

```python
import functools

import jax
import jax.numpy as jnp
from jax import lax
from jax.experimental import pallas as pl
from jax.experimental.pallas import tpu as pltpu
from jax.sharding import PartitionSpec as P

SMEM = pl.BlockSpec(memory_space=pltpu.SMEM)
VMEM = pl.BlockSpec(memory_space=pltpu.VMEM)
HBM = pl.BlockSpec(memory_space=pltpu.HBM)
MIB = 1 << 20


def add_pairs(shard, pairs, hist_ref, table, acc):
    src_ref, lag_ref, class_ref, dest_ref = pairs
    panels = table.shape[2]
    steps = hist_ref.shape[2] // panels
    lags = table.shape[1] // panels
    widths = range(min(steps, lags), 0, -1)

    @pl.loop(0, src_ref.shape[0])
    def _(i):
        offset = lag_ref[i] - shard * lags
        first = jnp.maximum(offset, 0)
        count = jnp.minimum(offset + steps, lags) - first

        @pl.when(count > 0)
        def _():
            rows = pl.multiple_of(first * panels, panels)
            columns = pl.multiple_of((first - offset) * panels, panels)
            for n in widths:
                @pl.when(count == n)
                def _():
                    acc[dest_ref[i]] += jnp.dot(
                        hist_ref[src_ref[i], :, pl.ds(columns, n * panels)],
                        table[class_ref[i], pl.ds(rows, n * panels), :],
                        preferred_element_type=jnp.float32,
                    )


def round_kernel(places, groups, begun, narrow, *refs):
    refs = list(refs)
    where = refs.pop(0)
    pairs = [[refs.pop(0) for _ in range(4)] for _ in range(groups)]
    hist_ref = refs.pop(0)
    pieces = [refs.pop(0) for _ in places]
    for _ in range(groups if begun else 0):
        refs.pop(0)
    sums = [refs.pop(0) for _ in range(groups)]
    rounded = refs.pop(0) if narrow else None
    table, sems = refs
    shard, group = where[0], where[1]

    copies = []
    for n, ((mask, height, klass), piece) in enumerate(zip(places, pieces)):
        start = pl.multiple_of((group ^ mask) * height, 16)
        count, rows, _ = piece.shape
        copies.append(
            pltpu.make_async_copy(
                piece, table.at[pl.ds(klass, count), pl.ds(start, rows), :], sems.at[n]
            )
        )
    for copy in copies:
        copy.start()
    if not begun:
        for acc in sums:
            acc[...] = jnp.zeros_like(acc)
    for copy in copies:
        copy.wait()
    for group_pairs, acc in zip(pairs, sums):
        add_pairs(shard, group_pairs, hist_ref, table, acc)
    if narrow:
        rounded[...] = sums[0][...].astype(rounded.dtype)


def run_round(shard, group, rows, pieces, pair_lists, hist_t, sums, counts, narrow=False):
    owned, excite, depth = hist_t.shape
    panels = pieces[0][2].shape[2]
    classes = max(klass + value.shape[0] for _, klass, value in pieces)
    places = [(mask, value.shape[1], klass) for mask, klass, value in pieces]
    groups = len(pair_lists)
    shapes = [(count, excite, panels) for count in counts]
    outs = [jax.ShapeDtypeStruct(s, jnp.float32) for s in shapes]
    if narrow:
        outs.append(jax.ShapeDtypeStruct(shapes[0], jnp.bfloat16))
    before = list(sums) if sums is not None else []
    first_sum = 1 + 4 * groups + 1 + len(places)
    pair_count = sum(lists[0].shape[0] for lists in pair_lists)
    return pl.pallas_call(
        functools.partial(round_kernel, places, groups, sums is not None, narrow),
        out_shape=outs,
        in_specs=[SMEM] * (1 + 4 * groups) + [VMEM] + [HBM] * len(places) + [VMEM] * len(before),
        out_specs=[VMEM] * len(outs),
        scratch_shapes=[
            pltpu.VMEM((classes, rows, panels), jnp.bfloat16),
            pltpu.SemaphoreType.DMA((len(places),)),
        ],
        input_output_aliases={first_sum + n: n for n in range(len(before))},
        compiler_params=pltpu.CompilerParams(vmem_limit_bytes=16 * MIB),
        cost_estimate=pl.CostEstimate(
            flops=2 * pair_count * panels * depth * excite,
            bytes_accessed=2 * classes * rows * panels,
            transcendentals=0,
        ),
    )(
        jnp.stack([shard, group]).astype(jnp.int32),
        *[x for lists in pair_lists for x in lists],
        hist_t,
        *[value for _, _, value in pieces],
        *before,
    )


def update_kernel(target_ref, near_ref, recv_ref, inverse_ref, incident_ref, out_ref, total):
    total[...] = near_ref[...]

    @pl.loop(0, target_ref.shape[0])
    def _(i):
        total[target_ref[i]] += recv_ref[i].astype(jnp.float32)

    for t in range(out_ref.shape[0]):
        residual = (incident_ref[t].astype(jnp.float32) - total[t].T).astype(jnp.bfloat16)
        out_ref[t] = jnp.dot(
            inverse_ref[t], residual, preferred_element_type=jnp.float32
        ).astype(out_ref.dtype)


def update(target, near, recv, inverse, incident):
    return pl.pallas_call(
        update_kernel,
        out_shape=jax.ShapeDtypeStruct(incident.shape, jnp.bfloat16),
        in_specs=[SMEM] + [VMEM] * 4,
        out_specs=VMEM,
        scratch_shapes=[pltpu.VMEM(near.shape, jnp.float32)],
        compiler_params=pltpu.CompilerParams(vmem_limit_bytes=32 * MIB),
    )(target, near, recv, inverse, incident)


def swap(value, bit, peers):
    return lax.ppermute(value, "grp", [(i, i ^ bit) for i in range(peers)])


def exchange(own, corner, peers):
    held = [(0, own, corner)]
    bit = 8
    while bit < peers:
        held += [(mask ^ bit, swap(a, bit, peers), swap(c, bit, peers)) for mask, a, c in held]
        bit *= 2
    return [(mask, a, swap(a, 2, peers), swap(a, 4, peers), c) for mask, a, c in held]


def finish(held, peers):
    found = []
    for mask, own, across, along, corner in held:
        third = corner.shape[0]
        found += [
            (mask, 0, own),
            (mask ^ 2, 0, across),
            (mask ^ 4, 0, along),
            (mask ^ 6, 0, corner),
            (mask ^ 6, third, swap(along[third : 2 * third], 2, peers)),
            (mask ^ 6, 2 * third, swap(across[2 * third :], 4, peers)),
        ]
    return found + [(mask ^ 1, klass, swap(value, 1, peers)) for mask, klass, value in found]


def per_device(
    weights,
    history,
    send_patch,
    send_lag,
    send_class,
    recv_target,
    local_src,
    local_lag,
    local_class,
    local_target,
    inverse_blocks,
    incident,
):
    classes, rows, _ = weights.shape
    owned = history.shape[0]
    peers, slots = send_patch.shape
    served_count = peers * slots
    height = rows // peers
    group = lax.axis_index("grp")
    lane = lax.axis_index("lag")
    lanes = lax.axis_size("lag")
    ring = [(i, (i - 1) % lanes) for i in range(lanes)]

    hist_t = jnp.swapaxes(history, 1, 2)
    served_pairs = (
        send_patch.reshape(-1),
        send_lag.reshape(-1),
        send_class.reshape(-1),
        jnp.arange(served_count, dtype=jnp.int32),
    )
    local_pairs = (local_src, local_lag, local_class, local_target)
    pairs = [served_pairs, local_pairs]
    counts = [served_count, owned]

    own = lax.dynamic_slice_in_dim(weights, group * height, height, 1)
    corner = lax.dynamic_slice_in_dim(
        weights[: classes // 3], (group ^ 6) * height, height, 1
    )
    sums = run_round(lane, group * 0, rows, [(0, 0, weights)], pairs, hist_t, None, counts)
    pieces = None
    for step in range(1, lanes):
        own = lax.ppermute(own, "lag", ring)
        own, corner = lax.optimization_barrier((own, corner))
        corner = lax.ppermute(corner, "lag", ring)
        if step == 1:
            own, sums = lax.optimization_barrier((own, sums))
        held = exchange(own, corner, peers)
        if step > 1:
            sums = run_round(shard, group, rows, pieces, pairs, hist_t, sums, counts)
            values, sums = lax.optimization_barrier(([h[1:] for h in held], sums))
            held = [(h[0], *v) for h, v in zip(held, values)]
        pieces = finish(held, peers)
        shard = lax.rem(lane + step, lanes)
    _, served = run_round(
        shard, group, rows, pieces, pairs[:1], hist_t, sums[:1], counts[:1], narrow=True
    )
    recv = lax.all_to_all(
        served.reshape(peers, slots, *served.shape[1:]), "grp", split_axis=0, concat_axis=0, tiled=True
    ).reshape(served.shape)
    near = run_round(shard, group, rows, pieces, pairs[1:], hist_t, sums[1:], counts[1:])[0]
    return update(recv_target.reshape(-1), near, recv, inverse_blocks, incident)


def solution(mesh):
    both = ("grp", "lag")
    return jax.shard_map(
        per_device,
        mesh=mesh,
        in_specs=(
            P(None, "lag", None),
            P(both, None, None),
            P(both, None),
            P(both, None),
            P(both, None),
            P(both, None),
            P(both),
            P(both),
            P(both),
            P(both),
            P(both, None, None),
            P(both, None, None),
        ),
        out_specs=P(both, None, None),
        check_vma=False,
    )
```

```python
import functools

import jax
import jax.numpy as jnp
from jax import lax
from jax.experimental import pallas as pl
from jax.experimental.pallas import tpu as pltpu
from jax.sharding import PartitionSpec as P

SMEM = pl.BlockSpec(memory_space=pltpu.SMEM)
VMEM = pl.BlockSpec(memory_space=pltpu.VMEM)
HBM = pl.BlockSpec(memory_space=pltpu.HBM)
MIB = 1 << 20
CLASS_BITS, SOURCE_BITS, LAG_BITS, STEP_BITS = 4, 8, 8, 4


def widths(steps):
    return [1 << b for b in range(steps.bit_length() - 1, -1, -1)]


def list_tasks(base, span, total, steps, pair, tasks, counts):
    source, klass, lag, place = pair
    start = lax.rem(lag - base + total, total)
    inside = start < span
    first = jnp.where(inside, start, 0)
    skip = jnp.where(inside, 0, total - start)
    count = jnp.maximum(jnp.where(inside, jnp.minimum(steps, span - start), steps - skip), 0)
    for b, width in enumerate(widths(steps)):
        has = jnp.where((count & width) != 0, 1, 0)
        done = count & ~(2 * width - 1)
        packed = place
        for value, bits in (
            (skip + done, STEP_BITS),
            (first + done, LAG_BITS),
            (source, SOURCE_BITS),
            (klass, CLASS_BITS),
        ):
            packed = (packed << bits) | value
        at = counts[b]
        tasks[b, at] = packed
        counts[b] = at + has


def run_tasks(steps, spare, tasks, counts, hist, table, acc):
    panels = table.shape[2]

    def product(packed, width):
        fields = []
        for bits in (CLASS_BITS, SOURCE_BITS, LAG_BITS, STEP_BITS):
            fields.append(packed & ((1 << bits) - 1))
            packed = packed >> bits
        klass, source, lag, step = fields
        rows = pl.multiple_of(lag * panels, panels)
        columns = pl.multiple_of(step * panels, panels)
        return packed, jnp.dot(
            hist[source, :, pl.ds(columns, width * panels)],
            table[klass, pl.ds(rows, width * panels), :],
            preferred_element_type=jnp.float32,
        )

    for b, width in enumerate(widths(steps)):
        count = counts[b]
        tasks[b, count] = spare << (CLASS_BITS + SOURCE_BITS + LAG_BITS + STEP_BITS)

        @pl.loop(0, (count + 1) // 2)
        def _(j):
            one, first = product(tasks[b, 2 * j], width)
            two, second = product(tasks[b, 2 * j + 1], width)
            acc[one] += first
            acc[two] += second


def window_kernel(config, *refs):
    served, local, begun, narrow, places, total, height = config
    refs = list(refs)
    where = refs.pop(0)
    served_refs = [refs.pop(0) for _ in range(3 if served else 0)]
    local_refs = [refs.pop(0) for _ in range(4 if local else 0)]
    hist_ref = refs.pop(0)
    pieces = [refs.pop(0) for _ in places]
    before = refs.pop(0) if begun else None
    out, table, hist, acc, tasks, counts, sems, ends = refs
    base, group = where[0], where[1]
    panels = table.shape[2]
    span = table.shape[1] // panels
    steps = hist.shape[2] // panels
    number = acc.shape[0] - 1

    copies = [pltpu.make_async_copy(hist_ref, hist, ends.at[0])]
    for n, ((slot, mask, klass), piece) in enumerate(zip(places, pieces)):
        depth, rows, _ = piece.shape
        start = pl.multiple_of(slot * height + (group ^ mask) * rows, 16)
        copies.append(
            pltpu.make_async_copy(
                piece, table.at[pl.ds(klass, depth), pl.ds(start, rows), :], sems.at[n]
            )
        )
    if begun:
        first = 0 if served else before.shape[0] - number
        copies.append(
            pltpu.make_async_copy(
                before.at[pl.ds(first, number)], acc.at[pl.ds(0, number)], ends.at[1]
            )
        )
    for copy in copies:
        copy.start()
    if not begun:
        acc[...] = jnp.zeros_like(acc)

    for b in range(len(widths(steps))):
        counts[b] = 0
    if served:
        peers, slots = served_refs[0].shape

        @pl.loop(0, peers)
        def _(i):
            for c in range(slots):
                source, lag, klass = (ref[i, c] for ref in served_refs)
                pair = (source, klass, lag, i * slots + c)
                list_tasks(base, span, total, steps, pair, tasks, counts)

    if local:
        lead = number - hist.shape[0]

        @pl.loop(0, local_refs[0].shape[0])
        def _(i):
            source, lag, klass, target = (ref[i] for ref in local_refs)
            pair = (source, klass, lag, target + lead)
            list_tasks(base, span, total, steps, pair, tasks, counts)

    for copy in copies:
        copy.wait()
    run_tasks(steps, number, tasks, counts, hist, table, acc)
    if narrow:
        out[...] = acc[pl.ds(0, number)].astype(out.dtype)
    else:
        copy = pltpu.make_async_copy(acc.at[pl.ds(0, number)], out, ends.at[1])
        copy.start()
        copy.wait()


def window_sums(base, group, served, local, hist_t, pieces, sums, lanes, height, narrow=False):
    owned, excite, depth = hist_t.shape
    panels = pieces[0][3].shape[2]
    classes = max(klass + value.shape[0] for _, _, klass, value in pieces)
    rows = height * (1 + max(slot for slot, _, _, _ in pieces))
    number = (served[0].size if served else 0) + (owned if local else 0)
    pairs = (served[0].size if served else 0) + (local[0].size if local else 0)
    steps = depth // panels
    config = (
        bool(served),
        bool(local),
        sums is not None,
        narrow,
        tuple(piece[:3] for piece in pieces),
        lanes * height // panels,
        height,
    )
    operands = [jnp.stack([base * (height // panels), group]).astype(jnp.int32), *served, *local]
    wide = [hist_t, *[piece[3] for piece in pieces], *([sums] if sums is not None else [])]
    return pl.pallas_call(
        functools.partial(window_kernel, config),
        out_shape=jax.ShapeDtypeStruct(
            (number, excite, panels), jnp.bfloat16 if narrow else jnp.float32
        ),
        in_specs=[SMEM] * len(operands) + [HBM] * len(wide),
        out_specs=VMEM if narrow else HBM,
        scratch_shapes=[
            pltpu.VMEM((classes, rows, panels), jnp.bfloat16),
            pltpu.VMEM(hist_t.shape, hist_t.dtype),
            pltpu.VMEM((number + 1, excite, panels), jnp.float32),
            pltpu.SMEM((len(widths(steps)), pairs + 2), jnp.int32),
            pltpu.SMEM((len(widths(steps)),), jnp.int32),
            pltpu.SemaphoreType.DMA((len(pieces),)),
            pltpu.SemaphoreType.DMA((2,)),
        ],
        compiler_params=pltpu.CompilerParams(vmem_limit_bytes=58 * MIB),
        cost_estimate=pl.CostEstimate(
            flops=2 * pairs * panels * depth * excite,
            bytes_accessed=2 * classes * rows * panels + 2 * hist_t.size,
            transcendentals=0,
        ),
    )(*operands, *wide)


def update_kernel(target_ref, near_ref, recv_ref, inverse_ref, incident_ref, out_ref, total):
    total[...] = near_ref[...]
    peers, slots = target_ref.shape

    @pl.loop(0, peers)
    def _(i):
        for c in range(slots):
            total[target_ref[i, c]] += recv_ref[i, c].astype(jnp.float32)

    for t in range(out_ref.shape[0]):
        residual = (incident_ref[t].astype(jnp.float32) - total[t].T).astype(jnp.bfloat16)
        out_ref[t] = jnp.dot(
            inverse_ref[t], residual, preferred_element_type=jnp.float32
        ).astype(out_ref.dtype)


def update(target, near, recv, inverse, incident):
    return pl.pallas_call(
        update_kernel,
        out_shape=jax.ShapeDtypeStruct(incident.shape, jnp.bfloat16),
        in_specs=[SMEM] + [VMEM] * 4,
        out_specs=VMEM,
        scratch_shapes=[pltpu.VMEM(near.shape, jnp.float32)],
        compiler_params=pltpu.CompilerParams(vmem_limit_bytes=32 * MIB),
    )(target, near, recv, inverse, incident)


def swap(value, bit, peers):
    return lax.ppermute(value, "grp", [(i, i ^ bit) for i in range(peers)])


def exchange(own, corner, peers):
    held = [(0, own, corner)]
    bit = 8
    while bit < peers:
        held += [(mask ^ bit, swap(a, bit, peers), swap(c, bit, peers)) for mask, a, c in held]
        bit *= 2
    return [(mask, a, swap(a, 2, peers), swap(a, 4, peers), c) for mask, a, c in held]


def finish(held, slot, peers):
    found = []
    for mask, own, across, along, corner in held:
        third = corner.shape[0]
        found += [
            (slot, mask, 0, own),
            (slot, mask ^ 2, 0, across),
            (slot, mask ^ 4, 0, along),
            (slot, mask ^ 6, 0, corner),
            (slot, mask ^ 6, third, swap(along[third : 2 * third], 2, peers)),
            (slot, mask ^ 6, 2 * third, swap(across[2 * third :], 4, peers)),
        ]
    return found + [(slot, mask ^ 1, klass, swap(v, 1, peers)) for slot, mask, klass, v in found]


def per_device(
    weights,
    history,
    send_patch,
    send_lag,
    send_class,
    recv_target,
    local_src,
    local_lag,
    local_class,
    local_target,
    inverse_blocks,
    incident,
):
    classes, rows, panels = weights.shape
    peers, slots = send_patch.shape
    height = rows // peers
    group = lax.axis_index("grp")
    lane = lax.axis_index("lag")
    lanes = lax.axis_size("lag")
    ring = [(i, (i - 1) % lanes) for i in range(lanes)]
    served = (send_patch, send_lag, send_class)
    local = (local_src, local_lag, local_class, local_target)

    hist_t = jnp.swapaxes(history, 1, 2)
    own = lax.dynamic_slice(weights, (0, group * height, 0), (classes, height, panels))
    corner = lax.dynamic_slice(
        weights, (0, (group ^ 6) * height, 0), (classes // 3, height, panels)
    )
    sums = window_sums(
        lane, group * 0, served, local, hist_t, [(0, 0, 0, weights)], None, lanes, rows
    )
    pieces = []
    for step in range(1, lanes):
        own = lax.ppermute(own, "lag", ring)
        own, corner = lax.optimization_barrier((own, corner))
        corner = lax.ppermute(corner, "lag", ring)
        if step == 1:
            own, sums = lax.optimization_barrier((own, sums))
        held = exchange(own, corner, peers)
        if step == lanes - 1:
            sums = window_sums(
                lax.rem(lane + 1, lanes), group, served, local, hist_t, pieces, sums, lanes, rows
            )
            values, sums = lax.optimization_barrier(([h[1:] for h in held], sums))
            held = [(h[0], *v) for h, v in zip(held, values)]
            pieces = finish(held, 0, peers)
        else:
            pieces += finish(held, step - 1, peers)
    last = lax.rem(lane + lanes - 1, lanes)
    contribution = window_sums(
        last, group, served, (), hist_t, pieces, sums, lanes, rows, narrow=True
    )
    recv = lax.all_to_all(
        contribution.reshape(peers, slots, *contribution.shape[1:]),
        "grp",
        split_axis=0,
        concat_axis=0,
        tiled=True,
    )
    near = window_sums(last, group, (), local, hist_t, pieces, sums, lanes, rows)
    return update(recv_target, near, recv, inverse_blocks, incident)


def solution(mesh):
    both = ("grp", "lag")
    return jax.shard_map(
        per_device,
        mesh=mesh,
        in_specs=(
            P(None, "lag", None),
            P(both, None, None),
            P(both, None),
            P(both, None),
            P(both, None),
            P(both, None),
            P(both),
            P(both),
            P(both),
            P(both),
            P(both, None, None),
            P(both, None, None),
        ),
        out_specs=P(both, None, None),
        check_vma=False,
    )
```

```python
import functools

import jax
import jax.numpy as jnp
from jax import lax
from jax.experimental import pallas as pl
from jax.experimental.pallas import tpu as pltpu
from jax.sharding import PartitionSpec as P

SMEM = pl.BlockSpec(memory_space=pltpu.SMEM)
VMEM = pl.BlockSpec(memory_space=pltpu.VMEM)
HBM = pl.BlockSpec(memory_space=pltpu.HBM)
MIB = 1 << 20
WIDTH_BITS, SOURCE_BITS, LAG_BITS, STEP_BITS = 5, 8, 8, 4
FIELDS = (WIDTH_BITS, SOURCE_BITS, LAG_BITS, STEP_BITS)
ROW_PARTS = 2


def list_task(base, span, total, steps, pair, tasks, counts):
    source, klass, lag, place = pair
    start = lax.rem(lag - base + total, total)
    inside = start < span
    first = jnp.where(inside, start, 0)
    skip = jnp.where(inside, 0, total - start)
    width = jnp.maximum(jnp.where(inside, jnp.minimum(steps, span - start), steps - skip), 0)
    packed = place
    for value, bits in ((skip, STEP_BITS), (first, LAG_BITS), (source, SOURCE_BITS), (width, WIDTH_BITS)):
        packed = (packed << bits) | value
    at = counts[klass]
    tasks[klass, at] = packed
    counts[klass] = at + jnp.where(width > 0, 1, 0)
    return width > 0


def run_width(width, low, high, run):
    if low == high:
        run(low)
        return
    middle = (low + high) // 2

    @pl.when(width <= middle)
    def _():
        run_width(width, low, middle, run)

    @pl.when(width > middle)
    def _():
        run_width(width, middle + 1, high, run)


def run_task(packed, klass, steps, hist, table, acc):
    panels = table.shape[2]
    part = hist.shape[1] // ROW_PARTS
    fields = []
    for bits in FIELDS:
        fields.append(packed & ((1 << bits) - 1))
        packed = packed >> bits
    width, source, lag, step = fields
    rows = pl.multiple_of(lag * panels, panels)
    columns = pl.multiple_of(step * panels, panels)

    def run(n):
        for p in range(ROW_PARTS):
            acc[packed, p * part : (p + 1) * part, :] += jnp.dot(
                hist[source, p * part : (p + 1) * part, pl.ds(columns, n * panels)],
                table[klass, pl.ds(rows, n * panels), :],
                preferred_element_type=jnp.float32,
            )

    run_width(width, 1, steps, run)


def window_kernel(config, *refs):
    served, local, begun, narrow, places, total, height, owned = config
    refs = list(refs)
    where = refs.pop(0)
    served_refs = [refs.pop(0) for _ in range(3 if served else 0)]
    local_refs = [refs.pop(0) for _ in range(4 if local else 0)]
    hist_ref = refs.pop(0)
    pieces = [refs.pop(0) for _ in places]
    before = [refs.pop(0) for _ in range((bool(served) + bool(local)) if begun else 0)]
    outs = [refs.pop(0) for _ in range(bool(served) + bool(local))]
    table, hist, acc, tasks, counts, used, sems, ends, served_sems = refs
    base, group = where[0], where[1]
    classes, _, panels = table.shape
    span = table.shape[1] // panels
    steps = hist.shape[2] // panels

    pltpu.make_async_copy(hist_ref, hist, ends.at[0]).start()
    near = acc.at[pl.ds(served, owned)] if local else None
    if local and begun:
        pltpu.make_async_copy(before[-1], near, ends.at[1]).start()
    for k in range(classes):
        for (mask, first), piece in zip(places, pieces):
            rows = piece.shape[1]
            start = pl.multiple_of((group ^ mask) * height + first, 16)
            pltpu.make_async_copy(
                piece.at[k], table.at[k, pl.ds(start, rows), :], sems.at[k]
            ).start()
    if not begun:
        acc[...] = jnp.zeros_like(acc)
    for k in range(classes):
        counts[k] = 0

    def served_copy(i, back):
        ends_of = (acc.at[i], outs[0].at[i]) if back else (before[0].at[i], acc.at[i])
        return pltpu.make_async_copy(*ends_of, served_sems.at[i])

    if served:
        peers, slots = served_refs[0].shape

        @pl.loop(0, peers)
        def _(i):
            for c in range(slots):
                source, lag, klass = (ref[i, c] for ref in served_refs)
                place = i * slots + c
                touched = list_task(
                    base, span, total, steps, (source, klass, lag, place), tasks, counts
                )
                needed = touched | narrow
                used[place] = jnp.where(touched, 1, 0)
                if begun:
                    @pl.when(needed)
                    def _():
                        served_copy(place, False).start()

    if local:
        @pl.loop(0, local_refs[0].shape[0])
        def _(i):
            source, lag, klass, target = (ref[i] for ref in local_refs)
            list_task(
                base, span, total, steps, (source, klass, lag, target + served), tasks, counts
            )

    pltpu.make_async_copy(hist_ref, hist, ends.at[0]).wait()
    if local and begun:
        pltpu.make_async_copy(before[-1], near, ends.at[1]).wait()
    if served and begun:
        @pl.loop(0, served)
        def _(i):
            @pl.when((used[i] != 0) | narrow)
            def _():
                served_copy(i, False).wait()

    @pl.loop(0, classes)
    def _(k):
        pltpu.make_async_copy(table.at[k], table.at[k], sems.at[k]).wait()

        @pl.loop(0, counts[k])
        def _(j):
            run_task(tasks[k, j], k, steps, hist, table, acc)

    if narrow:
        outs[0][...] = acc[...].astype(outs[0].dtype)
        return
    if local:
        pltpu.make_async_copy(near, outs[-1], ends.at[1]).start()
    if served:
        for wait in (False, True):
            @pl.loop(0, served)
            def _(i):
                @pl.when((used[i] != 0) | (not begun))
                def _():
                    copy = served_copy(i, True)
                    copy.wait() if wait else copy.start()
    if local:
        pltpu.make_async_copy(near, outs[-1], ends.at[1]).wait()


def window_sums(shard, group, served, local, hist_t, pieces, sums, lanes, rows, narrow=False):
    owned, excite, depth = hist_t.shape
    classes, _, panels = pieces[0][2].shape
    places = served[0].size if served else 0
    targets = owned if local else 0
    pairs = places + (local[0].size if local else 0)
    steps = depth // panels
    height = max(first + value.shape[1] for _, first, value in pieces)
    config = (
        places,
        bool(local),
        sums is not None,
        narrow,
        tuple(piece[:2] for piece in pieces),
        lanes * rows // panels,
        height,
        targets,
    )
    operands = [jnp.stack([shard * (rows // panels), group]).astype(jnp.int32), *served, *local]
    wide = [hist_t, *[piece[2] for piece in pieces]]
    before = list(sums) if sums is not None else []
    outs = [
        jax.ShapeDtypeStruct((n, excite, panels), jnp.bfloat16 if narrow else jnp.float32)
        for n in (places, targets)
        if n
    ]
    return pl.pallas_call(
        functools.partial(window_kernel, config),
        out_shape=outs,
        in_specs=[SMEM] * len(operands) + [HBM] * (len(wide) + len(before)),
        out_specs=[VMEM if narrow else HBM] * len(outs),
        scratch_shapes=[
            pltpu.VMEM((classes, rows, panels), jnp.bfloat16),
            pltpu.VMEM(hist_t.shape, hist_t.dtype),
            pltpu.VMEM((places + targets, excite, panels), jnp.float32),
            pltpu.SMEM((classes, pairs + 1), jnp.int32),
            pltpu.SMEM((classes,), jnp.int32),
            pltpu.SMEM((max(places, 1),), jnp.int32),
            pltpu.SemaphoreType.DMA((classes,)),
            pltpu.SemaphoreType.DMA((2,)),
            pltpu.SemaphoreType.DMA((max(places, 1),)),
        ],
        input_output_aliases={} if narrow else {
            len(operands) + len(wide) + n: n for n in range(len(before))
        },
        compiler_params=pltpu.CompilerParams(vmem_limit_bytes=58 * MIB),
        cost_estimate=pl.CostEstimate(
            flops=2 * pairs * panels * depth * excite,
            bytes_accessed=2 * classes * rows * panels + 2 * hist_t.size,
            transcendentals=0,
        ),
    )(*operands, *wide, *before)


def update_kernel(target_ref, near_ref, recv_ref, inverse_ref, incident_ref, out_ref, total):
    total[...] = near_ref[...]
    peers, slots = target_ref.shape

    @pl.loop(0, peers)
    def _(i):
        for c in range(slots):
            total[target_ref[i, c]] += recv_ref[i, c].astype(jnp.float32)

    for t in range(out_ref.shape[0]):
        residual = (incident_ref[t].astype(jnp.float32) - total[t].T).astype(jnp.bfloat16)
        out_ref[t] = jnp.dot(
            inverse_ref[t], residual, preferred_element_type=jnp.float32
        ).astype(out_ref.dtype)


def update(target, near, recv, inverse, incident):
    return pl.pallas_call(
        update_kernel,
        out_shape=jax.ShapeDtypeStruct(incident.shape, jnp.bfloat16),
        in_specs=[SMEM] + [VMEM] * 4,
        out_specs=VMEM,
        scratch_shapes=[pltpu.VMEM(near.shape, jnp.float32)],
        compiler_params=pltpu.CompilerParams(vmem_limit_bytes=32 * MIB),
    )(target, near, recv, inverse, incident)


def swap(value, bit, peers):
    return lax.ppermute(value, "grp", [(i, i ^ bit) for i in range(peers)])


def upper(value, peers):
    masks, held = [0], [value]
    bit = 8
    while bit < peers:
        masks += [mask ^ bit for mask in masks]
        held += [swap(value, bit, peers) for value in held]
        bit *= 2
    return masks, held


def with_other_core(found, peers):
    return found + [(mask ^ 1, first, swap(v, 1, peers)) for mask, first, v in found]


def per_device(
    weights,
    history,
    send_patch,
    send_lag,
    send_class,
    recv_target,
    local_src,
    local_lag,
    local_class,
    local_target,
    inverse_blocks,
    incident,
):
    classes, rows, panels = weights.shape
    peers, slots = send_patch.shape
    height = rows // peers
    group = lax.axis_index("grp")
    lane = lax.axis_index("lag")
    lanes = lax.axis_size("lag")
    ring = [(i, (i - 1) % lanes) for i in range(lanes)]
    served = (send_patch, send_lag, send_class)
    local = (local_src, local_lag, local_class, local_target)

    hist_t = jnp.swapaxes(history, 1, 2)
    half = height // 2

    def part(index):
        return lax.dynamic_slice(weights, (0, index * height, 0), (classes, height, panels))

    def add_shard(step, sums):
        shard = lax.rem(lane + step, lanes)
        return window_sums(shard, group, served, local, hist_t, rounds[step - 1], sums, lanes, rows)

    sums = window_sums(
        lane, group * 0, served, local, hist_t, [(0, 0, weights)], None, lanes, rows
    )
    own = part(group)
    corner = part(group ^ 6)
    rounds = []
    for step in range(1, lanes):
        own = lax.ppermute(own, "lag", ring)
        if step == 1:
            ready, sums = lax.optimization_barrier((own, sums))
        else:
            if step > 2:
                sums = add_shard(step - 2, sums)
            ready, corner, sums, across, along = lax.optimization_barrier(
                (own, corner, sums, across, along)
            )
            found = [(m, 0, v) for m, v in zip(masks, held)]
            found += [(m ^ 2, 0, v) for m, v in zip(masks, across)]
            found += [(m ^ 4, 0, v) for m, v in zip(masks, along)]
            found += [(m ^ 6, 0, swap(v[:, :half], 2, peers)) for m, v in zip(masks, along)]
            found += [(m ^ 6, half, swap(v[:, half:], 4, peers)) for m, v in zip(masks, across)]
            rounds.append(with_other_core(found, peers))
        masks, held = upper(ready, peers)
        across = [swap(value, 2, peers) for value in held]
        along = [swap(value, 4, peers) for value in held]
    corner = lax.ppermute(corner, "lag", [(j, i) for i, j in ring])
    if lanes > 2:
        sums = add_shard(lanes - 2, sums)
        across, along, corner, sums = lax.optimization_barrier((across, along, corner, sums))
    _, corners = upper(corner, peers)
    found = [(m, 0, v) for m, v in zip(masks, held)]
    found += [(m ^ 2, 0, v) for m, v in zip(masks, across)]
    found += [(m ^ 4, 0, v) for m, v in zip(masks, along)]
    found += [(m ^ 6, 0, v) for m, v in zip(masks, corners)]
    rounds.append(with_other_core(found, peers))
    last = lax.rem(lane + lanes - 1, lanes)
    contribution = window_sums(
        last, group, served, (), hist_t, rounds[-1], sums[:1], lanes, rows, narrow=True
    )[0]
    recv = lax.all_to_all(
        contribution.reshape(peers, slots, *contribution.shape[1:]),
        "grp",
        split_axis=0,
        concat_axis=0,
        tiled=True,
    )
    near = window_sums(last, group, (), local, hist_t, rounds[-1], sums[1:], lanes, rows)[0]
    return update(recv_target, near, recv, inverse_blocks, incident)


def solution(mesh):
    both = ("grp", "lag")
    return jax.shard_map(
        per_device,
        mesh=mesh,
        in_specs=(
            P(None, "lag", None),
            P(both, None, None),
            P(both, None),
            P(both, None),
            P(both, None),
            P(both, None),
            P(both),
            P(both),
            P(both),
            P(both),
            P(both, None, None),
            P(both, None, None),
        ),
        out_specs=P(both, None, None),
        check_vma=False,
    )
```

```python
import functools

import jax
import jax.numpy as jnp
from jax import lax
from jax.experimental import pallas as pl
from jax.experimental.pallas import tpu as pltpu
from jax.sharding import PartitionSpec as P

SMEM = pl.BlockSpec(memory_space=pltpu.SMEM)
VMEM = pl.BlockSpec(memory_space=pltpu.VMEM)
HBM = pl.BlockSpec(memory_space=pltpu.HBM)
MIB = 1 << 20
WIDTH_BITS, SOURCE_BITS, LAG_BITS, STEP_BITS = 5, 8, 8, 4
FIELDS = (WIDTH_BITS, SOURCE_BITS, LAG_BITS, STEP_BITS)
CHUNK = 4


def list_task(base, span, total, steps, pair, tasks, counts):
    source, klass, lag, place = pair
    start = lax.rem(lag - base + total, total)
    inside = start < span
    first = jnp.where(inside, start, 0)
    skip = jnp.where(inside, 0, total - start)
    width = jnp.maximum(jnp.where(inside, jnp.minimum(steps, span - start), steps - skip), 0)
    packed = place
    for value, bits in ((skip, STEP_BITS), (first, LAG_BITS), (source, SOURCE_BITS), (width, WIDTH_BITS)):
        packed = (packed << bits) | value
    at = counts[klass]
    tasks[klass, at] = packed
    counts[klass] = at + jnp.where(width > 0, 1, 0)
    return width > 0


def run_task(packed, klass, steps, hist, table, acc):
    panels = table.shape[2]
    fields = []
    for bits in FIELDS:
        fields.append(packed & ((1 << bits) - 1))
        packed = packed >> bits
    width, source, lag, step = fields

    def add(done, n):
        rows = pl.multiple_of((lag + done) * panels, panels)
        columns = pl.multiple_of((step + done) * panels, panels)
        acc[packed] += jnp.dot(
            hist[source, :, pl.ds(columns, n * panels)],
            table[klass, pl.ds(rows, n * panels), :],
            preferred_element_type=jnp.float32,
        )

    @pl.loop(0, width // CHUNK)
    def _(j):
        add(j * CHUNK, CHUNK)

    n = CHUNK // 2
    while n:
        @pl.when((width & n) != 0)
        def _(n=n):
            add(width & ~(2 * n - 1), n)

        n //= 2


def window_kernel(config, *refs):
    served, local, begun, narrow, places, total, height, owned = config
    refs = list(refs)
    where = refs.pop(0)
    served_refs = [refs.pop(0) for _ in range(3 if served else 0)]
    local_refs = [refs.pop(0) for _ in range(4 if local else 0)]
    hist_ref = refs.pop(0)
    pieces = [refs.pop(0) for _ in places]
    before = [refs.pop(0) for _ in range((bool(served) + bool(local)) if begun else 0)]
    outs = [refs.pop(0) for _ in range(bool(served) + bool(local))]
    table, hist, acc, tasks, counts, used, sems, ends, served_sems = refs
    base, group = where[0], where[1]
    classes, _, panels = table.shape
    span = table.shape[1] // panels
    steps = hist.shape[2] // panels

    pltpu.make_async_copy(hist_ref, hist, ends.at[0]).start()
    near = acc.at[pl.ds(served, owned)] if local else None
    if local and begun:
        pltpu.make_async_copy(before[-1], near, ends.at[1]).start()
    for k in range(classes):
        for (mask, first), piece in zip(places, pieces):
            rows = piece.shape[1]
            start = pl.multiple_of((group ^ mask) * height + first, 16)
            pltpu.make_async_copy(
                piece.at[k], table.at[k, pl.ds(start, rows), :], sems.at[k]
            ).start()
    if not begun:
        acc[...] = jnp.zeros_like(acc)
    for k in range(classes):
        counts[k] = 0

    def served_copy(i, back):
        ends_of = (acc.at[i], outs[0].at[i]) if back else (before[0].at[i], acc.at[i])
        return pltpu.make_async_copy(*ends_of, served_sems.at[i])

    if served:
        slots, peers = served_refs[0].shape

        @pl.loop(0, peers)
        def _(i):
            for c in range(slots):
                source, lag, klass = (ref[c, i] for ref in served_refs)
                place = i * slots + c
                touched = list_task(
                    base, span, total, steps, (source, klass, lag, place), tasks, counts
                )
                needed = touched | narrow
                used[place] = jnp.where(touched, 1, 0)
                if begun:
                    @pl.when(needed)
                    def _():
                        served_copy(place, False).start()

    if local:
        @pl.loop(0, local_refs[0].shape[0])
        def _(i):
            source, lag, klass, target = (ref[i] for ref in local_refs)
            list_task(
                base, span, total, steps, (source, klass, lag, target + served), tasks, counts
            )

    pltpu.make_async_copy(hist_ref, hist, ends.at[0]).wait()
    if local and begun:
        pltpu.make_async_copy(before[-1], near, ends.at[1]).wait()
    if served and begun:
        @pl.loop(0, served)
        def _(i):
            @pl.when((used[i] != 0) | narrow)
            def _():
                served_copy(i, False).wait()

    @pl.loop(0, classes)
    def _(k):
        pltpu.make_async_copy(table.at[k], table.at[k], sems.at[k]).wait()

        @pl.loop(0, counts[k])
        def _(j):
            run_task(tasks[k, j], k, steps, hist, table, acc)

    if narrow:
        outs[0][...] = acc[...].astype(outs[0].dtype)
        return
    if local:
        pltpu.make_async_copy(near, outs[-1], ends.at[1]).start()
    if served:
        for wait in (False, True):
            @pl.loop(0, served)
            def _(i):
                @pl.when((used[i] != 0) | (not begun))
                def _():
                    copy = served_copy(i, True)
                    copy.wait() if wait else copy.start()
    if local:
        pltpu.make_async_copy(near, outs[-1], ends.at[1]).wait()


def window_sums(shard, group, served, local, hist_t, pieces, sums, lanes, rows, narrow=False):
    owned, excite, depth = hist_t.shape
    classes, _, panels = pieces[0][2].shape
    places = served[0].size if served else 0
    targets = owned if local else 0
    pairs = places + (local[0].size if local else 0)
    steps = depth // panels
    height = max(first + value.shape[1] for _, first, value in pieces)
    config = (
        places,
        bool(local),
        sums is not None,
        narrow,
        tuple(piece[:2] for piece in pieces),
        lanes * rows // panels,
        height,
        targets,
    )
    operands = [jnp.stack([shard * (rows // panels), group]).astype(jnp.int32), *served, *local]
    wide = [hist_t, *[piece[2] for piece in pieces]]
    before = list(sums) if sums is not None else []
    outs = [
        jax.ShapeDtypeStruct((n, excite, panels), jnp.bfloat16 if narrow else jnp.float32)
        for n in (places, targets)
        if n
    ]
    return pl.pallas_call(
        functools.partial(window_kernel, config),
        out_shape=outs,
        in_specs=[SMEM] * len(operands) + [HBM] * (len(wide) + len(before)),
        out_specs=[VMEM if narrow else HBM] * len(outs),
        scratch_shapes=[
            pltpu.VMEM((classes, rows, panels), jnp.bfloat16),
            pltpu.VMEM(hist_t.shape, hist_t.dtype),
            pltpu.VMEM((places + targets, excite, panels), jnp.float32),
            pltpu.SMEM((classes, pairs + 1), jnp.int32),
            pltpu.SMEM((classes,), jnp.int32),
            pltpu.SMEM((max(places, 1),), jnp.int32),
            pltpu.SemaphoreType.DMA((classes,)),
            pltpu.SemaphoreType.DMA((2,)),
            pltpu.SemaphoreType.DMA((max(places, 1),)),
        ],
        input_output_aliases={} if narrow else {
            len(operands) + len(wide) + n: n for n in range(len(before))
        },
        compiler_params=pltpu.CompilerParams(vmem_limit_bytes=58 * MIB),
        cost_estimate=pl.CostEstimate(
            flops=2 * pairs * panels * depth * excite,
            bytes_accessed=2 * classes * rows * panels + 2 * hist_t.size,
            transcendentals=0,
        ),
    )(*operands, *wide, *before)


def update_kernel(target_ref, near_ref, recv_ref, inverse_ref, incident_ref, out_ref, total):
    total[...] = near_ref[...]
    slots, peers = target_ref.shape

    @pl.loop(0, peers)
    def _(i):
        for c in range(slots):
            total[target_ref[c, i]] += recv_ref[i, c].astype(jnp.float32)

    for t in range(out_ref.shape[0]):
        residual = (incident_ref[t].astype(jnp.float32) - total[t].T).astype(jnp.bfloat16)
        out_ref[t] = jnp.dot(
            inverse_ref[t], residual, preferred_element_type=jnp.float32
        ).astype(out_ref.dtype)


def update(target, near, recv, inverse, incident):
    return pl.pallas_call(
        update_kernel,
        out_shape=jax.ShapeDtypeStruct(incident.shape, jnp.bfloat16),
        in_specs=[SMEM] + [VMEM] * 4,
        out_specs=VMEM,
        scratch_shapes=[pltpu.VMEM(near.shape, jnp.float32)],
        compiler_params=pltpu.CompilerParams(vmem_limit_bytes=32 * MIB),
    )(target, near, recv, inverse, incident)


def swap(value, bit, peers):
    return lax.ppermute(value, "grp", [(i, i ^ bit) for i in range(peers)])


def upper(value, peers):
    masks, held = [0], [value]
    bit = 8
    while bit < peers:
        masks += [mask ^ bit for mask in masks]
        held += [swap(value, bit, peers) for value in held]
        bit *= 2
    return masks, held


def with_other_core(found, peers):
    return found + [(mask ^ 1, first, swap(v, 1, peers)) for mask, first, v in found]


def per_device(
    weights,
    history,
    send_patch,
    send_lag,
    send_class,
    recv_target,
    local_src,
    local_lag,
    local_class,
    local_target,
    inverse_blocks,
    incident,
):
    classes, rows, panels = weights.shape
    peers, slots = send_patch.shape
    height = rows // peers
    group = lax.axis_index("grp")
    lane = lax.axis_index("lag")
    lanes = lax.axis_size("lag")
    ring = [(i, (i - 1) % lanes) for i in range(lanes)]
    served = (send_patch.T, send_lag.T, send_class.T)
    local = (local_src, local_lag, local_class, local_target)

    hist_t = jnp.swapaxes(history, 1, 2)
    half = height // 2

    def part(index, first, count):
        return lax.dynamic_slice(weights, (0, index * height + first, 0), (classes, count, panels))

    def add_shard(step, sums):
        shard = lax.rem(lane + step, lanes)
        return window_sums(shard, group, served, local, hist_t, rounds[step - 1], sums, lanes, rows)

    def neighbours(values):
        return [swap(v, 2, peers) for v in values], [swap(v, 4, peers) for v in values]

    low = lax.ppermute(part(group, 0, half), "lag", ring)
    high = lax.ppermute(part(group, half, half), "lag", ring)
    low, hist_t = lax.optimization_barrier((low, hist_t))
    corner = part(group ^ 6, 0, height)
    masks, lows = upper(low, peers)
    _, highs = upper(high, peers)
    low_x, low_y = neighbours(lows)
    high_x, high_y = neighbours(highs)
    own = jnp.concatenate([low, high], axis=1)
    turned_x, turned_y = [swap(v, 2, peers) for v in low_y], [swap(v, 4, peers) for v in high_x]
    sums = window_sums(
        lane, group * 0, served, local, hist_t, [(0, 0, weights)], None, lanes, rows
    )
    turned_x, turned_y, sums = lax.optimization_barrier((turned_x, turned_y, sums))
    found = []
    for bit, first, values in (
        (0, 0, lows),
        (0, half, highs),
        (2, 0, low_x),
        (2, half, high_x),
        (4, 0, low_y),
        (4, half, high_y),
        (6, 0, turned_x),
        (6, half, turned_y),
    ):
        found += [(m ^ bit, first, v) for m, v in zip(masks, values)]
    rounds = [with_other_core(found, peers)]
    tied = (low_x, low_y, high_x, high_y)

    for step in range(2, lanes):
        own = lax.ppermute(own, "lag", ring)
        if step == 2:
            own, corner = lax.optimization_barrier((own, corner))
            corner = lax.ppermute(corner, "lag", [(j, i) for i, j in ring])
        else:
            sums = add_shard(step - 2, sums)
            corner, sums = lax.optimization_barrier((corner, sums))
        ready, sums, tied = lax.optimization_barrier((own, sums, tied))
        masks, held = upper(ready, peers)
        if step > 2:
            across, along = tied
            found += [(m ^ 6, 0, swap(v[:, :half], 2, peers)) for m, v in zip(masks, along)]
            found += [(m ^ 6, half, swap(v[:, half:], 4, peers)) for m, v in zip(masks, across)]
            rounds.append(with_other_core(found, peers))
        across, along = tied = neighbours(held)
        found = [(m, 0, v) for m, v in zip(masks, held)]
        found += [(m ^ 2, 0, v) for m, v in zip(masks, across)]
        found += [(m ^ 4, 0, v) for m, v in zip(masks, along)]
    _, corners = upper(corner, peers)
    sums = add_shard(lanes - 2, sums)
    across, along, sums = lax.optimization_barrier((across, along, sums))
    found = [(m, 0, v) for m, v in zip(masks, held)]
    found += [(m ^ 6, 0, v) for m, v in zip(masks, corners)]
    found += [(m ^ 2, 0, v) for m, v in zip(masks, across)]
    found += [(m ^ 4, 0, v) for m, v in zip(masks, along)]
    rounds.append(with_other_core(found, peers))
    last = lax.rem(lane + lanes - 1, lanes)
    contribution = window_sums(
        last, group, served, (), hist_t, rounds[-1], sums[:1], lanes, rows, narrow=True
    )[0]
    recv = lax.all_to_all(
        contribution.reshape(peers, slots, *contribution.shape[1:]),
        "grp",
        split_axis=0,
        concat_axis=0,
        tiled=True,
    )
    near = window_sums(last, group, (), local, hist_t, rounds[-1], sums[1:], lanes, rows)[0]
    return update(recv_target.T, near, recv, inverse_blocks, incident)


def solution(mesh):
    both = ("grp", "lag")
    return jax.shard_map(
        per_device,
        mesh=mesh,
        in_specs=(
            P(None, "lag", None),
            P(both, None, None),
            P(both, None),
            P(both, None),
            P(both, None),
            P(both, None),
            P(both),
            P(both),
            P(both),
            P(both),
            P(both, None, None),
            P(both, None, None),
        ),
        out_specs=P(both, None, None),
        check_vma=False,
    )
```

```python
import functools

import jax
import jax.numpy as jnp
from jax import lax
from jax.experimental import pallas as pl
from jax.experimental.pallas import tpu as pltpu
from jax.sharding import PartitionSpec as P

SMEM = pl.BlockSpec(memory_space=pltpu.SMEM)
VMEM = pl.BlockSpec(memory_space=pltpu.VMEM)
HBM = pl.BlockSpec(memory_space=pltpu.HBM)
MIB = 1 << 20
STEP_BITS, SOURCE_BITS, LAG_BITS = 4, 8, 8
FIELDS = (STEP_BITS, SOURCE_BITS, LAG_BITS)
CHUNK = 4


def pack(step, source, lag, place):
    packed = place
    for value, bits in ((lag, LAG_BITS), (source, SOURCE_BITS), (step, STEP_BITS)):
        packed = (packed << bits) | value
    return packed


def list_tasks(base, span, total, steps, pair, tasks, counts):
    source, klass, lag, place = pair
    touched = None
    for step in range(steps // CHUNK):
        start = lax.rem(lag + step * CHUNK - base + total, total)
        first = jnp.where(start < span, start, start - total) + CHUNK - 1
        active = first >= 0
        at = counts[klass]
        tasks[klass, at] = pack(step, source, jnp.maximum(first, 0), place)
        counts[klass] = at + jnp.where(active, 1, 0)
        touched = active if touched is None else touched | active
    return touched


def run_tasks(number, klass, tasks, hist, table, acc):
    panels = table.shape[2]
    products = []
    for n in range(number):
        packed = tasks[n]
        fields = []
        for bits in FIELDS:
            fields.append(packed & ((1 << bits) - 1))
            packed = packed >> bits
        step, source, lag = fields
        columns = pl.multiple_of(step * (CHUNK * panels), CHUNK * panels)
        rows = pl.multiple_of(lag * panels, panels)
        products.append((packed, jnp.dot(
            hist[source, :, pl.ds(columns, CHUNK * panels)],
            table[klass, pl.ds(rows, CHUNK * panels), :],
            preferred_element_type=jnp.float32,
        )))
    for place, product in products:
        acc[place] += product


def window_kernel(config, *refs):
    served, local, begun, narrow, places, total, height, owned, unroll = config
    refs = list(refs)
    where = refs.pop(0)
    served_refs = [refs.pop(0) for _ in range(3 if served else 0)]
    local_refs = [refs.pop(0) for _ in range(4 if local else 0)]
    hist_ref = refs.pop(0)
    pieces = [refs.pop(0) for _ in places]
    before = [refs.pop(0) for _ in range((bool(served) + bool(local)) if begun else 0)]
    outs = [refs.pop(0) for _ in range(bool(served) + bool(local))]
    table, hist, acc, tasks, counts, used, sems, ends, served_sems = refs
    base, group = where[0], where[1]
    classes, _, panels = table.shape
    margin = (CHUNK - 1) * panels
    span = (table.shape[1] - 2 * margin) // panels
    steps = hist.shape[2] // panels

    pltpu.make_async_copy(hist_ref, hist, ends.at[0]).start()
    near = acc.at[pl.ds(served, owned)] if local else None
    if local and begun:
        pltpu.make_async_copy(before[-1], near, ends.at[1]).start()
    for k in range(classes):
        for (mask, first), piece in zip(places, pieces):
            rows = piece.shape[1]
            start = pl.multiple_of(margin + (group ^ mask) * height + first, 16)
            pltpu.make_async_copy(
                piece.at[k], table.at[k, pl.ds(start, rows), :], sems.at[k]
            ).start()
    if not begun:
        acc[...] = jnp.zeros_like(acc)
    ends_of_table = jnp.zeros((margin, panels), table.dtype)
    for k in range(classes):
        counts[k] = 0
        table[k, pl.ds(0, margin), :] = ends_of_table
        table[k, pl.ds(margin + span * panels, margin), :] = ends_of_table

    def served_copy(i, back):
        ends_of = (acc.at[i], outs[0].at[i]) if back else (before[0].at[i], acc.at[i])
        return pltpu.make_async_copy(*ends_of, served_sems.at[i])

    if served:
        slots, peers = served_refs[0].shape

        @pl.loop(0, peers)
        def _(i):
            for c in range(slots):
                source, lag, klass = (ref[c, i] for ref in served_refs)
                place = i * slots + c
                touched = list_tasks(
                    base, span, total, steps, (source, klass, lag, place), tasks, counts
                )
                needed = touched | narrow
                used[place] = jnp.where(touched, 1, 0)
                if begun:
                    @pl.when(needed)
                    def _():
                        served_copy(place, False).start()

    if local:
        @pl.loop(0, local_refs[0].shape[0])
        def _(i):
            source, lag, klass, target = (ref[i] for ref in local_refs)
            list_tasks(
                base, span, total, steps, (source, klass, lag, target + served), tasks, counts
            )

    pltpu.make_async_copy(hist_ref, hist, ends.at[0]).wait()
    if local and begun:
        pltpu.make_async_copy(before[-1], near, ends.at[1]).wait()
    if served and begun:
        @pl.loop(0, served)
        def _(i):
            @pl.when((used[i] != 0) | narrow)
            def _():
                served_copy(i, False).wait()

    spare = acc.shape[0] - 1

    @pl.loop(0, classes)
    def _(k):
        count = counts[k]
        for n in range(unroll - 1):
            tasks[k, count + n] = pack(0, 0, 0, spare)
        inner = table.at[k, pl.ds(margin, span * panels), :]
        pltpu.make_async_copy(inner, inner, sems.at[k]).wait()

        @pl.loop(0, (count + unroll - 1) // unroll)
        def _(j):
            first = j * unroll
            run_tasks(unroll, k, [tasks[k, first + n] for n in range(unroll)], hist, table, acc)

    if narrow:
        outs[0][...] = acc[pl.ds(0, served)].astype(outs[0].dtype)
        return
    if local:
        pltpu.make_async_copy(near, outs[-1], ends.at[1]).start()
    if served:
        for wait in (False, True):
            @pl.loop(0, served)
            def _(i):
                @pl.when((used[i] != 0) | (not begun))
                def _():
                    copy = served_copy(i, True)
                    copy.wait() if wait else copy.start()
    if local:
        pltpu.make_async_copy(near, outs[-1], ends.at[1]).wait()


def window_sums(shard, group, served, local, hist_t, pieces, sums, lanes, rows, narrow=False):
    owned, excite, depth = hist_t.shape
    classes, _, panels = pieces[0][2].shape
    places = served[0].size if served else 0
    targets = owned if local else 0
    pairs = places + (local[0].size if local else 0)
    steps = depth // panels
    height = max(first + value.shape[1] for _, first, value in pieces)
    config = (
        places,
        bool(local),
        sums is not None,
        narrow,
        tuple(piece[:2] for piece in pieces),
        lanes * rows // panels,
        height,
        targets,
        4 if local else 2,
    )
    operands = [jnp.stack([shard * (rows // panels), group]).astype(jnp.int32), *served, *local]
    wide = [hist_t, *[piece[2] for piece in pieces]]
    before = list(sums) if sums is not None else []
    outs = [
        jax.ShapeDtypeStruct((n, excite, panels), jnp.bfloat16 if narrow else jnp.float32)
        for n in (places, targets)
        if n
    ]
    return pl.pallas_call(
        functools.partial(window_kernel, config),
        out_shape=outs,
        in_specs=[SMEM] * len(operands) + [HBM] * (len(wide) + len(before)),
        out_specs=[VMEM if narrow else HBM] * len(outs),
        scratch_shapes=[
            pltpu.VMEM((classes, rows + 2 * (CHUNK - 1) * panels, panels), jnp.bfloat16),
            pltpu.VMEM(hist_t.shape, hist_t.dtype),
            pltpu.VMEM((places + targets + 1, excite, panels), jnp.float32),
            pltpu.SMEM((classes, pairs * (steps // CHUNK) + 4), jnp.int32),
            pltpu.SMEM((classes,), jnp.int32),
            pltpu.SMEM((max(places, 1),), jnp.int32),
            pltpu.SemaphoreType.DMA((classes,)),
            pltpu.SemaphoreType.DMA((2,)),
            pltpu.SemaphoreType.DMA((max(places, 1),)),
        ],
        input_output_aliases={} if narrow else {
            len(operands) + len(wide) + n: n for n in range(len(before))
        },
        compiler_params=pltpu.CompilerParams(vmem_limit_bytes=58 * MIB),
        cost_estimate=pl.CostEstimate(
            flops=2 * pairs * panels * depth * excite,
            bytes_accessed=2 * classes * rows * panels + 2 * hist_t.size,
            transcendentals=0,
        ),
    )(*operands, *wide, *before)


def update_kernel(target_ref, near_ref, recv_ref, inverse_ref, incident_ref, out_ref, total):
    total[...] = near_ref[...]
    slots, peers = target_ref.shape

    @pl.loop(0, peers)
    def _(i):
        for c in range(slots):
            total[target_ref[c, i]] += recv_ref[i, c].astype(jnp.float32)

    for t in range(out_ref.shape[0]):
        residual = (incident_ref[t].astype(jnp.float32) - total[t].T).astype(jnp.bfloat16)
        out_ref[t] = jnp.dot(
            inverse_ref[t], residual, preferred_element_type=jnp.float32
        ).astype(out_ref.dtype)


def update(target, near, recv, inverse, incident):
    return pl.pallas_call(
        update_kernel,
        out_shape=jax.ShapeDtypeStruct(incident.shape, jnp.bfloat16),
        in_specs=[SMEM] + [VMEM] * 4,
        out_specs=VMEM,
        scratch_shapes=[pltpu.VMEM(near.shape, jnp.float32)],
        compiler_params=pltpu.CompilerParams(vmem_limit_bytes=32 * MIB),
    )(target, near, recv, inverse, incident)


def swap(value, bit, peers):
    return lax.ppermute(value, "grp", [(i, i ^ bit) for i in range(peers)])


def upper(value, peers):
    masks, held = [0], [value]
    bit = 8
    while bit < peers:
        masks += [mask ^ bit for mask in masks]
        held += [swap(value, bit, peers) for value in held]
        bit *= 2
    return masks, held


def with_other_core(found, peers):
    return found + [(mask ^ 1, first, swap(v, 1, peers)) for mask, first, v in found]


def per_device(
    weights,
    history,
    send_patch,
    send_lag,
    send_class,
    recv_target,
    local_src,
    local_lag,
    local_class,
    local_target,
    inverse_blocks,
    incident,
):
    classes, rows, panels = weights.shape
    peers, slots = send_patch.shape
    height = rows // peers
    group = lax.axis_index("grp")
    lane = lax.axis_index("lag")
    lanes = lax.axis_size("lag")
    ring = [(i, (i - 1) % lanes) for i in range(lanes)]
    served = (send_patch.T, send_lag.T, send_class.T)
    local = (local_src, local_lag, local_class, local_target)

    hist_t = jnp.swapaxes(history, 1, 2)
    half = height // 2

    def part(index):
        return lax.dynamic_slice(weights, (0, index * height, 0), (classes, height, panels))

    def add_shard(step, sums):
        shard = lax.rem(lane + step, lanes)
        return window_sums(shard, group, served, local, hist_t, rounds[step - 1], sums, lanes, rows)

    sums = window_sums(
        lane, group * 0, served, local, hist_t, [(0, 0, weights)], None, lanes, rows
    )
    own = part(group)
    corner = part(group ^ 6)
    rounds = []
    for step in range(1, lanes):
        own = lax.ppermute(own, "lag", ring)
        if step == 1:
            ready, sums = lax.optimization_barrier((own, sums))
        else:
            if step > 2:
                sums = add_shard(step - 2, sums)
            ready, corner, sums, across, along = lax.optimization_barrier(
                (own, corner, sums, across, along)
            )
            found = [(m, 0, v) for m, v in zip(masks, held)]
            found += [(m ^ 2, 0, v) for m, v in zip(masks, across)]
            found += [(m ^ 4, 0, v) for m, v in zip(masks, along)]
            found += [(m ^ 6, 0, swap(v[:, :half], 2, peers)) for m, v in zip(masks, along)]
            found += [(m ^ 6, half, swap(v[:, half:], 4, peers)) for m, v in zip(masks, across)]
            rounds.append(with_other_core(found, peers))
        masks, held = upper(ready, peers)
        across = [swap(value, 2, peers) for value in held]
        along = [swap(value, 4, peers) for value in held]
    corner = lax.ppermute(corner, "lag", [(j, i) for i, j in ring])
    if lanes > 2:
        sums = add_shard(lanes - 2, sums)
        across, along, corner, sums = lax.optimization_barrier((across, along, corner, sums))
    _, corners = upper(corner, peers)
    found = [(m, 0, v) for m, v in zip(masks, held)]
    found += [(m ^ 2, 0, v) for m, v in zip(masks, across)]
    found += [(m ^ 4, 0, v) for m, v in zip(masks, along)]
    found += [(m ^ 6, 0, v) for m, v in zip(masks, corners)]
    rounds.append(with_other_core(found, peers))
    last = lax.rem(lane + lanes - 1, lanes)
    contribution = window_sums(
        last, group, served, (), hist_t, rounds[-1], sums[:1], lanes, rows, narrow=True
    )[0]
    recv = lax.all_to_all(
        contribution.reshape(peers, slots, *contribution.shape[1:]),
        "grp",
        split_axis=0,
        concat_axis=0,
        tiled=True,
    )
    near = window_sums(last, group, (), local, hist_t, rounds[-1], sums[1:], lanes, rows)[0]
    return update(recv_target.T, near, recv, inverse_blocks, incident)


def solution(mesh):
    both = ("grp", "lag")
    return jax.shard_map(
        per_device,
        mesh=mesh,
        in_specs=(
            P(None, "lag", None),
            P(both, None, None),
            P(both, None),
            P(both, None),
            P(both, None),
            P(both, None),
            P(both),
            P(both),
            P(both),
            P(both),
            P(both, None, None),
            P(both, None, None),
        ),
        out_specs=P(both, None, None),
        check_vma=False,
    )
```

```python
import functools

import jax
import jax.numpy as jnp
from jax import lax
from jax.experimental import pallas as pl
from jax.experimental.pallas import tpu as pltpu
from jax.sharding import PartitionSpec as P

SMEM = pl.BlockSpec(memory_space=pltpu.SMEM)
VMEM = pl.BlockSpec(memory_space=pltpu.VMEM)
HBM = pl.BlockSpec(memory_space=pltpu.HBM)
MIB = 1 << 20
STEP_BITS, SOURCE_BITS, LAG_BITS = 4, 8, 8
FIELDS = (STEP_BITS, SOURCE_BITS, LAG_BITS)
CHUNK = 4


def pack(step, source, lag, place):
    packed = place
    for value, bits in ((lag, LAG_BITS), (source, SOURCE_BITS), (step, STEP_BITS)):
        packed = (packed << bits) | value
    return packed


def list_tasks(base, span, total, steps, pair, tasks, counts):
    source, klass, lag, place = pair
    touched = None
    for step in range(steps // CHUNK):
        start = lax.rem(lag + step * CHUNK - base + total, total)
        first = jnp.where(start < span, start, start - total) + CHUNK - 1
        active = first >= 0
        at = counts[klass]
        tasks[klass, at] = pack(step, source, jnp.maximum(first, 0), place)
        counts[klass] = at + jnp.where(active, 1, 0)
        touched = active if touched is None else touched | active
    return touched


def run_tasks(number, klass, tasks, hist, table, acc):
    panels = table.shape[2]
    products = []
    for n in range(number):
        packed = tasks[n]
        fields = []
        for bits in FIELDS:
            fields.append(packed & ((1 << bits) - 1))
            packed = packed >> bits
        step, source, lag = fields
        columns = pl.multiple_of(step * (CHUNK * panels), CHUNK * panels)
        rows = pl.multiple_of(lag * panels, panels)
        products.append((packed, jnp.dot(
            hist[source, :, pl.ds(columns, CHUNK * panels)],
            table[klass, pl.ds(rows, CHUNK * panels), :],
            preferred_element_type=jnp.float32,
        )))
    for place, product in products:
        acc[place] += product


def window_kernel(config, *refs):
    served, local, begun, narrow, places, total, height, owned, unroll = config
    refs = list(refs)
    where = refs.pop(0)
    served_refs = [refs.pop(0) for _ in range(3 if served else 0)]
    local_refs = [refs.pop(0) for _ in range(4 if local else 0)]
    hist_ref = refs.pop(0)
    pieces = [refs.pop(0) for _ in places]
    before = [refs.pop(0) for _ in range((bool(served) + bool(local)) if begun else 0)]
    outs = [refs.pop(0) for _ in range(bool(served) + bool(local))]
    table, hist, acc, tasks, counts, used, sems, ends, served_sems = refs
    base, group = where[0], where[1]
    classes, _, panels = table.shape
    margin = (CHUNK - 1) * panels
    span = (table.shape[1] - 2 * margin) // panels
    steps = hist.shape[2] // panels

    pltpu.make_async_copy(hist_ref, hist, ends.at[0]).start()
    near = acc.at[pl.ds(served, owned)] if local else None
    if local and begun:
        pltpu.make_async_copy(before[-1], near, ends.at[1]).start()
    for k in range(classes):
        for (mask, first), piece in zip(places, pieces):
            rows = piece.shape[1]
            start = pl.multiple_of(margin + (group ^ mask) * height + first, 16)
            pltpu.make_async_copy(
                piece.at[k], table.at[k, pl.ds(start, rows), :], sems.at[k]
            ).start()
    if not begun:
        acc[...] = jnp.zeros_like(acc)
    ends_of_table = jnp.zeros((margin, panels), table.dtype)
    for k in range(classes):
        counts[k] = 0
        table[k, pl.ds(0, margin), :] = ends_of_table
        table[k, pl.ds(margin + span * panels, margin), :] = ends_of_table

    def served_copy(i, back):
        ends_of = (acc.at[i], outs[0].at[i]) if back else (before[0].at[i], acc.at[i])
        return pltpu.make_async_copy(*ends_of, served_sems.at[i])

    if served:
        slots, peers = served_refs[0].shape

        @pl.loop(0, peers)
        def _(i):
            for c in range(slots):
                source, lag, klass = (ref[c, i] for ref in served_refs)
                place = i * slots + c
                touched = list_tasks(
                    base, span, total, steps, (source, klass, lag, place), tasks, counts
                )
                needed = touched | narrow
                used[place] = jnp.where(touched, 1, 0)
                if begun:
                    @pl.when(needed)
                    def _():
                        served_copy(place, False).start()

    if local:
        @pl.loop(0, local_refs[0].shape[0])
        def _(i):
            source, lag, klass, target = (ref[i] for ref in local_refs)
            list_tasks(
                base, span, total, steps, (source, klass, lag, target + served), tasks, counts
            )

    pltpu.make_async_copy(hist_ref, hist, ends.at[0]).wait()
    if local and begun:
        pltpu.make_async_copy(before[-1], near, ends.at[1]).wait()
    if served and begun:
        @pl.loop(0, served)
        def _(i):
            @pl.when((used[i] != 0) | narrow)
            def _():
                served_copy(i, False).wait()

    spare = acc.shape[0] - 1

    @pl.loop(0, classes)
    def _(k):
        count = counts[k]
        for n in range(unroll - 1):
            tasks[k, count + n] = pack(0, 0, 0, spare)
        inner = table.at[k, pl.ds(margin, span * panels), :]
        pltpu.make_async_copy(inner, inner, sems.at[k]).wait()

        @pl.loop(0, (count + unroll - 1) // unroll)
        def _(j):
            first = j * unroll
            run_tasks(unroll, k, [tasks[k, first + n] for n in range(unroll)], hist, table, acc)

    if narrow:
        outs[0][...] = acc[pl.ds(0, served)].astype(outs[0].dtype)
        return
    if local:
        pltpu.make_async_copy(near, outs[-1], ends.at[1]).start()
    if served:
        for wait in (False, True):
            @pl.loop(0, served)
            def _(i):
                @pl.when((used[i] != 0) | (not begun))
                def _():
                    copy = served_copy(i, True)
                    copy.wait() if wait else copy.start()
    if local:
        pltpu.make_async_copy(near, outs[-1], ends.at[1]).wait()


def window_sums(shard, group, served, local, hist_t, pieces, sums, lanes, rows, narrow=False):
    owned, excite, depth = hist_t.shape
    classes, _, panels = pieces[0][2].shape
    places = served[0].size if served else 0
    targets = owned if local else 0
    pairs = places + (local[0].size if local else 0)
    steps = depth // panels
    height = max(first + value.shape[1] for _, first, value in pieces)
    config = (
        places,
        bool(local),
        sums is not None,
        narrow,
        tuple(piece[:2] for piece in pieces),
        lanes * rows // panels,
        height,
        targets,
        4 if local else 2,
    )
    operands = [jnp.stack([shard * (rows // panels), group]).astype(jnp.int32), *served, *local]
    wide = [hist_t, *[piece[2] for piece in pieces]]
    before = list(sums) if sums is not None else []
    outs = [
        jax.ShapeDtypeStruct((n, excite, panels), jnp.bfloat16 if narrow else jnp.float32)
        for n in (places, targets)
        if n
    ]
    return pl.pallas_call(
        functools.partial(window_kernel, config),
        out_shape=outs,
        in_specs=[SMEM] * len(operands) + [HBM] * (len(wide) + len(before)),
        out_specs=[VMEM if narrow else HBM] * len(outs),
        scratch_shapes=[
            pltpu.VMEM((classes, rows + 2 * (CHUNK - 1) * panels, panels), jnp.bfloat16),
            pltpu.VMEM(hist_t.shape, hist_t.dtype),
            pltpu.VMEM((places + targets + 1, excite, panels), jnp.float32),
            pltpu.SMEM((classes, pairs * (steps // CHUNK) + 4), jnp.int32),
            pltpu.SMEM((classes,), jnp.int32),
            pltpu.SMEM((max(places, 1),), jnp.int32),
            pltpu.SemaphoreType.DMA((classes,)),
            pltpu.SemaphoreType.DMA((2,)),
            pltpu.SemaphoreType.DMA((max(places, 1),)),
        ],
        input_output_aliases={} if narrow else {
            len(operands) + len(wide) + n: n for n in range(len(before))
        },
        compiler_params=pltpu.CompilerParams(vmem_limit_bytes=58 * MIB),
        cost_estimate=pl.CostEstimate(
            flops=2 * pairs * panels * depth * excite,
            bytes_accessed=2 * classes * rows * panels + 2 * hist_t.size,
            transcendentals=0,
        ),
    )(*operands, *wide, *before)


def update_kernel(target_ref, near_ref, recv_ref, inverse_ref, incident_ref, out_ref, total):
    total[...] = near_ref[...]
    slots, peers = target_ref.shape

    @pl.loop(0, peers)
    def _(i):
        for c in range(slots):
            total[target_ref[c, i]] += recv_ref[i, c].astype(jnp.float32)

    for t in range(out_ref.shape[0]):
        residual = (incident_ref[t].astype(jnp.float32) - total[t].T).astype(jnp.bfloat16)
        out_ref[t] = jnp.dot(
            inverse_ref[t], residual, preferred_element_type=jnp.float32
        ).astype(out_ref.dtype)


def update(target, near, recv, inverse, incident):
    return pl.pallas_call(
        update_kernel,
        out_shape=jax.ShapeDtypeStruct(incident.shape, jnp.bfloat16),
        in_specs=[SMEM] + [VMEM] * 4,
        out_specs=VMEM,
        scratch_shapes=[pltpu.VMEM(near.shape, jnp.float32)],
        compiler_params=pltpu.CompilerParams(vmem_limit_bytes=32 * MIB),
    )(target, near, recv, inverse, incident)


def swap(value, bit, peers):
    return lax.ppermute(value, "grp", [(i, i ^ bit) for i in range(peers)])


def upper(value, peers):
    masks, held = [0], [value]
    bit = 8
    while bit < peers:
        masks += [mask ^ bit for mask in masks]
        held += [swap(value, bit, peers) for value in held]
        bit *= 2
    return masks, held


def with_other_core(found, peers):
    return found + [(mask ^ 1, first, swap(v, 1, peers)) for mask, first, v in found]


def per_device(
    weights,
    history,
    send_patch,
    send_lag,
    send_class,
    recv_target,
    local_src,
    local_lag,
    local_class,
    local_target,
    inverse_blocks,
    incident,
):
    classes, rows, panels = weights.shape
    peers, slots = send_patch.shape
    height = rows // peers
    group = lax.axis_index("grp")
    lane = lax.axis_index("lag")
    lanes = lax.axis_size("lag")
    ring = [(i, (i - 1) % lanes) for i in range(lanes)]
    served = (send_patch.T, send_lag.T, send_class.T)
    local = (local_src, local_lag, local_class, local_target)

    hist_t = jnp.swapaxes(history, 1, 2)
    half = height // 2

    def part(index):
        return lax.dynamic_slice(weights, (0, index * height, 0), (classes, height, panels))

    def add_shard(step, sums):
        shard = lax.rem(lane + step, lanes)
        return window_sums(shard, group, served, local, hist_t, rounds[step - 1], sums, lanes, rows)

    sums = window_sums(
        lane, group * 0, served, local, hist_t, [(0, 0, weights)], None, lanes, rows
    )
    own = part(group)
    corner = part(group ^ 6)

    def neighbours(value):
        masks, held = upper(value, peers)
        return (
            [(m, 0, v) for m, v in zip(masks, held)],
            [(m ^ 2, 0, swap(v, 2, peers)) for m, v in zip(masks, held)],
            [(m ^ 4, 0, swap(v, 4, peers)) for m, v in zip(masks, held)],
        )

    def tie(*values):
        leaves, tree = jax.tree.flatten(values)
        arrays = lax.optimization_barrier([v for v in leaves if not isinstance(v, int)])
        return jax.tree.unflatten(
            tree, [v if isinstance(v, int) else arrays.pop(0) for v in leaves]
        )

    def corners(value):
        masks, held = upper(value, peers)
        return [(m ^ 6, 0, v) for m, v in zip(masks, held)]

    own = lax.ppermute(own, "lag", ring)
    own, sums = tie(own, sums)
    trio = neighbours(own)
    own = lax.ppermute(own, "lag", ring)
    trio, own, corner = tie(trio, own, corner)
    found = with_other_core(sum(trio, []), peers)
    held, across, along = neighbours(own)
    diagonal = lax.ppermute(corner, "lag", ring)
    held = with_other_core(held, peers)
    across, along, own, diagonal, found, held = tie(across, along, own, diagonal, found, held)
    diagonal = with_other_core(corners(diagonal), peers)
    rounds = [found + diagonal]
    for step in range(2, lanes - 1):
        own = lax.ppermute(own, "lag", ring)
        turned = [(m ^ 2, 0, swap(v[:, :half], 2, peers)) for m, _, v in along]
        turned += [(m ^ 4, half, swap(v[:, half:], 4, peers)) for m, _, v in across]
        if step == 2:
            rounds[0], across, along = tie(rounds[0], across, along)
        found = held + with_other_core(across + along, peers)
        sums = add_shard(step - 1, sums)
        own, turned, sums, corner, found = tie(own, turned, sums, corner, found)
        held, across, along = neighbours(own)
        found, held = tie(found + with_other_core(turned, peers), held)
        rounds.append(found)
        held = with_other_core(held, peers)
        if step < lanes - 2:
            across, along, own = tie(across, along, own)
    diagonal = lax.ppermute(corner, "lag", [(j, i) for i, j in ring])
    sums = add_shard(lanes - 2, sums)
    across, along, diagonal, sums = tie(across, along, diagonal, sums)
    rounds.append(held + with_other_core(across + along + corners(diagonal), peers))
    last = lax.rem(lane + lanes - 1, lanes)
    contribution = window_sums(
        last, group, served, (), hist_t, rounds[-1], sums[:1], lanes, rows, narrow=True
    )[0]
    recv = lax.all_to_all(
        contribution.reshape(peers, slots, *contribution.shape[1:]),
        "grp",
        split_axis=0,
        concat_axis=0,
        tiled=True,
    )
    near = window_sums(last, group, (), local, hist_t, rounds[-1], sums[1:], lanes, rows)[0]
    return update(recv_target.T, near, recv, inverse_blocks, incident)


def solution(mesh):
    both = ("grp", "lag")
    return jax.shard_map(
        per_device,
        mesh=mesh,
        in_specs=(
            P(None, "lag", None),
            P(both, None, None),
            P(both, None),
            P(both, None),
            P(both, None),
            P(both, None),
            P(both),
            P(both),
            P(both),
            P(both),
            P(both, None, None),
            P(both, None, None),
        ),
        out_specs=P(both, None, None),
        check_vma=False,
    )
```

```python
import functools

import jax
import jax.numpy as jnp
from jax import lax
from jax.experimental import pallas as pl
from jax.experimental.pallas import tpu as pltpu
from jax.sharding import PartitionSpec as P

SMEM = pl.BlockSpec(memory_space=pltpu.SMEM)
VMEM = pl.BlockSpec(memory_space=pltpu.VMEM)
HBM = pl.BlockSpec(memory_space=pltpu.HBM)
MIB = 1 << 20
HALF_BITS, SOURCE_BITS, CLASS_BITS, LAG_BITS = 1, 8, 4, 8
FIELDS = (HALF_BITS, SOURCE_BITS, CLASS_BITS, LAG_BITS)
UNROLL = 2


def pack(half, source, klass, lag, place):
    packed = place
    for value, bits in ((lag, LAG_BITS), (klass, CLASS_BITS), (source, SOURCE_BITS), (half, HALF_BITS)):
        packed = (packed << bits) | value
    return packed


def list_task(base, span, total, steps, phased, pair, tasks, counts):
    source, klass, lag, place = pair
    half = steps // 2
    start = lax.rem(lag - base + total, total)
    first = jnp.where(start < span, start, start - total)
    whole = (first > -half) & (first < span - half)
    lower = (first >= span - half) & (first < span)
    upper_half = (first > -steps) & (first <= -half)
    row = jnp.maximum(first + half - 1, 0)
    number = 2 * klass if phased else 0
    at = counts[number]
    tasks[number, at] = pack(0, source, klass, row, place)
    counts[number] = at + jnp.where(whole, 1, 0)
    at = counts[number + 1]
    second = jnp.where(upper_half, 1, 0)
    row = jnp.maximum(first + half - 1 + half * second, 0)
    tasks[number + 1, at] = pack(second, source, klass, row, place)
    counts[number + 1] = at + jnp.where(lower | upper_half, 1, 0)
    return whole | lower | upper_half


def run_list(number, width, spare, tasks, counts, hist, table, acc):
    panels = table.shape[2]
    count = counts[number]
    for n in range(UNROLL - 1):
        tasks[number, count + n] = pack(0, 0, 0, 0, spare)

    @pl.loop(0, (count + UNROLL - 1) // UNROLL)
    def _(j):
        for n in range(UNROLL):
            packed = tasks[number, j * UNROLL + n]
            fields = []
            for bits in FIELDS:
                fields.append(packed & ((1 << bits) - 1))
                packed = packed >> bits
            half, source, klass, lag = fields
            columns = pl.multiple_of(half * (width * panels), width * panels)
            rows = pl.multiple_of(lag * panels, panels)
            acc[packed] += jnp.dot(
                hist[source, :, pl.ds(columns, width * panels)],
                table[klass, pl.ds(rows, width * panels), :],
                preferred_element_type=jnp.float32,
            )


def window_kernel(config, *refs):
    served, local, begun, narrow, places, total, rows, height, owned = config
    refs = list(refs)
    where = refs.pop(0)
    served_refs = [refs.pop(0) for _ in range(3 if served else 0)]
    local_refs = [refs.pop(0) for _ in range(4 if local else 0)]
    hist_ref = refs.pop(0)
    pieces = [refs.pop(0) for _ in places]
    before = [refs.pop(0) for _ in range((bool(served) + bool(local)) if begun else 0)]
    outs = [refs.pop(0) for _ in range(bool(served) + bool(local))]
    table, hist, acc, tasks, counts, used, sems, ends, served_sems = refs
    base, group = where[0], where[1]
    classes, _, panels = table.shape
    steps = hist.shape[2] // panels
    margin = (steps // 2 - 1) * panels
    span = (table.shape[1] - 2 * margin) // panels
    phased = bool(local)

    pltpu.make_async_copy(hist_ref, hist, ends.at[0]).start()
    near = acc.at[pl.ds(served, owned)] if local else None
    if local and begun:
        pltpu.make_async_copy(before[-1], near, ends.at[1]).start()
    for k in range(classes):
        for (slot, mask, first), piece in zip(places, pieces):
            start = pl.multiple_of(margin + slot * rows + (group ^ mask) * height + first, 16)
            pltpu.make_async_copy(
                piece.at[k], table.at[k, pl.ds(start, piece.shape[1]), :], sems.at[k]
            ).start()
    if not begun:
        acc[...] = jnp.zeros_like(acc)
    ends_of_table = jnp.zeros((margin, panels), table.dtype)
    for k in range(classes):
        counts[2 * k] = 0
        counts[2 * k + 1] = 0
        table[k, pl.ds(0, margin), :] = ends_of_table
        table[k, pl.ds(margin + span * panels, margin), :] = ends_of_table

    def served_copy(i, back):
        ends_of = (acc.at[i], outs[0].at[i]) if back else (before[0].at[i], acc.at[i])
        return pltpu.make_async_copy(*ends_of, served_sems.at[i])

    if served:
        slots, peers = served_refs[0].shape

        @pl.loop(0, peers)
        def _(i):
            for c in range(slots):
                source, lag, klass = (ref[c, i] for ref in served_refs)
                place = i * slots + c
                pair = (source, klass, lag, place)
                touched = list_task(base, span, total, steps, phased, pair, tasks, counts)
                needed = touched | narrow
                used[place] = jnp.where(touched, 1, 0)
                if begun:
                    @pl.when(needed)
                    def _():
                        served_copy(place, False).start()

    if local:
        @pl.loop(0, local_refs[0].shape[0])
        def _(i):
            source, lag, klass, target = (ref[i] for ref in local_refs)
            pair = (source, klass, lag, target + served)
            list_task(base, span, total, steps, phased, pair, tasks, counts)

    pltpu.make_async_copy(hist_ref, hist, ends.at[0]).wait()
    if local and begun:
        pltpu.make_async_copy(before[-1], near, ends.at[1]).wait()
    if served and begun:
        @pl.loop(0, served)
        def _(i):
            @pl.when((used[i] != 0) | narrow)
            def _():
                served_copy(i, False).wait()

    spare = acc.shape[0] - 1

    def wait_class(k):
        inner = table.at[k, pl.ds(margin, span * panels), :]
        pltpu.make_async_copy(inner, inner, sems.at[k]).wait()

    def run_lists(number):
        run_list(number, steps, spare, tasks, counts, hist, table, acc)
        run_list(number + 1, steps // 2, spare, tasks, counts, hist, table, acc)

    if phased:
        @pl.loop(0, classes)
        def _(k):
            wait_class(k)
            run_lists(2 * k)
    else:
        for k in range(classes):
            wait_class(k)
        run_lists(0)

    if narrow:
        outs[0][...] = acc[pl.ds(0, served)].astype(outs[0].dtype)
        return
    if local:
        pltpu.make_async_copy(near, outs[-1], ends.at[1]).start()
    if served:
        for wait in (False, True):
            @pl.loop(0, served)
            def _(i):
                @pl.when((used[i] != 0) | (not begun))
                def _():
                    copy = served_copy(i, True)
                    copy.wait() if wait else copy.start()
    if local:
        pltpu.make_async_copy(near, outs[-1], ends.at[1]).wait()


def window_sums(shard, group, served, local, hist_t, shards, sums, lanes, rows, narrow=False):
    owned, excite, depth = hist_t.shape
    pieces = [(slot, *piece) for slot, found in enumerate(shards) for piece in found]
    classes, _, panels = pieces[0][3].shape
    places = served[0].size if served else 0
    targets = owned if local else 0
    pairs = places + (local[0].size if local else 0)
    steps = depth // panels
    config = (
        places,
        bool(local),
        sums is not None,
        narrow,
        tuple(piece[:3] for piece in pieces),
        lanes * rows // panels,
        rows,
        max(first + value.shape[1] for _, _, first, value in pieces),
        targets,
    )
    operands = [jnp.stack([shard * (rows // panels), group]).astype(jnp.int32), *served, *local]
    wide = [hist_t, *[piece[3] for piece in pieces]]
    before = list(sums) if sums is not None else []
    outs = [
        jax.ShapeDtypeStruct((n, excite, panels), jnp.bfloat16 if narrow else jnp.float32)
        for n in (places, targets)
        if n
    ]
    depth_of_table = len(shards) * rows + 2 * (steps // 2 - 1) * panels
    return pl.pallas_call(
        functools.partial(window_kernel, config),
        out_shape=outs,
        in_specs=[SMEM] * len(operands) + [HBM] * (len(wide) + len(before)),
        out_specs=[VMEM if narrow else HBM] * len(outs),
        scratch_shapes=[
            pltpu.VMEM((classes, depth_of_table, panels), jnp.bfloat16),
            pltpu.VMEM(hist_t.shape, hist_t.dtype),
            pltpu.VMEM((places + targets + 1, excite, panels), jnp.float32),
            pltpu.SMEM((2 * classes, pairs + UNROLL), jnp.int32),
            pltpu.SMEM((2 * classes,), jnp.int32),
            pltpu.SMEM((max(places, 1),), jnp.int32),
            pltpu.SemaphoreType.DMA((classes,)),
            pltpu.SemaphoreType.DMA((2,)),
            pltpu.SemaphoreType.DMA((max(places, 1),)),
        ],
        input_output_aliases={} if narrow else {
            len(operands) + len(wide) + n: n for n in range(len(before))
        },
        compiler_params=pltpu.CompilerParams(vmem_limit_bytes=58 * MIB),
        cost_estimate=pl.CostEstimate(
            flops=2 * pairs * panels * depth * excite,
            bytes_accessed=2 * classes * len(shards) * rows * panels + 2 * hist_t.size,
            transcendentals=0,
        ),
    )(*operands, *wide, *before)


def update_kernel(target_ref, near_ref, recv_ref, inverse_ref, incident_ref, out_ref, total):
    total[...] = near_ref[...]
    slots, peers = target_ref.shape

    @pl.loop(0, peers)
    def _(i):
        for c in range(slots):
            total[target_ref[c, i]] += recv_ref[i, c].astype(jnp.float32)

    for t in range(out_ref.shape[0]):
        residual = (incident_ref[t].astype(jnp.float32) - total[t].T).astype(jnp.bfloat16)
        out_ref[t] = jnp.dot(
            inverse_ref[t], residual, preferred_element_type=jnp.float32
        ).astype(out_ref.dtype)


def update(target, near, recv, inverse, incident):
    return pl.pallas_call(
        update_kernel,
        out_shape=jax.ShapeDtypeStruct(incident.shape, jnp.bfloat16),
        in_specs=[SMEM] + [VMEM] * 4,
        out_specs=VMEM,
        scratch_shapes=[pltpu.VMEM(near.shape, jnp.float32)],
        compiler_params=pltpu.CompilerParams(vmem_limit_bytes=32 * MIB),
    )(target, near, recv, inverse, incident)


def swap(value, bit, peers):
    return lax.ppermute(value, "grp", [(i, i ^ bit) for i in range(peers)])


def upper(value, peers):
    masks, held = [0], [value]
    bit = 8
    while bit < peers:
        masks += [mask ^ bit for mask in masks]
        held += [swap(value, bit, peers) for value in held]
        bit *= 2
    return masks, held


def with_other_core(found, peers):
    return found + [(mask ^ 1, first, swap(v, 1, peers)) for mask, first, v in found]


def per_device(
    weights,
    history,
    send_patch,
    send_lag,
    send_class,
    recv_target,
    local_src,
    local_lag,
    local_class,
    local_target,
    inverse_blocks,
    incident,
):
    classes, rows, panels = weights.shape
    peers, slots = send_patch.shape
    height = rows // peers
    group = lax.axis_index("grp")
    lane = lax.axis_index("lag")
    lanes = lax.axis_size("lag")
    ring = [(i, (i - 1) % lanes) for i in range(lanes)]
    served = (send_patch.T, send_lag.T, send_class.T)
    local = (local_src, local_lag, local_class, local_target)

    hist_t = jnp.swapaxes(history, 1, 2)
    half = height // 2

    def part(index):
        return lax.dynamic_slice(weights, (0, index * height, 0), (classes, height, panels))

    def add_shard(step, sums, served=served, local=local, **options):
        shard = lax.rem(lane + step, lanes)
        shards = rounds[step - 1 : step] if served else rounds[step - 1 :]
        return window_sums(
            shard, group, served, local, hist_t, shards, sums, lanes, rows, **options
        )

    sums = window_sums(
        lane, group * 0, served, local, hist_t, [[(0, 0, weights)]], None, lanes, rows
    )
    own = part(group)
    corner = part(group ^ 6)

    def neighbours(value):
        masks, held = upper(value, peers)
        return (
            [(m, 0, v) for m, v in zip(masks, held)],
            [(m ^ 2, 0, swap(v, 2, peers)) for m, v in zip(masks, held)],
            [(m ^ 4, 0, swap(v, 4, peers)) for m, v in zip(masks, held)],
        )

    def tie(*values):
        leaves, tree = jax.tree.flatten(values)
        arrays = lax.optimization_barrier([v for v in leaves if not isinstance(v, int)])
        return jax.tree.unflatten(
            tree, [v if isinstance(v, int) else arrays.pop(0) for v in leaves]
        )

    def corners(value):
        masks, held = upper(value, peers)
        return [(m ^ 6, 0, v) for m, v in zip(masks, held)]

    own = lax.ppermute(own, "lag", ring)
    own, sums = tie(own, sums)
    trio = neighbours(own)
    own = lax.ppermute(own, "lag", ring)
    trio, own, corner = tie(trio, own, corner)
    found = with_other_core(sum(trio, []), peers)
    held, across, along = neighbours(own)
    diagonal = lax.ppermute(corner, "lag", ring)
    held = with_other_core(held, peers)
    across, along, own, diagonal, found, held = tie(across, along, own, diagonal, found, held)
    diagonal = with_other_core(corners(diagonal), peers)
    rounds = [found + diagonal]
    for step in range(2, lanes - 1):
        own = lax.ppermute(own, "lag", ring)
        turned = [(m ^ 2, 0, swap(v[:, :half], 2, peers)) for m, _, v in along]
        turned += [(m ^ 4, half, swap(v[:, half:], 4, peers)) for m, _, v in across]
        if step == 2:
            rounds[0], across, along = tie(rounds[0], across, along)
        found = held + with_other_core(across + along, peers)
        sums = add_shard(step - 1, sums)
        own, turned, sums, corner, found = tie(own, turned, sums, corner, found)
        held, across, along = neighbours(own)
        found, held = tie(found + with_other_core(turned, peers), held)
        rounds.append(found)
        held = with_other_core(held, peers)
        if step < lanes - 2:
            across, along, own = tie(across, along, own)
    diagonal = lax.ppermute(corner, "lag", [(j, i) for i, j in ring])
    served_sums, near = sums
    served_sums = add_shard(lanes - 2, [served_sums], local=())[0]
    across, along, diagonal, served_sums = tie(across, along, diagonal, served_sums)
    rounds.append(held + with_other_core(across + along + corners(diagonal), peers))
    contribution = add_shard(lanes - 1, [served_sums], local=(), narrow=True)[0]
    recv = lax.all_to_all(
        contribution.reshape(peers, slots, *contribution.shape[1:]),
        "grp",
        split_axis=0,
        concat_axis=0,
        tiled=True,
    )
    near = add_shard(lanes - 2, [near], served=())[0]
    return update(recv_target.T, near, recv, inverse_blocks, incident)


def solution(mesh):
    both = ("grp", "lag")
    return jax.shard_map(
        per_device,
        mesh=mesh,
        in_specs=(
            P(None, "lag", None),
            P(both, None, None),
            P(both, None),
            P(both, None),
            P(both, None),
            P(both, None),
            P(both),
            P(both),
            P(both),
            P(both),
            P(both, None, None),
            P(both, None, None),
        ),
        out_specs=P(both, None, None),
        check_vma=False,
    )
```

```python
import functools

import jax
import jax.numpy as jnp
from jax import lax
from jax.experimental import pallas as pl
from jax.experimental.pallas import tpu as pltpu
from jax.sharding import PartitionSpec as P

SMEM = pl.BlockSpec(memory_space=pltpu.SMEM)
VMEM = pl.BlockSpec(memory_space=pltpu.VMEM)
HBM = pl.BlockSpec(memory_space=pltpu.HBM)
MIB = 1 << 20
CLASS_BITS, LAG_BITS = 4, 8
BESIDE = 2


def pack(klass, lag, place):
    return (((place << LAG_BITS) | lag) << CLASS_BITS) | klass


def list_task(base, span, total, steps, pair, tasks, counts):
    source, klass, lag, place = pair
    half = steps // 2
    start = lax.rem(lag - base + total, total)
    first = jnp.where(start < span, start, start - total)
    whole = (first > -half) & (first < span - half)
    lower = (first >= span - half) & (first < span)
    higher = (first > -steps) & (first <= -half)
    row = jnp.maximum(first + half - 1 + jnp.where(higher, half, 0), 0)
    number = 3 * source + jnp.where(lower, 1, 0) + jnp.where(higher, 2, 0)
    active = whole | lower | higher
    at = counts[number]
    tasks[number, at] = pack(klass, row, place)
    counts[number] = at + jnp.where(active, 1, 0)
    return active


def run_list(number, source, column, width, spare, tasks, counts, hist, table, acc):
    panels = table.shape[2]
    count = counts[number]
    for n in range(BESIDE - 1):
        tasks[number, count + n] = pack(0, 0, spare)

    @pl.loop(0, (count + BESIDE - 1) // BESIDE)
    def _(j):
        windows, places = [], []
        for n in range(BESIDE):
            packed = tasks[number, j * BESIDE + n]
            klass = packed & ((1 << CLASS_BITS) - 1)
            lag = (packed >> CLASS_BITS) & ((1 << LAG_BITS) - 1)
            places.append(packed >> (CLASS_BITS + LAG_BITS))
            rows = pl.multiple_of(lag * panels, panels)
            windows.append(table[klass, pl.ds(rows, width * panels), :])
        product = jnp.dot(
            hist[source, :, pl.ds(pl.multiple_of(column, panels), width * panels)],
            jnp.concatenate(windows, axis=1),
            preferred_element_type=jnp.float32,
        )
        for n, place in enumerate(places):
            acc[place] += product[:, n * panels : (n + 1) * panels]


def window_kernel(config, *refs):
    served, local, begun, narrow, places, total, rows, height, owned = config
    refs = list(refs)
    where = refs.pop(0)
    served_refs = [refs.pop(0) for _ in range(3 if served else 0)]
    local_refs = [refs.pop(0) for _ in range(4 if local else 0)]
    hist_ref = refs.pop(0)
    pieces = [refs.pop(0) for _ in places]
    before = [refs.pop(0) for _ in range((bool(served) + bool(local)) if begun else 0)]
    outs = [refs.pop(0) for _ in range(bool(served) + bool(local))]
    table, hist, acc, tasks, counts, used, sems, hist_sems, ends, served_sems = refs
    base, group = where[0], where[1]
    classes, _, panels = table.shape
    steps = hist.shape[2] // panels
    margin = (steps // 2 - 1) * panels
    span = (table.shape[1] - 2 * margin) // panels
    sources = hist.shape[0]

    near = acc.at[pl.ds(served, owned)] if local else None
    if local and begun:
        pltpu.make_async_copy(before[-1], near, ends).start()
    for k in range(classes):
        for (slot, mask, first), piece in zip(places, pieces):
            start = pl.multiple_of(margin + slot * rows + (group ^ mask) * height + first, 16)
            pltpu.make_async_copy(
                piece.at[k], table.at[k, pl.ds(start, piece.shape[1]), :], sems.at[k]
            ).start()

    def history_copy(i):
        return pltpu.make_async_copy(hist_ref.at[i], hist.at[i], hist_sems.at[i])

    for i in range(sources):
        history_copy(i).start()
    if not begun:
        acc[...] = jnp.zeros_like(acc)
    ends_of_table = jnp.zeros((margin, panels), table.dtype)
    for n in range(3 * sources):
        counts[n] = 0
    for k in range(classes):
        table[k, pl.ds(0, margin), :] = ends_of_table
        table[k, pl.ds(margin + span * panels, margin), :] = ends_of_table

    def served_copy(i, back):
        ends_of = (acc.at[i], outs[0].at[i]) if back else (before[0].at[i], acc.at[i])
        return pltpu.make_async_copy(*ends_of, served_sems.at[i])

    if served:
        slots, peers = served_refs[0].shape

        @pl.loop(0, peers)
        def _(i):
            for c in range(slots):
                source, lag, klass = (ref[c, i] for ref in served_refs)
                place = i * slots + c
                pair = (source, klass, lag, place)
                touched = list_task(base, span, total, steps, pair, tasks, counts)
                needed = touched | narrow
                used[place] = jnp.where(touched, 1, 0)
                if begun:
                    @pl.when(needed)
                    def _():
                        served_copy(place, False).start()

    if local:
        @pl.loop(0, local_refs[0].shape[0])
        def _(i):
            source, lag, klass, target = (ref[i] for ref in local_refs)
            pair = (source, klass, lag, target + served)
            list_task(base, span, total, steps, pair, tasks, counts)

    if local and begun:
        pltpu.make_async_copy(before[-1], near, ends).wait()
    if served and begun:
        @pl.loop(0, served)
        def _(i):
            @pl.when((used[i] != 0) | narrow)
            def _():
                served_copy(i, False).wait()

    spare = acc.shape[0] - 1

    for k in range(classes):
        inner = table.at[k, pl.ds(margin, span * panels), :]
        pltpu.make_async_copy(inner, inner, sems.at[k]).wait()

    @pl.loop(0, sources)
    def _(i):
        history_copy(i).wait()
        half = steps // 2
        run_list(3 * i, i, 0, steps, spare, tasks, counts, hist, table, acc)

        @pl.loop(0, 2)
        def _(h):
            column = h * (half * panels)
            run_list(3 * i + 1 + h, i, column, half, spare, tasks, counts, hist, table, acc)

    if narrow:
        outs[0][...] = acc[pl.ds(0, served)].astype(outs[0].dtype)
        return
    if local:
        pltpu.make_async_copy(near, outs[-1], ends).start()
    if served:
        for wait in (False, True):
            @pl.loop(0, served)
            def _(i):
                @pl.when((used[i] != 0) | (not begun))
                def _():
                    copy = served_copy(i, True)
                    copy.wait() if wait else copy.start()
    if local:
        pltpu.make_async_copy(near, outs[-1], ends).wait()


def window_sums(shard, group, served, local, hist_t, shards, sums, lanes, rows, narrow=False):
    owned, excite, depth = hist_t.shape
    pieces = [(slot, *piece) for slot, found in enumerate(shards) for piece in found]
    classes, _, panels = pieces[0][3].shape
    places = served[0].size if served else 0
    targets = owned if local else 0
    pairs = places + (local[0].size if local else 0)
    steps = depth // panels
    config = (
        places,
        bool(local),
        sums is not None,
        narrow,
        tuple(piece[:3] for piece in pieces),
        lanes * rows // panels,
        rows,
        max(first + value.shape[1] for _, _, first, value in pieces),
        targets,
    )
    operands = [jnp.stack([shard * (rows // panels), group]).astype(jnp.int32), *served, *local]
    wide = [hist_t, *[piece[3] for piece in pieces]]
    before = list(sums) if sums is not None else []
    outs = [
        jax.ShapeDtypeStruct((n, excite, panels), jnp.bfloat16 if narrow else jnp.float32)
        for n in (places, targets)
        if n
    ]
    depth_of_table = len(shards) * rows + 2 * (steps // 2 - 1) * panels
    return pl.pallas_call(
        functools.partial(window_kernel, config),
        out_shape=outs,
        in_specs=[SMEM] * len(operands) + [HBM] * (len(wide) + len(before)),
        out_specs=[VMEM if narrow else HBM] * len(outs),
        scratch_shapes=[
            pltpu.VMEM((classes, depth_of_table, panels), jnp.bfloat16),
            pltpu.VMEM(hist_t.shape, hist_t.dtype),
            pltpu.VMEM((places + targets + 1, excite, panels), jnp.float32),
            pltpu.SMEM((3 * owned, pairs + BESIDE), jnp.int32),
            pltpu.SMEM((3 * owned,), jnp.int32),
            pltpu.SMEM((max(places, 1),), jnp.int32),
            pltpu.SemaphoreType.DMA((classes,)),
            pltpu.SemaphoreType.DMA((owned,)),
            pltpu.SemaphoreType.DMA,
            pltpu.SemaphoreType.DMA((max(places, 1),)),
        ],
        input_output_aliases={} if narrow else {
            len(operands) + len(wide) + n: n for n in range(len(before))
        },
        compiler_params=pltpu.CompilerParams(vmem_limit_bytes=58 * MIB),
        cost_estimate=pl.CostEstimate(
            flops=2 * pairs * panels * depth * excite,
            bytes_accessed=2 * classes * len(shards) * rows * panels + 2 * hist_t.size,
            transcendentals=0,
        ),
    )(*operands, *wide, *before)


def update_kernel(target_ref, near_ref, recv_ref, inverse_ref, incident_ref, out_ref, total):
    total[...] = near_ref[...]
    slots, peers = target_ref.shape

    @pl.loop(0, peers)
    def _(i):
        for c in range(slots):
            total[target_ref[c, i]] += recv_ref[i, c].astype(jnp.float32)

    for t in range(out_ref.shape[0]):
        residual = (incident_ref[t].astype(jnp.float32) - total[t].T).astype(jnp.bfloat16)
        out_ref[t] = jnp.dot(
            inverse_ref[t], residual, preferred_element_type=jnp.float32
        ).astype(out_ref.dtype)


def update(target, near, recv, inverse, incident):
    return pl.pallas_call(
        update_kernel,
        out_shape=jax.ShapeDtypeStruct(incident.shape, jnp.bfloat16),
        in_specs=[SMEM] + [VMEM] * 4,
        out_specs=VMEM,
        scratch_shapes=[pltpu.VMEM(near.shape, jnp.float32)],
        compiler_params=pltpu.CompilerParams(vmem_limit_bytes=32 * MIB),
    )(target, near, recv, inverse, incident)


def swap(value, bit, peers):
    return lax.ppermute(value, "grp", [(i, i ^ bit) for i in range(peers)])


def upper(value, peers):
    masks, held = [0], [value]
    bit = 8
    while bit < peers:
        masks += [mask ^ bit for mask in masks]
        held += [swap(value, bit, peers) for value in held]
        bit *= 2
    return masks, held


def with_other_core(found, peers):
    return found + [(mask ^ 1, first, swap(v, 1, peers)) for mask, first, v in found]


def per_device(
    weights,
    history,
    send_patch,
    send_lag,
    send_class,
    recv_target,
    local_src,
    local_lag,
    local_class,
    local_target,
    inverse_blocks,
    incident,
):
    classes, rows, panels = weights.shape
    peers, slots = send_patch.shape
    height = rows // peers
    group = lax.axis_index("grp")
    lane = lax.axis_index("lag")
    lanes = lax.axis_size("lag")
    ring = [(i, (i - 1) % lanes) for i in range(lanes)]
    served = (send_patch.T, send_lag.T, send_class.T)
    local = (local_src, local_lag, local_class, local_target)

    hist_t = jnp.swapaxes(history, 1, 2)
    half = height // 2

    def part(index):
        return lax.dynamic_slice(weights, (0, index * height, 0), (classes, height, panels))

    def add_shard(step, sums, served=served, local=local, **options):
        shard = lax.rem(lane + step, lanes)
        shards = rounds[step - 1 : step] if served else rounds[step - 1 :]
        return window_sums(
            shard, group, served, local, hist_t, shards, sums, lanes, rows, **options
        )

    sums = window_sums(
        lane, group * 0, served, local, hist_t, [[(0, 0, weights)]], None, lanes, rows
    )
    own = part(group)
    corner = part(group ^ 6)

    def neighbours(value):
        masks, held = upper(value, peers)
        return (
            [(m, 0, v) for m, v in zip(masks, held)],
            [(m ^ 2, 0, swap(v, 2, peers)) for m, v in zip(masks, held)],
            [(m ^ 4, 0, swap(v, 4, peers)) for m, v in zip(masks, held)],
        )

    def tie(*values):
        leaves, tree = jax.tree.flatten(values)
        arrays = lax.optimization_barrier([v for v in leaves if not isinstance(v, int)])
        return jax.tree.unflatten(
            tree, [v if isinstance(v, int) else arrays.pop(0) for v in leaves]
        )

    def corners(value):
        masks, held = upper(value, peers)
        return [(m ^ 6, 0, v) for m, v in zip(masks, held)]

    own = lax.ppermute(own, "lag", ring)
    own, sums = tie(own, sums)
    trio = neighbours(own)
    own = lax.ppermute(own, "lag", ring)
    trio, own, corner = tie(trio, own, corner)
    found = with_other_core(sum(trio, []), peers)
    held, across, along = neighbours(own)
    diagonal = lax.ppermute(corner, "lag", ring)
    held = with_other_core(held, peers)
    across, along, own, diagonal, found, held = tie(across, along, own, diagonal, found, held)
    diagonal = with_other_core(corners(diagonal), peers)
    rounds = [found + diagonal]
    for step in range(2, lanes - 1):
        own = lax.ppermute(own, "lag", ring)
        turned = [(m ^ 2, 0, swap(v[:, :half], 2, peers)) for m, _, v in along]
        turned += [(m ^ 4, half, swap(v[:, half:], 4, peers)) for m, _, v in across]
        if step == 2:
            rounds[0], across, along = tie(rounds[0], across, along)
        found = held + with_other_core(across + along, peers)
        sums = add_shard(step - 1, sums)
        own, turned, sums, corner, found = tie(own, turned, sums, corner, found)
        held, across, along = neighbours(own)
        found, held = tie(found + with_other_core(turned, peers), held)
        rounds.append(found)
        held = with_other_core(held, peers)
        if step < lanes - 2:
            across, along, own = tie(across, along, own)
    diagonal = lax.ppermute(corner, "lag", [(j, i) for i, j in ring])
    served_sums, near = sums
    served_sums = add_shard(lanes - 2, [served_sums], local=())[0]
    across, along, diagonal, served_sums = tie(across, along, diagonal, served_sums)
    rounds.append(held + with_other_core(across + along + corners(diagonal), peers))
    contribution = add_shard(lanes - 1, [served_sums], local=(), narrow=True)[0]
    recv = lax.all_to_all(
        contribution.reshape(peers, slots, *contribution.shape[1:]),
        "grp",
        split_axis=0,
        concat_axis=0,
        tiled=True,
    )
    near = add_shard(lanes - 2, [near], served=())[0]
    return update(recv_target.T, near, recv, inverse_blocks, incident)


def solution(mesh):
    both = ("grp", "lag")
    return jax.shard_map(
        per_device,
        mesh=mesh,
        in_specs=(
            P(None, "lag", None),
            P(both, None, None),
            P(both, None),
            P(both, None),
            P(both, None),
            P(both, None),
            P(both),
            P(both),
            P(both),
            P(both),
            P(both, None, None),
            P(both, None, None),
        ),
        out_specs=P(both, None, None),
        check_vma=False,
    )
```

```python
import functools

import jax
import jax.numpy as jnp
from jax import lax
from jax.experimental import pallas as pl
from jax.experimental.pallas import tpu as pltpu
from jax.sharding import PartitionSpec as P

SMEM = pl.BlockSpec(memory_space=pltpu.SMEM)
VMEM = pl.BlockSpec(memory_space=pltpu.VMEM)
HBM = pl.BlockSpec(memory_space=pltpu.HBM)
MIB = 1 << 20
HALF_BITS, SOURCE_BITS, CLASS_BITS, LAG_BITS = 1, 8, 4, 8
FIELDS = (HALF_BITS, SOURCE_BITS, CLASS_BITS, LAG_BITS)
UNROLL = 2


def pack(half, source, klass, lag, place):
    packed = place
    for value, bits in ((lag, LAG_BITS), (klass, CLASS_BITS), (source, SOURCE_BITS), (half, HALF_BITS)):
        packed = (packed << bits) | value
    return packed


def list_task(base, span, total, steps, phased, pair, tasks, counts):
    source, klass, lag, place = pair
    half = steps // 2
    start = lax.rem(lag - base + total, total)
    first = jnp.where(start < span, start, start - total)
    whole = (first > -half) & (first < span - half)
    lower = (first >= span - half) & (first < span)
    upper_half = (first > -steps) & (first <= -half)
    row = jnp.maximum(first + half - 1, 0)
    number = 2 * klass if phased else 0
    at = counts[number]
    tasks[number, at] = pack(0, source, klass, row, place)
    counts[number] = at + jnp.where(whole, 1, 0)
    at = counts[number + 1]
    second = jnp.where(upper_half, 1, 0)
    row = jnp.maximum(first + half - 1 + half * second, 0)
    tasks[number + 1, at] = pack(second, source, klass, row, place)
    counts[number + 1] = at + jnp.where(lower | upper_half, 1, 0)
    return whole | lower | upper_half


def run_list(number, width, spare, tasks, counts, hist, table, acc):
    panels = table.shape[2]
    count = counts[number]
    for n in range(UNROLL - 1):
        tasks[number, count + n] = pack(0, 0, 0, 0, spare)

    @pl.loop(0, (count + UNROLL - 1) // UNROLL)
    def _(j):
        for n in range(UNROLL):
            packed = tasks[number, j * UNROLL + n]
            fields = []
            for bits in FIELDS:
                fields.append(packed & ((1 << bits) - 1))
                packed = packed >> bits
            half, source, klass, lag = fields
            columns = pl.multiple_of(half * (width * panels), width * panels)
            rows = pl.multiple_of(lag * panels, panels)
            acc[packed] += jnp.dot(
                hist[source, :, pl.ds(columns, width * panels)],
                table[klass, pl.ds(rows, width * panels), :],
                preferred_element_type=jnp.float32,
            )


def window_kernel(config, *refs):
    served, local, begun, narrow, places, total, rows, height, owned = config
    refs = list(refs)
    where = refs.pop(0)
    served_refs = [refs.pop(0) for _ in range(3 if served else 0)]
    local_refs = [refs.pop(0) for _ in range(4 if local else 0)]
    hist_ref = refs.pop(0)
    pieces = [refs.pop(0) for _ in places]
    before = [refs.pop(0) for _ in range((bool(served) + bool(local)) if begun else 0)]
    outs = [refs.pop(0) for _ in range(bool(served) + bool(local))]
    table, hist, acc, tasks, counts, used, sems, ends, served_sems = refs
    base, group = where[0], where[1]
    classes, _, panels = table.shape
    steps = hist.shape[2] // panels
    margin = (steps // 2 - 1) * panels
    span = (table.shape[1] - 2 * margin) // panels
    phased = bool(local) or span * panels > rows

    pltpu.make_async_copy(hist_ref, hist, ends.at[0]).start()
    near = acc.at[pl.ds(served, owned)] if local else None
    if local and begun:
        pltpu.make_async_copy(before[-1], near, ends.at[1]).start()
    for k in range(classes):
        for (slot, mask, first), piece in zip(places, pieces):
            start = pl.multiple_of(margin + slot * rows + (group ^ mask) * height + first, 16)
            pltpu.make_async_copy(
                piece.at[k], table.at[k, pl.ds(start, piece.shape[1]), :], sems.at[k]
            ).start()
    if not begun:
        acc[...] = jnp.zeros_like(acc)
    ends_of_table = jnp.zeros((margin, panels), table.dtype)
    for k in range(classes):
        counts[2 * k] = 0
        counts[2 * k + 1] = 0
        table[k, pl.ds(0, margin), :] = ends_of_table
        table[k, pl.ds(margin + span * panels, margin), :] = ends_of_table

    def served_copy(i, back):
        ends_of = (acc.at[i], outs[0].at[i]) if back else (before[0].at[i], acc.at[i])
        return pltpu.make_async_copy(*ends_of, served_sems.at[i])

    if served:
        slots, peers = served_refs[0].shape

        @pl.loop(0, peers)
        def _(i):
            for c in range(slots):
                source, lag, klass = (ref[c, i] for ref in served_refs)
                place = i * slots + c
                pair = (source, klass, lag, place)
                touched = list_task(base, span, total, steps, phased, pair, tasks, counts)
                needed = touched | narrow
                used[place] = jnp.where(touched, 1, 0)
                if begun:
                    @pl.when(needed)
                    def _():
                        served_copy(place, False).start()

    if local:
        @pl.loop(0, local_refs[0].shape[0])
        def _(i):
            source, lag, klass, target = (ref[i] for ref in local_refs)
            pair = (source, klass, lag, target + served)
            list_task(base, span, total, steps, phased, pair, tasks, counts)

    pltpu.make_async_copy(hist_ref, hist, ends.at[0]).wait()
    if local and begun:
        pltpu.make_async_copy(before[-1], near, ends.at[1]).wait()
    if served and begun:
        @pl.loop(0, served)
        def _(i):
            @pl.when((used[i] != 0) | narrow)
            def _():
                served_copy(i, False).wait()

    spare = acc.shape[0] - 1

    def wait_class(k):
        inner = table.at[k, pl.ds(margin, span * panels), :]
        pltpu.make_async_copy(inner, inner, sems.at[k]).wait()

    def run_lists(number):
        run_list(number, steps, spare, tasks, counts, hist, table, acc)
        run_list(number + 1, steps // 2, spare, tasks, counts, hist, table, acc)

    if phased:
        @pl.loop(0, classes)
        def _(k):
            wait_class(k)
            run_lists(2 * k)
    else:
        for k in range(classes):
            wait_class(k)
        run_lists(0)

    if narrow:
        outs[0][...] = acc[pl.ds(0, served)].astype(outs[0].dtype)
        return
    if local:
        pltpu.make_async_copy(near, outs[-1], ends.at[1]).start()
    if served:
        for wait in (False, True):
            @pl.loop(0, served)
            def _(i):
                @pl.when((used[i] != 0) | (not begun))
                def _():
                    copy = served_copy(i, True)
                    copy.wait() if wait else copy.start()
    if local:
        pltpu.make_async_copy(near, outs[-1], ends.at[1]).wait()


def window_sums(shard, group, served, local, hist_t, shards, sums, lanes, rows, narrow=False):
    owned, excite, depth = hist_t.shape
    pieces = [(slot, *piece) for slot, found in enumerate(shards) for piece in found]
    classes, _, panels = pieces[0][3].shape
    places = served[0].size if served else 0
    targets = owned if local else 0
    pairs = places + (local[0].size if local else 0)
    steps = depth // panels
    config = (
        places,
        bool(local),
        sums is not None,
        narrow,
        tuple(piece[:3] for piece in pieces),
        lanes * rows // panels,
        rows,
        max(first + value.shape[1] for _, _, first, value in pieces),
        targets,
    )
    operands = [jnp.stack([shard * (rows // panels), group]).astype(jnp.int32), *served, *local]
    wide = [hist_t, *[piece[3] for piece in pieces]]
    before = list(sums) if sums is not None else []
    outs = [
        jax.ShapeDtypeStruct((n, excite, panels), jnp.bfloat16 if narrow else jnp.float32)
        for n in (places, targets)
        if n
    ]
    depth_of_table = len(shards) * rows + 2 * (steps // 2 - 1) * panels
    return pl.pallas_call(
        functools.partial(window_kernel, config),
        out_shape=outs,
        in_specs=[SMEM] * len(operands) + [HBM] * (len(wide) + len(before)),
        out_specs=[VMEM if narrow else HBM] * len(outs),
        scratch_shapes=[
            pltpu.VMEM((classes, depth_of_table, panels), jnp.bfloat16),
            pltpu.VMEM(hist_t.shape, hist_t.dtype),
            pltpu.VMEM((places + targets + 1, excite, panels), jnp.float32),
            pltpu.SMEM((2 * classes, pairs + UNROLL), jnp.int32),
            pltpu.SMEM((2 * classes,), jnp.int32),
            pltpu.SMEM((max(places, 1),), jnp.int32),
            pltpu.SemaphoreType.DMA((classes,)),
            pltpu.SemaphoreType.DMA((2,)),
            pltpu.SemaphoreType.DMA((max(places, 1),)),
        ],
        input_output_aliases={} if narrow else {
            len(operands) + len(wide) + n: n for n in range(len(before))
        },
        compiler_params=pltpu.CompilerParams(vmem_limit_bytes=58 * MIB),
        cost_estimate=pl.CostEstimate(
            flops=2 * pairs * panels * depth * excite,
            bytes_accessed=2 * classes * len(shards) * rows * panels + 2 * hist_t.size,
            transcendentals=0,
        ),
    )(*operands, *wide, *before)


def update_kernel(target_ref, near_ref, recv_ref, inverse_ref, incident_ref, out_ref, total, sem):
    copy = pltpu.make_async_copy(near_ref, total, sem)
    copy.start()
    copy.wait()
    slots, peers = target_ref.shape

    @pl.loop(0, peers)
    def _(i):
        for c in range(slots):
            total[target_ref[c, i]] += recv_ref[i, c].astype(jnp.float32)

    for t in range(out_ref.shape[0]):
        residual = (incident_ref[t].astype(jnp.float32) - total[t].T).astype(jnp.bfloat16)
        out_ref[t] = jnp.dot(
            inverse_ref[t], residual, preferred_element_type=jnp.float32
        ).astype(out_ref.dtype)


def update(target, near, recv, inverse, incident):
    return pl.pallas_call(
        update_kernel,
        out_shape=jax.ShapeDtypeStruct(incident.shape, jnp.bfloat16),
        in_specs=[SMEM, HBM] + [VMEM] * 3,
        out_specs=VMEM,
        scratch_shapes=[pltpu.VMEM(near.shape, jnp.float32), pltpu.SemaphoreType.DMA],
        compiler_params=pltpu.CompilerParams(vmem_limit_bytes=32 * MIB),
    )(target, near, recv, inverse, incident)


def swap(value, bit, peers):
    return lax.ppermute(value, "grp", [(i, i ^ bit) for i in range(peers)])


def upper(value, peers):
    masks, held = [0], [value]
    bit = 8
    while bit < peers:
        masks += [mask ^ bit for mask in masks]
        held += [swap(value, bit, peers) for value in held]
        bit *= 2
    return masks, held


def with_other_core(found, peers):
    return found + [(mask ^ 1, first, swap(v, 1, peers)) for mask, first, v in found]


def per_device(
    weights,
    history,
    send_patch,
    send_lag,
    send_class,
    recv_target,
    local_src,
    local_lag,
    local_class,
    local_target,
    inverse_blocks,
    incident,
):
    classes, rows, panels = weights.shape
    peers, slots = send_patch.shape
    height = rows // peers
    group = lax.axis_index("grp")
    lane = lax.axis_index("lag")
    lanes = lax.axis_size("lag")
    ring = [(i, (i - 1) % lanes) for i in range(lanes)]
    served = (send_patch.T, send_lag.T, send_class.T)
    local = (local_src, local_lag, local_class, local_target)

    hist_t = jnp.swapaxes(history, 1, 2)
    half = height // 2

    def part(index):
        return lax.dynamic_slice(weights, (0, index * height, 0), (classes, height, panels))

    def add_shards(first, end, served, local, sums, **options):
        shard = lax.rem(lane + first, lanes)
        shards = rounds[first - 1 : end - 1]
        return window_sums(
            shard, group, served, local, hist_t, shards, [sums], lanes, rows, **options
        )[0]

    own = part(group)
    corner = part(group ^ 6)

    def neighbours(value):
        masks, held = upper(value, peers)
        return (
            [(m, 0, v) for m, v in zip(masks, held)],
            [(m ^ 2, 0, swap(v, 2, peers)) for m, v in zip(masks, held)],
            [(m ^ 4, 0, swap(v, 4, peers)) for m, v in zip(masks, held)],
        )

    def tie(*values):
        leaves, tree = jax.tree.flatten(values)
        arrays = lax.optimization_barrier([v for v in leaves if not isinstance(v, int)])
        return jax.tree.unflatten(
            tree, [v if isinstance(v, int) else arrays.pop(0) for v in leaves]
        )

    def corners(value):
        masks, held = upper(value, peers)
        return [(m ^ 6, 0, v) for m, v in zip(masks, held)]

    own = lax.ppermute(own, "lag", ring)
    own, hist_t = tie(own, hist_t)
    trio = neighbours(own)
    own = lax.ppermute(own, "lag", ring)
    served_sums, near = window_sums(
        lane, group * 0, served, local, hist_t, [[(0, 0, weights)]], None, lanes, rows
    )
    trio, own, corner, served_sums, near = tie(trio, own, corner, served_sums, near)
    held, across, along = trio
    found, across = tie(with_other_core(held, peers), across)
    found += with_other_core(across, peers)
    more = with_other_core(along, peers)
    held, across, along = neighbours(own)
    more, held = tie(more, held)
    found += more
    diagonal = lax.ppermute(corner, "lag", ring)
    held = with_other_core(held, peers)
    across, along, own, diagonal, found, held = tie(across, along, own, diagonal, found, held)
    diagonal = with_other_core(corners(diagonal), peers)
    rounds = [found + diagonal]
    for step in range(2, lanes - 1):
        own = lax.ppermute(own, "lag", ring)
        turned = [(m ^ 2, 0, swap(v[:, :half], 2, peers)) for m, _, v in along]
        turned += [(m ^ 4, half, swap(v[:, half:], 4, peers)) for m, _, v in across]
        if step == 2:
            rounds[0], across, along = tie(rounds[0], across, along)
        found = held + with_other_core(across + along, peers)
        near = add_shards(step - 1, step, (), local, near)
        own, turned, near, corner, found = tie(own, turned, near, corner, found)
        held, across, along = neighbours(own)
        found, held = tie(found + with_other_core(turned, peers), held)
        rounds.append(found)
        held = with_other_core(held, peers)
        if step < lanes - 2:
            across, along, own = tie(across, along, own)
    diagonal = lax.ppermute(corner, "lag", [(j, i) for i, j in ring])
    served_sums = add_shards(1, lanes - 1, served, (), served_sums)
    across, along, diagonal, served_sums = tie(across, along, diagonal, served_sums)
    rounds.append(held + with_other_core(across + along + corners(diagonal), peers))
    contribution = add_shards(lanes - 1, lanes, served, (), served_sums, narrow=True)
    recv = lax.all_to_all(
        contribution.reshape(peers, slots, *contribution.shape[1:]),
        "grp",
        split_axis=0,
        concat_axis=0,
        tiled=True,
    )
    near = add_shards(lanes - 2, lanes, (), local, near)
    return update(recv_target.T, near, recv, inverse_blocks, incident)


def solution(mesh):
    both = ("grp", "lag")
    return jax.shard_map(
        per_device,
        mesh=mesh,
        in_specs=(
            P(None, "lag", None),
            P(both, None, None),
            P(both, None),
            P(both, None),
            P(both, None),
            P(both, None),
            P(both),
            P(both),
            P(both),
            P(both),
            P(both, None, None),
            P(both, None, None),
        ),
        out_specs=P(both, None, None),
        check_vma=False,
    )
```

```python
import functools

import jax
import jax.numpy as jnp
from jax import lax
from jax.experimental import pallas as pl
from jax.experimental.pallas import tpu as pltpu
from jax.sharding import PartitionSpec as P

SMEM = pl.BlockSpec(memory_space=pltpu.SMEM)
VMEM = pl.BlockSpec(memory_space=pltpu.VMEM)
HBM = pl.BlockSpec(memory_space=pltpu.HBM)
MIB = 1 << 20
HALF_BITS, SOURCE_BITS, CLASS_BITS, LAG_BITS = 1, 8, 4, 8
FIELDS = (HALF_BITS, SOURCE_BITS, CLASS_BITS, LAG_BITS)
UNROLL = 2


def pack(half, source, klass, lag, place):
    packed = place
    for value, bits in ((lag, LAG_BITS), (klass, CLASS_BITS), (source, SOURCE_BITS), (half, HALF_BITS)):
        packed = (packed << bits) | value
    return packed


def list_task(base, span, total, steps, phased, pair, tasks, counts):
    source, klass, lag, place = pair
    half = steps // 2
    start = lax.rem(lag - base + total, total)
    first = jnp.where(start < span, start, start - total)
    whole = (first > -half) & (first < span - half)
    lower = (first >= span - half) & (first < span)
    upper_half = (first > -steps) & (first <= -half)
    row = jnp.maximum(first + half - 1, 0)
    number = 2 * klass if phased else 0
    at = counts[number]
    tasks[number, at] = pack(0, source, klass, row, place)
    counts[number] = at + jnp.where(whole, 1, 0)
    at = counts[number + 1]
    second = jnp.where(upper_half, 1, 0)
    row = jnp.maximum(first + half - 1 + half * second, 0)
    tasks[number + 1, at] = pack(second, source, klass, row, place)
    counts[number + 1] = at + jnp.where(lower | upper_half, 1, 0)
    return whole | lower | upper_half


def run_list(number, width, spare, tasks, counts, hist, table, acc):
    panels = table.shape[2]
    count = counts[number]
    for n in range(UNROLL - 1):
        tasks[number, count + n] = pack(0, 0, 0, 0, spare)

    @pl.loop(0, (count + UNROLL - 1) // UNROLL)
    def _(j):
        for n in range(UNROLL):
            packed = tasks[number, j * UNROLL + n]
            fields = []
            for bits in FIELDS:
                fields.append(packed & ((1 << bits) - 1))
                packed = packed >> bits
            half, source, klass, lag = fields
            columns = pl.multiple_of(half * (width * panels), width * panels)
            rows = pl.multiple_of(lag * panels, panels)
            acc[packed] += jnp.dot(
                hist[source, :, pl.ds(columns, width * panels)],
                table[klass, pl.ds(rows, width * panels), :],
                preferred_element_type=jnp.float32,
            )


def window_kernel(config, *refs):
    served, local, begun, narrow, places, total, rows, height, owned = config
    refs = list(refs)
    where = refs.pop(0)
    served_refs = [refs.pop(0) for _ in range(3 if served else 0)]
    local_refs = [refs.pop(0) for _ in range(4 if local else 0)]
    hist_ref = refs.pop(0)
    pieces = [refs.pop(0) for _ in places]
    before = [refs.pop(0) for _ in range((bool(served) + bool(local)) if begun else 0)]
    outs = [refs.pop(0) for _ in range(bool(served) + bool(local))]
    table, hist, acc, prior, tasks, counts, used, sems, ends, served_sems = refs
    base, group = where[0], where[1]
    classes, _, panels = table.shape
    steps = hist.shape[2] // panels
    margin = (steps // 2 - 1) * panels
    span = (table.shape[1] - 2 * margin) // panels
    phased = bool(local) or span * panels > rows

    pltpu.make_async_copy(hist_ref, hist, ends.at[0]).start()
    near = acc.at[pl.ds(served, owned)] if local else None
    if local and begun:
        pltpu.make_async_copy(before[-1], near, ends.at[1]).start()
    for k in range(classes):
        for (slot, mask, first), piece in zip(places, pieces):
            start = pl.multiple_of(margin + slot * rows + (group ^ mask) * height + first, 16)
            pltpu.make_async_copy(
                piece.at[k], table.at[k, pl.ds(start, piece.shape[1]), :], sems.at[k]
            ).start()
    if not begun or narrow:
        acc[...] = jnp.zeros_like(acc)
    ends_of_table = jnp.zeros((margin, panels), table.dtype)
    for k in range(classes):
        counts[2 * k] = 0
        counts[2 * k + 1] = 0
        table[k, pl.ds(0, margin), :] = ends_of_table
        table[k, pl.ds(margin + span * panels, margin), :] = ends_of_table

    def served_copy(i, back):
        ends_of = (acc.at[i], outs[0].at[i]) if back else (before[0].at[i], acc.at[i])
        return pltpu.make_async_copy(*ends_of, served_sems.at[i])

    prior_copy = pltpu.make_async_copy(before[0], prior, ends.at[1]) if narrow else None
    if narrow:
        prior_copy.start()

    if served:
        slots, peers = served_refs[0].shape

        @pl.loop(0, peers)
        def _(i):
            for c in range(slots):
                source, lag, klass = (ref[c, i] for ref in served_refs)
                place = i * slots + c
                pair = (source, klass, lag, place)
                touched = list_task(base, span, total, steps, phased, pair, tasks, counts)
                used[place] = jnp.where(touched, 1, 0)
                if begun and not narrow:
                    @pl.when(touched)
                    def _():
                        served_copy(place, False).start()

    if local:
        @pl.loop(0, local_refs[0].shape[0])
        def _(i):
            source, lag, klass, target = (ref[i] for ref in local_refs)
            pair = (source, klass, lag, target + served)
            list_task(base, span, total, steps, phased, pair, tasks, counts)

    pltpu.make_async_copy(hist_ref, hist, ends.at[0]).wait()
    if local and begun:
        pltpu.make_async_copy(before[-1], near, ends.at[1]).wait()
    if served and begun and not narrow:
        @pl.loop(0, served)
        def _(i):
            @pl.when(used[i] != 0)
            def _():
                served_copy(i, False).wait()

    spare = acc.shape[0] - 1

    def wait_class(k):
        inner = table.at[k, pl.ds(margin, span * panels), :]
        pltpu.make_async_copy(inner, inner, sems.at[k]).wait()

    def run_lists(number):
        run_list(number, steps, spare, tasks, counts, hist, table, acc)
        run_list(number + 1, steps // 2, spare, tasks, counts, hist, table, acc)

    if phased:
        @pl.loop(0, classes)
        def _(k):
            wait_class(k)
            run_lists(2 * k)
    else:
        for k in range(classes):
            wait_class(k)
        run_lists(0)

    if narrow:
        prior_copy.wait()
        outs[0][...] = (prior[...] + acc[pl.ds(0, served)]).astype(outs[0].dtype)
        return
    if local:
        pltpu.make_async_copy(near, outs[-1], ends.at[1]).start()
    if served:
        for wait in (False, True):
            @pl.loop(0, served)
            def _(i):
                @pl.when((used[i] != 0) | (not begun))
                def _():
                    copy = served_copy(i, True)
                    copy.wait() if wait else copy.start()
    if local:
        pltpu.make_async_copy(near, outs[-1], ends.at[1]).wait()


def window_sums(shard, group, served, local, hist_t, shards, sums, lanes, rows, narrow=False):
    owned, excite, depth = hist_t.shape
    pieces = [(slot, *piece) for slot, found in enumerate(shards) for piece in found]
    classes, _, panels = pieces[0][3].shape
    places = served[0].size if served else 0
    targets = owned if local else 0
    pairs = places + (local[0].size if local else 0)
    steps = depth // panels
    config = (
        places,
        bool(local),
        sums is not None,
        narrow,
        tuple(piece[:3] for piece in pieces),
        lanes * rows // panels,
        rows,
        max(first + value.shape[1] for _, _, first, value in pieces),
        targets,
    )
    operands = [jnp.stack([shard * (rows // panels), group]).astype(jnp.int32), *served, *local]
    wide = [hist_t, *[piece[3] for piece in pieces]]
    before = list(sums) if sums is not None else []
    outs = [
        jax.ShapeDtypeStruct((n, excite, panels), jnp.bfloat16 if narrow else jnp.float32)
        for n in (places, targets)
        if n
    ]
    depth_of_table = len(shards) * rows + 2 * (steps // 2 - 1) * panels
    return pl.pallas_call(
        functools.partial(window_kernel, config),
        out_shape=outs,
        in_specs=[SMEM] * len(operands) + [HBM] * (len(wide) + len(before)),
        out_specs=[VMEM if narrow else HBM] * len(outs),
        scratch_shapes=[
            pltpu.VMEM((classes, depth_of_table, panels), jnp.bfloat16),
            pltpu.VMEM(hist_t.shape, hist_t.dtype),
            pltpu.VMEM((places + targets + 1, excite, panels), jnp.float32),
            pltpu.VMEM((places if narrow else 1, excite, panels), jnp.float32),
            pltpu.SMEM((2 * classes, pairs + UNROLL), jnp.int32),
            pltpu.SMEM((2 * classes,), jnp.int32),
            pltpu.SMEM((max(places, 1),), jnp.int32),
            pltpu.SemaphoreType.DMA((classes,)),
            pltpu.SemaphoreType.DMA((2,)),
            pltpu.SemaphoreType.DMA((max(places, 1),)),
        ],
        input_output_aliases={} if narrow else {
            len(operands) + len(wide) + n: n for n in range(len(before))
        },
        compiler_params=pltpu.CompilerParams(vmem_limit_bytes=58 * MIB),
        cost_estimate=pl.CostEstimate(
            flops=2 * pairs * panels * depth * excite,
            bytes_accessed=2 * classes * len(shards) * rows * panels + 2 * hist_t.size,
            transcendentals=0,
        ),
    )(*operands, *wide, *before)


def update_kernel(target_ref, near_ref, recv_ref, inverse_ref, incident_ref, out_ref, total):
    total[...] = near_ref[...]
    slots, peers = target_ref.shape

    @pl.loop(0, peers)
    def _(i):
        for c in range(slots):
            total[target_ref[c, i]] += recv_ref[i, c].astype(jnp.float32)

    for t in range(out_ref.shape[0]):
        residual = (incident_ref[t].astype(jnp.float32) - total[t].T).astype(jnp.bfloat16)
        out_ref[t] = jnp.dot(
            inverse_ref[t], residual, preferred_element_type=jnp.float32
        ).astype(out_ref.dtype)


def update(target, near, recv, inverse, incident):
    return pl.pallas_call(
        update_kernel,
        out_shape=jax.ShapeDtypeStruct(incident.shape, jnp.bfloat16),
        in_specs=[SMEM] + [VMEM] * 4,
        out_specs=VMEM,
        scratch_shapes=[pltpu.VMEM(near.shape, jnp.float32)],
        compiler_params=pltpu.CompilerParams(vmem_limit_bytes=58 * MIB),
    )(target, near, recv, inverse, incident)


def swap(value, bit, peers):
    return lax.ppermute(value, "grp", [(i, i ^ bit) for i in range(peers)])


def upper(value, peers):
    masks, held = [0], [value]
    bit = 8
    while bit < peers:
        masks += [mask ^ bit for mask in masks]
        held += [swap(value, bit, peers) for value in held]
        bit *= 2
    return masks, held


def with_other_core(found, peers):
    return found + [(mask ^ 1, first, swap(v, 1, peers)) for mask, first, v in found]


def per_device(
    weights,
    history,
    send_patch,
    send_lag,
    send_class,
    recv_target,
    local_src,
    local_lag,
    local_class,
    local_target,
    inverse_blocks,
    incident,
):
    classes, rows, panels = weights.shape
    peers, slots = send_patch.shape
    height = rows // peers
    group = lax.axis_index("grp")
    lane = lax.axis_index("lag")
    lanes = lax.axis_size("lag")
    ring = [(i, (i - 1) % lanes) for i in range(lanes)]
    served = (send_patch.T, send_lag.T, send_class.T)
    local = (local_src, local_lag, local_class, local_target)

    hist_t = jnp.swapaxes(history, 1, 2)
    half = height // 2

    def part(index):
        return lax.dynamic_slice(weights, (0, index * height, 0), (classes, height, panels))

    def add_shards(first, end, served, local, sums, **options):
        shard = lax.rem(lane + first, lanes)
        shards = rounds[first - 1 : end - 1]
        return window_sums(
            shard, group, served, local, hist_t, shards, [sums], lanes, rows, **options
        )[0]

    own = part(group)

    def neighbours(value):
        masks, held = upper(value, peers)
        return (
            [(m, 0, v) for m, v in zip(masks, held)],
            [(m ^ 2, 0, swap(v, 2, peers)) for m, v in zip(masks, held)],
            [(m ^ 4, 0, swap(v, 4, peers)) for m, v in zip(masks, held)],
        )

    def tie(*values):
        leaves, tree = jax.tree.flatten(values)
        arrays = lax.optimization_barrier([v for v in leaves if not isinstance(v, int)])
        return jax.tree.unflatten(
            tree, [v if isinstance(v, int) else arrays.pop(0) for v in leaves]
        )

    def corners(value):
        masks, held = upper(value, peers)
        return [(m ^ 6, 0, v) for m, v in zip(masks, held)]

    own = lax.ppermute(own, "lag", ring)
    own, hist_t, opposite = tie(own, hist_t, group ^ 6)
    corner = part(opposite)
    trio = neighbours(own)
    own = lax.ppermute(own, "lag", ring)
    served_sums, near = window_sums(
        lane, group * 0, served, local, hist_t, [[(0, 0, weights)]], None, lanes, rows
    )
    trio, own, corner, served_sums, near = tie(trio, own, corner, served_sums, near)
    held, across, along = trio
    found, across = tie(with_other_core(held, peers), across)
    found += with_other_core(across, peers)
    more = with_other_core(along, peers)
    held, across, along = neighbours(own)
    more, held = tie(more, held)
    found += more
    diagonal = lax.ppermute(corner, "lag", ring)
    held = with_other_core(held, peers)
    across, along, own, diagonal, found, held = tie(across, along, own, diagonal, found, held)
    diagonal = with_other_core(corners(diagonal), peers)
    rounds = [found + diagonal]
    for step in range(2, lanes - 1):
        own = lax.ppermute(own, "lag", ring)
        if step == 2:
            rounds[0], across, along = tie(rounds[0], across, along)
        turned = [(m ^ 2, 0, swap(v[:, :half], 2, peers)) for m, _, v in along]
        turned += [(m ^ 4, half, swap(v[:, half:], 4, peers)) for m, _, v in across]
        found = held + with_other_core(across + along, peers)
        near = add_shards(step - 1, step, (), local, near)
        own, turned, near, corner, found = tie(own, turned, near, corner, found)
        held, across, along = neighbours(own)
        found, held = tie(found + with_other_core(turned, peers), held)
        rounds.append(found)
        held = with_other_core(held, peers)
        if step < lanes - 2:
            across, along, own = tie(across, along, own)
    diagonal = lax.ppermute(corner, "lag", [(j, i) for i, j in ring])
    served_sums = add_shards(1, lanes - 1, served, (), served_sums)
    across, along, diagonal, served_sums = tie(across, along, diagonal, served_sums)
    rounds.append(held + with_other_core(across + along + corners(diagonal), peers))
    contribution = add_shards(lanes - 1, lanes, served, (), served_sums, narrow=True)
    recv = lax.all_to_all(
        contribution.reshape(peers, slots, *contribution.shape[1:]),
        "grp",
        split_axis=0,
        concat_axis=0,
        tiled=True,
    )
    near = add_shards(lanes - 2, lanes, (), local, near)
    return update(recv_target.T, near, recv, inverse_blocks, incident)


def solution(mesh):
    both = ("grp", "lag")
    return jax.shard_map(
        per_device,
        mesh=mesh,
        in_specs=(
            P(None, "lag", None),
            P(both, None, None),
            P(both, None),
            P(both, None),
            P(both, None),
            P(both, None),
            P(both),
            P(both),
            P(both),
            P(both),
            P(both, None, None),
            P(both, None, None),
        ),
        out_specs=P(both, None, None),
        check_vma=False,
    )
```

```python
import functools

import jax
import jax.numpy as jnp
from jax import lax
from jax.experimental import pallas as pl
from jax.experimental.pallas import tpu as pltpu
from jax.sharding import PartitionSpec as P

SMEM = pl.BlockSpec(memory_space=pltpu.SMEM)
VMEM = pl.BlockSpec(memory_space=pltpu.VMEM)
HBM = pl.BlockSpec(memory_space=pltpu.HBM)
MIB = 1 << 20
HALF_BITS, SOURCE_BITS, CLASS_BITS, LAG_BITS = 1, 8, 4, 8
FIELDS = (HALF_BITS, SOURCE_BITS, CLASS_BITS, LAG_BITS)
UNROLL = 2


def pack(half, source, klass, lag, place):
    packed = place
    for value, bits in ((lag, LAG_BITS), (klass, CLASS_BITS), (source, SOURCE_BITS), (half, HALF_BITS)):
        packed = (packed << bits) | value
    return packed


def list_task(base, span, total, steps, phased, pair, tasks, counts):
    source, klass, lag, place = pair
    half = steps // 2
    start = lax.rem(lag - base + total, total)
    first = jnp.where(start < span, start, start - total)
    whole = (first > -half) & (first < span - half)
    lower = (first >= span - half) & (first < span)
    upper_half = (first > -steps) & (first <= -half)
    row = jnp.maximum(first + half - 1, 0)
    number = 2 * klass if phased else 0
    at = counts[number]
    tasks[number, at] = pack(0, source, klass, row, place)
    counts[number] = at + jnp.where(whole, 1, 0)
    at = counts[number + 1]
    second = jnp.where(upper_half, 1, 0)
    row = jnp.maximum(first + half - 1 + half * second, 0)
    tasks[number + 1, at] = pack(second, source, klass, row, place)
    counts[number + 1] = at + jnp.where(lower | upper_half, 1, 0)
    return whole | lower | upper_half


def run_list(number, width, tasks, counts, hist, table, acc):
    panels = table.shape[2]

    def run(n):
        packed = tasks[number, n]
        fields = []
        for bits in FIELDS:
            fields.append(packed & ((1 << bits) - 1))
            packed = packed >> bits
        half, source, klass, lag = fields
        columns = pl.multiple_of(half * (width * panels), width * panels)
        rows = pl.multiple_of(lag * panels, panels)
        acc[packed] += jnp.dot(
            hist[source, :, pl.ds(columns, width * panels)],
            table[klass, pl.ds(rows, width * panels), :],
            preferred_element_type=jnp.float32,
        )

    count = counts[number]

    @pl.loop(0, count // UNROLL)
    def _(j):
        for n in range(UNROLL):
            run(j * UNROLL + n)

    @pl.loop(count // UNROLL * UNROLL, count)
    def _(j):
        run(j)


def window_kernel(config, *refs):
    served, local, begun, narrow, places, total, rows, height, owned = config
    refs = list(refs)
    where = refs.pop(0)
    served_refs = [refs.pop(0) for _ in range(3 if served else 0)]
    local_refs = [refs.pop(0) for _ in range(4 if local else 0)]
    hist_ref = refs.pop(0)
    pieces = [refs.pop(0) for _ in places]
    before = [refs.pop(0) for _ in range((bool(served) + bool(local)) if begun else 0)]
    outs = [refs.pop(0) for _ in range(bool(served) + bool(local))]
    table, hist, acc, prior, tasks, counts, used, sems, ends, served_sems = refs
    base, group = where[0], where[1]
    classes, _, panels = table.shape
    steps = hist.shape[2] // panels
    margin = (steps // 2 - 1) * panels
    span = (table.shape[1] - 2 * margin) // panels
    phased = bool(local) or span * panels > rows

    pltpu.make_async_copy(hist_ref, hist, ends.at[0]).start()
    near = acc.at[pl.ds(served, owned)] if local else None
    if local and begun:
        pltpu.make_async_copy(before[-1], near, ends.at[1]).start()
    for k in range(classes):
        for (slot, mask, first), piece in zip(places, pieces):
            start = pl.multiple_of(margin + slot * rows + (group ^ mask) * height + first, 16)
            pltpu.make_async_copy(
                piece.at[k], table.at[k, pl.ds(start, piece.shape[1]), :], sems.at[k]
            ).start()
    if not begun or narrow:
        acc[...] = jnp.zeros_like(acc)
    ends_of_table = jnp.zeros((margin, panels), table.dtype)
    for k in range(classes):
        counts[2 * k] = 0
        counts[2 * k + 1] = 0
        table[k, pl.ds(0, margin), :] = ends_of_table
        table[k, pl.ds(margin + span * panels, margin), :] = ends_of_table

    def served_copy(i, back):
        ends_of = (acc.at[i], outs[0].at[i]) if back else (before[0].at[i], acc.at[i])
        return pltpu.make_async_copy(*ends_of, served_sems.at[i])

    prior_copy = pltpu.make_async_copy(before[0], prior, ends.at[1]) if narrow else None
    if narrow:
        prior_copy.start()

    if served:
        slots, peers = served_refs[0].shape

        @pl.loop(0, peers)
        def _(i):
            for c in range(slots):
                source, lag, klass = (ref[c, i] for ref in served_refs)
                place = i * slots + c
                pair = (source, klass, lag, place)
                touched = list_task(base, span, total, steps, phased, pair, tasks, counts)
                used[place] = jnp.where(touched, 1, 0)
                if begun and not narrow:
                    @pl.when(touched)
                    def _():
                        served_copy(place, False).start()

    if local:
        @pl.loop(0, local_refs[0].shape[0])
        def _(i):
            source, lag, klass, target = (ref[i] for ref in local_refs)
            pair = (source, klass, lag, target + served)
            list_task(base, span, total, steps, phased, pair, tasks, counts)

    pltpu.make_async_copy(hist_ref, hist, ends.at[0]).wait()
    if local and begun:
        pltpu.make_async_copy(before[-1], near, ends.at[1]).wait()
    if served and begun and not narrow:
        @pl.loop(0, served)
        def _(i):
            @pl.when(used[i] != 0)
            def _():
                served_copy(i, False).wait()

    def wait_class(k):
        inner = table.at[k, pl.ds(margin, span * panels), :]
        pltpu.make_async_copy(inner, inner, sems.at[k]).wait()

    def run_lists(number):
        run_list(number, steps, tasks, counts, hist, table, acc)
        run_list(number + 1, steps // 2, tasks, counts, hist, table, acc)

    if phased:
        @pl.loop(0, classes)
        def _(k):
            wait_class(k)
            run_lists(2 * k)
    else:
        for k in range(classes):
            wait_class(k)
        run_lists(0)

    if narrow:
        prior_copy.wait()
        outs[0][...] = (prior[...] + acc[pl.ds(0, served)]).astype(outs[0].dtype)
        return
    if local:
        pltpu.make_async_copy(near, outs[-1], ends.at[1]).start()
    if served:
        for wait in (False, True):
            @pl.loop(0, served)
            def _(i):
                @pl.when((used[i] != 0) | (not begun))
                def _():
                    copy = served_copy(i, True)
                    copy.wait() if wait else copy.start()
    if local:
        pltpu.make_async_copy(near, outs[-1], ends.at[1]).wait()


def window_sums(shard, group, served, local, hist_t, shards, sums, lanes, rows, narrow=False):
    owned, excite, depth = hist_t.shape
    pieces = [(slot, *piece) for slot, found in enumerate(shards) for piece in found]
    classes, _, panels = pieces[0][3].shape
    places = served[0].size if served else 0
    targets = owned if local else 0
    pairs = places + (local[0].size if local else 0)
    steps = depth // panels
    config = (
        places,
        bool(local),
        sums is not None,
        narrow,
        tuple(piece[:3] for piece in pieces),
        lanes * rows // panels,
        rows,
        max(first + value.shape[1] for _, _, first, value in pieces),
        targets,
    )
    operands = [jnp.stack([shard * (rows // panels), group]).astype(jnp.int32), *served, *local]
    wide = [hist_t, *[piece[3] for piece in pieces]]
    before = list(sums) if sums is not None else []
    outs = [
        jax.ShapeDtypeStruct((n, excite, panels), jnp.bfloat16 if narrow else jnp.float32)
        for n in (places, targets)
        if n
    ]
    depth_of_table = len(shards) * rows + 2 * (steps // 2 - 1) * panels
    return pl.pallas_call(
        functools.partial(window_kernel, config),
        out_shape=outs,
        in_specs=[SMEM] * len(operands) + [HBM] * (len(wide) + len(before)),
        out_specs=[VMEM if narrow else HBM] * len(outs),
        scratch_shapes=[
            pltpu.VMEM((classes, depth_of_table, panels), jnp.bfloat16),
            pltpu.VMEM(hist_t.shape, hist_t.dtype),
            pltpu.VMEM((places + targets, excite, panels), jnp.float32),
            pltpu.VMEM((places if narrow else 1, excite, panels), jnp.float32),
            pltpu.SMEM((2 * classes, pairs + 1), jnp.int32),
            pltpu.SMEM((2 * classes,), jnp.int32),
            pltpu.SMEM((max(places, 1),), jnp.int32),
            pltpu.SemaphoreType.DMA((classes,)),
            pltpu.SemaphoreType.DMA((2,)),
            pltpu.SemaphoreType.DMA((max(places, 1),)),
        ],
        input_output_aliases={} if narrow else {
            len(operands) + len(wide) + n: n for n in range(len(before))
        },
        compiler_params=pltpu.CompilerParams(vmem_limit_bytes=58 * MIB),
        cost_estimate=pl.CostEstimate(
            flops=2 * pairs * panels * depth * excite,
            bytes_accessed=2 * classes * len(shards) * rows * panels + 2 * hist_t.size,
            transcendentals=0,
        ),
    )(*operands, *wide, *before)


def update_kernel(target_ref, near_ref, recv_ref, inverse_ref, incident_ref, out_ref, total, sem):
    copy = pltpu.make_async_copy(near_ref, total, sem)
    copy.start()
    copy.wait()
    slots, peers = target_ref.shape

    @pl.loop(0, peers)
    def _(i):
        for c in range(slots):
            total[target_ref[c, i]] += recv_ref[i, c].astype(jnp.float32)

    for t in range(out_ref.shape[0]):
        residual = (incident_ref[t].astype(jnp.float32) - total[t].T).astype(jnp.bfloat16)
        out_ref[t] = jnp.dot(
            inverse_ref[t], residual, preferred_element_type=jnp.float32
        ).astype(out_ref.dtype)


def update(target, near, recv, inverse, incident):
    return pl.pallas_call(
        update_kernel,
        out_shape=jax.ShapeDtypeStruct(incident.shape, jnp.bfloat16),
        in_specs=[SMEM, HBM] + [VMEM] * 3,
        out_specs=VMEM,
        scratch_shapes=[pltpu.VMEM(near.shape, jnp.float32), pltpu.SemaphoreType.DMA],
        compiler_params=pltpu.CompilerParams(vmem_limit_bytes=32 * MIB),
    )(target, near, recv, inverse, incident)


def swap(value, bit, peers):
    return lax.ppermute(value, "grp", [(i, i ^ bit) for i in range(peers)])


def upper(value, peers):
    masks, held = [0], [value]
    bit = 8
    while bit < peers:
        masks += [mask ^ bit for mask in masks]
        held += [swap(value, bit, peers) for value in held]
        bit *= 2
    return masks, held


def with_other_core(found, peers):
    return found + [(mask ^ 1, first, swap(v, 1, peers)) for mask, first, v in found]


def per_device(
    weights,
    history,
    send_patch,
    send_lag,
    send_class,
    recv_target,
    local_src,
    local_lag,
    local_class,
    local_target,
    inverse_blocks,
    incident,
):
    classes, rows, panels = weights.shape
    peers, slots = send_patch.shape
    height = rows // peers
    group = lax.axis_index("grp")
    lane = lax.axis_index("lag")
    lanes = lax.axis_size("lag")
    ring = [(i, (i - 1) % lanes) for i in range(lanes)]
    served = (send_patch.T, send_lag.T, send_class.T)
    local = (local_src, local_lag, local_class, local_target)

    hist_t = jnp.swapaxes(history, 1, 2)
    half = height // 2

    def part(index):
        return lax.dynamic_slice(weights, (0, index * height, 0), (classes, height, panels))

    def add_shards(first, end, served, local, sums, **options):
        shard = lax.rem(lane + first, lanes)
        shards = rounds[first - 1 : end - 1]
        return window_sums(
            shard, group, served, local, hist_t, shards, [sums], lanes, rows, **options
        )[0]

    own = part(group)

    def neighbours(value):
        masks, held = upper(value, peers)
        return (
            [(m, 0, v) for m, v in zip(masks, held)],
            [(m ^ 2, 0, swap(v, 2, peers)) for m, v in zip(masks, held)],
            [(m ^ 4, 0, swap(v, 4, peers)) for m, v in zip(masks, held)],
        )

    def tie(*values):
        leaves, tree = jax.tree.flatten(values)
        arrays = lax.optimization_barrier([v for v in leaves if not isinstance(v, int)])
        return jax.tree.unflatten(
            tree, [v if isinstance(v, int) else arrays.pop(0) for v in leaves]
        )

    def corners(value):
        masks, held = upper(value, peers)
        return [(m ^ 6, 0, v) for m, v in zip(masks, held)]

    own = lax.ppermute(own, "lag", ring)
    own, hist_t, opposite = tie(own, hist_t, group ^ 6)
    corner = part(opposite)
    trio = neighbours(own)
    own, corner = tie(own, corner)
    own = lax.ppermute(own, "lag", ring)
    served_sums, near = window_sums(
        lane, group * 0, served, local, hist_t, [[(0, 0, weights)]], None, lanes, rows
    )
    trio, own, corner, served_sums, near = tie(trio, own, corner, served_sums, near)
    held, across, along = trio
    found, across = tie(with_other_core(held, peers), across)
    found += with_other_core(across, peers)
    more = with_other_core(along, peers)
    held, across, along = neighbours(own)
    more, held = tie(more, held)
    found += more
    diagonal = lax.ppermute(corner, "lag", ring)
    held = with_other_core(held, peers)
    across, along, own, diagonal, found, held = tie(across, along, own, diagonal, found, held)
    diagonal = with_other_core(corners(diagonal), peers)
    rounds = [found + diagonal]
    for step in range(2, lanes - 1):
        own = lax.ppermute(own, "lag", ring)
        if step == 2:
            rounds[0], across, along = tie(rounds[0], across, along)
        turned = [(m ^ 2, 0, swap(v[:, :half], 2, peers)) for m, _, v in along]
        turned += [(m ^ 4, half, swap(v[:, half:], 4, peers)) for m, _, v in across]
        found = held + with_other_core(across + along, peers)
        near = add_shards(step - 1, step, (), local, near)
        own, turned, near, corner, found = tie(own, turned, near, corner, found)
        held, across, along = neighbours(own)
        found, held = tie(found + with_other_core(turned, peers), held)
        rounds.append(found)
        held = with_other_core(held, peers)
        if step < lanes - 2:
            across, along, own = tie(across, along, own)
    diagonal = lax.ppermute(corner, "lag", [(j, i) for i, j in ring])
    served_sums = add_shards(1, lanes - 1, served, (), served_sums)
    across, along, diagonal, served_sums = tie(across, along, diagonal, served_sums)
    rounds.append(held + with_other_core(across + along + corners(diagonal), peers))
    contribution = add_shards(lanes - 1, lanes, served, (), served_sums, narrow=True)
    recv = lax.all_to_all(
        contribution.reshape(peers, slots, *contribution.shape[1:]),
        "grp",
        split_axis=0,
        concat_axis=0,
        tiled=True,
    )
    near = add_shards(lanes - 2, lanes, (), local, near)
    return update(recv_target.T, near, recv, inverse_blocks, incident)


def solution(mesh):
    both = ("grp", "lag")
    return jax.shard_map(
        per_device,
        mesh=mesh,
        in_specs=(
            P(None, "lag", None),
            P(both, None, None),
            P(both, None),
            P(both, None),
            P(both, None),
            P(both, None),
            P(both),
            P(both),
            P(both),
            P(both),
            P(both, None, None),
            P(both, None, None),
        ),
        out_specs=P(both, None, None),
        check_vma=False,
    )
```

```python
import functools

import jax
import jax.numpy as jnp
from jax import lax
from jax.experimental import pallas as pl
from jax.experimental.pallas import tpu as pltpu
from jax.sharding import PartitionSpec as P

SMEM = pl.BlockSpec(memory_space=pltpu.SMEM)
VMEM = pl.BlockSpec(memory_space=pltpu.VMEM)
HBM = pl.BlockSpec(memory_space=pltpu.HBM)
MIB = 1 << 20
HALF_BITS, SOURCE_BITS, CLASS_BITS, LAG_BITS = 1, 8, 4, 8
FIELDS = (HALF_BITS, SOURCE_BITS, CLASS_BITS, LAG_BITS)
UNROLL = 2


def pack(half, source, klass, lag, place):
    packed = place
    for value, bits in ((lag, LAG_BITS), (klass, CLASS_BITS), (source, SOURCE_BITS), (half, HALF_BITS)):
        packed = (packed << bits) | value
    return packed


def list_task(bases, span, steps, phased, pair, tasks, counts):
    source, klass, lag, place = pair
    half = steps // 2
    number = 2 * klass if phased else 0
    touched = None
    for slot, base in enumerate(bases):
        first = lag - base
        whole = (first > -half) & (first < span - half)
        lower = (first >= span - half) & (first < span)
        higher = (first > -steps) & (first <= -half)
        second = jnp.where(higher, 1, 0)
        row = slot * (span + half - 1) + half - 1
        at = counts[number]
        tasks[number, at] = pack(0, source, klass, jnp.maximum(row + first, 0), place)
        counts[number] = at + jnp.where(whole, 1, 0)
        at = counts[number + 1]
        begin = jnp.maximum(row + first + half * second, 0)
        tasks[number + 1, at] = pack(second, source, klass, begin, place)
        counts[number + 1] = at + jnp.where(lower | higher, 1, 0)
        active = whole | lower | higher
        touched = active if touched is None else touched | active
    return touched


def run_list(number, width, tasks, counts, hist, table, acc):
    panels = table.shape[2]

    def run(n):
        packed = tasks[number, n]
        fields = []
        for bits in FIELDS:
            fields.append(packed & ((1 << bits) - 1))
            packed = packed >> bits
        half, source, klass, lag = fields
        columns = pl.multiple_of(half * (width * panels), width * panels)
        rows = pl.multiple_of(lag * panels, panels)
        acc[packed] += jnp.dot(
            hist[source, :, pl.ds(columns, width * panels)],
            table[klass, pl.ds(rows, width * panels), :],
            preferred_element_type=jnp.float32,
        )

    count = counts[number]

    @pl.loop(0, count // UNROLL)
    def _(j):
        for n in range(UNROLL):
            run(j * UNROLL + n)

    @pl.loop(count // UNROLL * UNROLL, count)
    def _(j):
        run(j)


def window_kernel(config, *refs):
    served, local, begun, narrow, places, shards, rows, height, owned = config
    refs = list(refs)
    where = refs.pop(0)
    served_refs = [refs.pop(0) for _ in range(3 if served else 0)]
    local_refs = [refs.pop(0) for _ in range(4 if local else 0)]
    hist_ref = refs.pop(0)
    pieces = [refs.pop(0) for _ in places]
    before = [refs.pop(0) for _ in range((bool(served) + bool(local)) if begun else 0)]
    outs = [refs.pop(0) for _ in range(bool(served) + bool(local))]
    table, hist, acc, prior, tasks, counts, used, sems, ends, served_sems = refs
    group = where[0]
    bases = [where[1 + n] for n in range(shards)]
    classes, _, panels = table.shape
    steps = hist.shape[2] // panels
    margin = (steps // 2 - 1) * panels
    span = rows // panels
    phased = bool(local) or shards > 1

    pltpu.make_async_copy(hist_ref, hist, ends.at[0]).start()
    near = acc.at[pl.ds(served, owned)] if local else None
    if local and begun:
        pltpu.make_async_copy(before[-1], near, ends.at[1]).start()
    for k in range(classes):
        for (slot, mask, first), piece in zip(places, pieces):
            start = margin + slot * (rows + margin) + (group ^ mask) * height + first
            start = pl.multiple_of(start, 16)
            pltpu.make_async_copy(
                piece.at[k], table.at[k, pl.ds(start, piece.shape[1]), :], sems.at[k]
            ).start()
    if not begun or narrow:
        acc[...] = jnp.zeros_like(acc)
    ends_of_table = jnp.zeros((margin, panels), table.dtype)
    for k in range(classes):
        counts[2 * k] = 0
        counts[2 * k + 1] = 0
        for n in range(shards + 1):
            table[k, pl.ds(n * (rows + margin), margin), :] = ends_of_table

    def served_copy(i, back):
        ends_of = (acc.at[i], outs[0].at[i]) if back else (before[0].at[i], acc.at[i])
        return pltpu.make_async_copy(*ends_of, served_sems.at[i])

    prior_copy = pltpu.make_async_copy(before[0], prior, ends.at[1]) if narrow else None
    if narrow:
        prior_copy.start()

    if served:
        slots, peers = served_refs[0].shape

        @pl.loop(0, peers)
        def _(i):
            for c in range(slots):
                source, lag, klass = (ref[c, i] for ref in served_refs)
                place = i * slots + c
                pair = (source, klass, lag, place)
                touched = list_task(bases, span, steps, phased, pair, tasks, counts)
                used[place] = jnp.where(touched, 1, 0)
                if begun and not narrow:
                    @pl.when(touched)
                    def _():
                        served_copy(place, False).start()

    if local:
        @pl.loop(0, local_refs[0].shape[0])
        def _(i):
            source, lag, klass, target = (ref[i] for ref in local_refs)
            pair = (source, klass, lag, target + served)
            list_task(bases, span, steps, phased, pair, tasks, counts)

    pltpu.make_async_copy(hist_ref, hist, ends.at[0]).wait()
    if local and begun:
        pltpu.make_async_copy(before[-1], near, ends.at[1]).wait()
    if served and begun and not narrow:
        @pl.loop(0, served)
        def _(i):
            @pl.when(used[i] != 0)
            def _():
                served_copy(i, False).wait()

    def wait_class(k):
        inner = table.at[k, pl.ds(margin, shards * rows), :]
        pltpu.make_async_copy(inner, inner, sems.at[k]).wait()

    def run_lists(number):
        run_list(number, steps, tasks, counts, hist, table, acc)
        run_list(number + 1, steps // 2, tasks, counts, hist, table, acc)

    if phased:
        @pl.loop(0, classes)
        def _(k):
            wait_class(k)
            run_lists(2 * k)
    else:
        for k in range(classes):
            wait_class(k)
        run_lists(0)

    if narrow:
        prior_copy.wait()
        outs[0][...] = (prior[...] + acc[pl.ds(0, served)]).astype(outs[0].dtype)
        return
    if local:
        pltpu.make_async_copy(near, outs[-1], ends.at[1]).start()
    if served:
        for wait in (False, True):
            @pl.loop(0, served)
            def _(i):
                @pl.when((used[i] != 0) | (not begun))
                def _():
                    copy = served_copy(i, True)
                    copy.wait() if wait else copy.start()
    if local:
        pltpu.make_async_copy(near, outs[-1], ends.at[1]).wait()


def window_sums(numbers, group, served, local, hist_t, shards, sums, rows, narrow=False):
    owned, excite, depth = hist_t.shape
    pieces = [(slot, *piece) for slot, found in enumerate(shards) for piece in found]
    classes, _, panels = pieces[0][3].shape
    places = served[0].size if served else 0
    targets = owned if local else 0
    pairs = places + (local[0].size if local else 0)
    steps = depth // panels
    config = (
        places,
        bool(local),
        sums is not None,
        narrow,
        tuple(piece[:3] for piece in pieces),
        len(shards),
        rows,
        max(first + value.shape[1] for _, _, first, value in pieces),
        targets,
    )
    bases = [number * (rows // panels) for number in numbers]
    operands = [jnp.stack([group, *bases]).astype(jnp.int32), *served, *local]
    wide = [hist_t, *[piece[3] for piece in pieces]]
    before = list(sums) if sums is not None else []
    outs = [
        jax.ShapeDtypeStruct((n, excite, panels), jnp.bfloat16 if narrow else jnp.float32)
        for n in (places, targets)
        if n
    ]
    depth_of_table = len(shards) * rows + (len(shards) + 1) * (steps // 2 - 1) * panels
    return pl.pallas_call(
        functools.partial(window_kernel, config),
        out_shape=outs,
        in_specs=[SMEM] * len(operands) + [HBM] * (len(wide) + len(before)),
        out_specs=[VMEM if narrow else HBM] * len(outs),
        scratch_shapes=[
            pltpu.VMEM((classes, depth_of_table, panels), jnp.bfloat16),
            pltpu.VMEM(hist_t.shape, hist_t.dtype),
            pltpu.VMEM((places + targets, excite, panels), jnp.float32),
            pltpu.VMEM((places if narrow else 1, excite, panels), jnp.float32),
            pltpu.SMEM((2 * classes, 2 * pairs + 1), jnp.int32),
            pltpu.SMEM((2 * classes,), jnp.int32),
            pltpu.SMEM((max(places, 1),), jnp.int32),
            pltpu.SemaphoreType.DMA((classes,)),
            pltpu.SemaphoreType.DMA((2,)),
            pltpu.SemaphoreType.DMA((max(places, 1),)),
        ],
        input_output_aliases={} if narrow else {
            len(operands) + len(wide) + n: n for n in range(len(before))
        },
        compiler_params=pltpu.CompilerParams(vmem_limit_bytes=58 * MIB),
        cost_estimate=pl.CostEstimate(
            flops=2 * pairs * panels * depth * excite,
            bytes_accessed=2 * classes * len(shards) * rows * panels + 2 * hist_t.size,
            transcendentals=0,
        ),
    )(*operands, *wide, *before)


def update_kernel(target_ref, near_ref, recv_ref, inverse_ref, incident_ref, out_ref, total, sem):
    copy = pltpu.make_async_copy(near_ref, total, sem)
    copy.start()
    copy.wait()
    slots, peers = target_ref.shape

    @pl.loop(0, peers)
    def _(i):
        for c in range(slots):
            total[target_ref[c, i]] += recv_ref[i, c].astype(jnp.float32)

    for t in range(out_ref.shape[0]):
        residual = (incident_ref[t].astype(jnp.float32) - total[t].T).astype(jnp.bfloat16)
        out_ref[t] = jnp.dot(
            inverse_ref[t], residual, preferred_element_type=jnp.float32
        ).astype(out_ref.dtype)


def update(target, near, recv, inverse, incident):
    return pl.pallas_call(
        update_kernel,
        out_shape=jax.ShapeDtypeStruct(incident.shape, jnp.bfloat16),
        in_specs=[SMEM, HBM] + [VMEM] * 3,
        out_specs=VMEM,
        scratch_shapes=[pltpu.VMEM(near.shape, jnp.float32), pltpu.SemaphoreType.DMA],
        compiler_params=pltpu.CompilerParams(vmem_limit_bytes=32 * MIB),
    )(target, near, recv, inverse, incident)


def swap(value, bit, peers):
    return lax.ppermute(value, "grp", [(i, i ^ bit) for i in range(peers)])


def upper(value, peers):
    masks, held = [0], [value]
    bit = 8
    while bit < peers:
        masks += [mask ^ bit for mask in masks]
        held += [swap(value, bit, peers) for value in held]
        bit *= 2
    return masks, held


def with_other_core(found, peers):
    return found + [(mask ^ 1, first, swap(v, 1, peers)) for mask, first, v in found]


def per_device(
    weights,
    history,
    send_patch,
    send_lag,
    send_class,
    recv_target,
    local_src,
    local_lag,
    local_class,
    local_target,
    inverse_blocks,
    incident,
):
    classes, rows, panels = weights.shape
    peers, slots = send_patch.shape
    height = rows // peers
    group = lax.axis_index("grp")
    lane = lax.axis_index("lag")
    lanes = lax.axis_size("lag")
    order = list(range(0, lanes, 2)) + list(range(1, lanes, 2))[::-1]
    ring = [(order[(i + 1) % lanes], order[i]) for i in range(lanes)]

    def ahead(step):
        number = lane
        for at, to in [(i, order[(order.index(i) + step) % lanes]) for i in range(lanes)]:
            number = jnp.where(lane == at, to, number)
        return number
    served = (send_patch.T, send_lag.T, send_class.T)
    local = (local_src, local_lag, local_class, local_target)

    hist_t = jnp.swapaxes(history, 1, 2)
    half = height // 2

    def part(index):
        return lax.dynamic_slice(weights, (0, index * height, 0), (classes, height, panels))

    def add_shards(first, end, served, local, sums, **options):
        numbers = [ahead(step) for step in range(first, end)]
        shards = rounds[first - 1 : end - 1]
        return window_sums(
            numbers, group, served, local, hist_t, shards, [sums], rows, **options
        )[0]

    own = part(group)

    def neighbours(value):
        masks, held = upper(value, peers)
        return (
            [(m, 0, v) for m, v in zip(masks, held)],
            [(m ^ 2, 0, swap(v, 2, peers)) for m, v in zip(masks, held)],
            [(m ^ 4, 0, swap(v, 4, peers)) for m, v in zip(masks, held)],
        )

    def tie(*values):
        leaves, tree = jax.tree.flatten(values)
        arrays = lax.optimization_barrier([v for v in leaves if not isinstance(v, int)])
        return jax.tree.unflatten(
            tree, [v if isinstance(v, int) else arrays.pop(0) for v in leaves]
        )

    def corners(value):
        masks, held = upper(value, peers)
        return [(m ^ 6, 0, v) for m, v in zip(masks, held)]

    own = lax.ppermute(own, "lag", ring)
    own, hist_t, opposite = tie(own, hist_t, group ^ 6)
    corner = part(opposite)
    trio = neighbours(own)
    own, corner = tie(own, corner)
    own = lax.ppermute(own, "lag", ring)
    served_sums, near = window_sums(
        [lane], group * 0, served, local, hist_t, [[(0, 0, weights)]], None, rows
    )
    trio, own, corner, served_sums, near = tie(trio, own, corner, served_sums, near)
    held, across, along = trio
    found, across = tie(with_other_core(held, peers), across)
    found += with_other_core(across, peers)
    more = with_other_core(along, peers)
    held, across, along = neighbours(own)
    more, held = tie(more, held)
    found += more
    diagonal = lax.ppermute(corner, "lag", ring)
    held = with_other_core(held, peers)
    across, along, own, diagonal, found, held = tie(across, along, own, diagonal, found, held)
    diagonal = with_other_core(corners(diagonal), peers)
    rounds = [found + diagonal]
    for step in range(2, lanes - 1):
        own = lax.ppermute(own, "lag", ring)
        if step == 2:
            rounds[0], across, along = tie(rounds[0], across, along)
        turned = [(m ^ 2, 0, swap(v[:, :half], 2, peers)) for m, _, v in along]
        turned += [(m ^ 4, half, swap(v[:, half:], 4, peers)) for m, _, v in across]
        found = held + with_other_core(across + along, peers)
        near = add_shards(step - 1, step, (), local, near)
        own, turned, near, corner, found = tie(own, turned, near, corner, found)
        held, across, along = neighbours(own)
        found, held = tie(found + with_other_core(turned, peers), held)
        rounds.append(found)
        held = with_other_core(held, peers)
        if step < lanes - 2:
            across, along, own = tie(across, along, own)
    diagonal = lax.ppermute(corner, "lag", [(j, i) for i, j in ring])
    served_sums = add_shards(1, lanes - 1, served, (), served_sums)
    across, along, diagonal, served_sums = tie(across, along, diagonal, served_sums)
    rounds.append(held + with_other_core(across + along + corners(diagonal), peers))
    contribution = add_shards(lanes - 1, lanes, served, (), served_sums, narrow=True)
    recv = lax.all_to_all(
        contribution.reshape(peers, slots, *contribution.shape[1:]),
        "grp",
        split_axis=0,
        concat_axis=0,
        tiled=True,
    )
    near = add_shards(lanes - 2, lanes, (), local, near)
    return update(recv_target.T, near, recv, inverse_blocks, incident)


def solution(mesh):
    both = ("grp", "lag")
    return jax.shard_map(
        per_device,
        mesh=mesh,
        in_specs=(
            P(None, "lag", None),
            P(both, None, None),
            P(both, None),
            P(both, None),
            P(both, None),
            P(both, None),
            P(both),
            P(both),
            P(both),
            P(both),
            P(both, None, None),
            P(both, None, None),
        ),
        out_specs=P(both, None, None),
        check_vma=False,
    )
```

```python
import functools

import jax
import jax.numpy as jnp
from jax import lax
from jax.experimental import pallas as pl
from jax.experimental.pallas import tpu as pltpu
from jax.sharding import PartitionSpec as P

SMEM = pl.BlockSpec(memory_space=pltpu.SMEM)
VMEM = pl.BlockSpec(memory_space=pltpu.VMEM)
HBM = pl.BlockSpec(memory_space=pltpu.HBM)
MIB = 1 << 20
HALF_BITS, SOURCE_BITS, CLASS_BITS, LAG_BITS = 1, 8, 4, 8
FIELDS = (HALF_BITS, SOURCE_BITS, CLASS_BITS, LAG_BITS)
UNROLL = 2


def pack(half, source, klass, lag, place):
    packed = place
    for value, bits in ((lag, LAG_BITS), (klass, CLASS_BITS), (source, SOURCE_BITS), (half, HALF_BITS)):
        packed = (packed << bits) | value
    return packed


def list_task(bases, span, steps, phased, pair, tasks, counts):
    source, klass, lag, place = pair
    half = steps // 2
    number = 2 * klass if phased else 0
    touched = None
    for slot, base in enumerate(bases):
        first = lag - base
        whole = (first > -half) & (first < span - half)
        lower = (first >= span - half) & (first < span)
        higher = (first > -steps) & (first <= -half)
        second = jnp.where(higher, 1, 0)
        row = slot * (span + half - 1) + half - 1
        at = counts[number]
        tasks[number, at] = pack(0, source, klass, jnp.maximum(row + first, 0), place)
        counts[number] = at + jnp.where(whole, 1, 0)
        at = counts[number + 1]
        begin = jnp.maximum(row + first + half * second, 0)
        tasks[number + 1, at] = pack(second, source, klass, begin, place)
        counts[number + 1] = at + jnp.where(lower | higher, 1, 0)
        active = whole | lower | higher
        touched = active if touched is None else touched | active
    return touched


def run_list(number, width, tasks, counts, hist, table, acc):
    panels = table.shape[2]

    def run(n):
        packed = tasks[number, n]
        fields = []
        for bits in FIELDS:
            fields.append(packed & ((1 << bits) - 1))
            packed = packed >> bits
        half, source, klass, lag = fields
        columns = pl.multiple_of(half * (width * panels), width * panels)
        rows = pl.multiple_of(lag * panels, panels)
        acc[packed] += jnp.dot(
            hist[source, :, pl.ds(columns, width * panels)],
            table[klass, pl.ds(rows, width * panels), :],
            preferred_element_type=jnp.float32,
        )

    count = counts[number]

    @pl.loop(0, count // UNROLL)
    def _(j):
        for n in range(UNROLL):
            run(j * UNROLL + n)

    @pl.loop(count // UNROLL * UNROLL, count)
    def _(j):
        run(j)


def window_kernel(config, *refs):
    served, local, begun, narrow, places, shards, rows, height, owned = config
    refs = list(refs)
    where = refs.pop(0)
    served_refs = [refs.pop(0) for _ in range(3 if served else 0)]
    local_refs = [refs.pop(0) for _ in range(4 if local else 0)]
    hist_ref = refs.pop(0)
    pieces = [refs.pop(0) for _ in places]
    before = [refs.pop(0) for _ in range((bool(served) + bool(local)) if begun else 0)]
    outs = [refs.pop(0) for _ in range(bool(served) + bool(local))]
    table, hist, acc, prior, tasks, counts, used, sems, ends, served_sems = refs
    group = where[0]
    bases = [where[1 + n] for n in range(shards)]
    classes, _, panels = table.shape
    steps = hist.shape[2] // panels
    margin = (steps // 2 - 1) * panels
    span = rows // panels
    phased = bool(local) or shards > 1

    pltpu.make_async_copy(hist_ref, hist, ends.at[0]).start()
    near = acc.at[pl.ds(served, owned)] if local else None
    if local and begun:
        pltpu.make_async_copy(before[-1], near, ends.at[1]).start()
    for k in range(classes):
        for (slot, mask, first), piece in zip(places, pieces):
            start = margin + slot * (rows + margin) + (group ^ mask) * height + first
            start = pl.multiple_of(start, 16)
            pltpu.make_async_copy(
                piece.at[k], table.at[k, pl.ds(start, piece.shape[1]), :], sems.at[k]
            ).start()
    if not begun or narrow:
        acc[...] = jnp.zeros_like(acc)
    ends_of_table = jnp.zeros((margin, panels), table.dtype)
    for k in range(classes):
        counts[2 * k] = 0
        counts[2 * k + 1] = 0
        for n in range(shards + 1):
            table[k, pl.ds(n * (rows + margin), margin), :] = ends_of_table

    def served_copy(i, back):
        ends_of = (acc.at[i], outs[0].at[i]) if back else (before[0].at[i], acc.at[i])
        return pltpu.make_async_copy(*ends_of, served_sems.at[i])

    prior_copy = pltpu.make_async_copy(before[0], prior, ends.at[1]) if narrow else None
    if narrow:
        prior_copy.start()

    if served:
        slots, peers = served_refs[0].shape

        @pl.loop(0, peers)
        def _(i):
            for c in range(slots):
                source, lag, klass = (ref[c, i] for ref in served_refs)
                place = i * slots + c
                pair = (source, klass, lag, place)
                touched = list_task(bases, span, steps, phased, pair, tasks, counts)
                used[place] = jnp.where(touched, 1, 0)
                if begun and not narrow:
                    @pl.when(touched)
                    def _():
                        served_copy(place, False).start()

    if local:
        @pl.loop(0, local_refs[0].shape[0])
        def _(i):
            source, lag, klass, target = (ref[i] for ref in local_refs)
            pair = (source, klass, lag, target + served)
            list_task(bases, span, steps, phased, pair, tasks, counts)

    pltpu.make_async_copy(hist_ref, hist, ends.at[0]).wait()
    if local and begun:
        pltpu.make_async_copy(before[-1], near, ends.at[1]).wait()
    if served and begun and not narrow:
        @pl.loop(0, served)
        def _(i):
            @pl.when(used[i] != 0)
            def _():
                served_copy(i, False).wait()

    def wait_class(k):
        inner = table.at[k, pl.ds(margin, shards * rows), :]
        pltpu.make_async_copy(inner, inner, sems.at[k]).wait()

    def run_lists(number):
        run_list(number, steps, tasks, counts, hist, table, acc)
        run_list(number + 1, steps // 2, tasks, counts, hist, table, acc)

    if phased:
        @pl.loop(0, classes)
        def _(k):
            wait_class(k)
            run_lists(2 * k)
    else:
        for k in range(classes):
            wait_class(k)
        run_lists(0)

    if narrow:
        prior_copy.wait()
        outs[0][...] = (prior[...] + acc[pl.ds(0, served)]).astype(outs[0].dtype)
        return
    if local:
        pltpu.make_async_copy(near, outs[-1], ends.at[1]).start()
    if served:
        for wait in (False, True):
            @pl.loop(0, served)
            def _(i):
                @pl.when((used[i] != 0) | (not begun))
                def _():
                    copy = served_copy(i, True)
                    copy.wait() if wait else copy.start()
    if local:
        pltpu.make_async_copy(near, outs[-1], ends.at[1]).wait()


def window_sums(numbers, group, served, local, hist_t, shards, sums, rows, narrow=False):
    owned, excite, depth = hist_t.shape
    pieces = [(slot, *piece) for slot, found in enumerate(shards) for piece in found]
    classes, _, panels = pieces[0][3].shape
    places = served[0].size if served else 0
    targets = owned if local else 0
    pairs = places + (local[0].size if local else 0)
    steps = depth // panels
    config = (
        places,
        bool(local),
        sums is not None,
        narrow,
        tuple(piece[:3] for piece in pieces),
        len(shards),
        rows,
        max(first + value.shape[1] for _, _, first, value in pieces),
        targets,
    )
    bases = [number * (rows // panels) for number in numbers]
    operands = [jnp.stack([group, *bases]).astype(jnp.int32), *served, *local]
    wide = [hist_t, *[piece[3] for piece in pieces]]
    before = list(sums) if sums is not None else []
    outs = [
        jax.ShapeDtypeStruct((n, excite, panels), jnp.bfloat16 if narrow else jnp.float32)
        for n in (places, targets)
        if n
    ]
    depth_of_table = len(shards) * rows + (len(shards) + 1) * (steps // 2 - 1) * panels
    return pl.pallas_call(
        functools.partial(window_kernel, config),
        out_shape=outs,
        in_specs=[SMEM] * len(operands) + [HBM] * (len(wide) + len(before)),
        out_specs=[VMEM if narrow else HBM] * len(outs),
        scratch_shapes=[
            pltpu.VMEM((classes, depth_of_table, panels), jnp.bfloat16),
            pltpu.VMEM(hist_t.shape, hist_t.dtype),
            pltpu.VMEM((places + targets, excite, panels), jnp.float32),
            pltpu.VMEM((places if narrow else 1, excite, panels), jnp.float32),
            pltpu.SMEM((2 * classes, 2 * pairs + 1), jnp.int32),
            pltpu.SMEM((2 * classes,), jnp.int32),
            pltpu.SMEM((max(places, 1),), jnp.int32),
            pltpu.SemaphoreType.DMA((classes,)),
            pltpu.SemaphoreType.DMA((2,)),
            pltpu.SemaphoreType.DMA((max(places, 1),)),
        ],
        input_output_aliases={} if narrow else {
            len(operands) + len(wide) + n: n for n in range(len(before))
        },
        compiler_params=pltpu.CompilerParams(vmem_limit_bytes=58 * MIB),
        cost_estimate=pl.CostEstimate(
            flops=2 * pairs * panels * depth * excite,
            bytes_accessed=2 * classes * len(shards) * rows * panels + 2 * hist_t.size,
            transcendentals=0,
        ),
    )(*operands, *wide, *before)


def update_kernel(target_ref, near_ref, recv_ref, inverse_ref, incident_ref, out_ref, total, sem):
    copy = pltpu.make_async_copy(near_ref, total, sem)
    copy.start()
    copy.wait()
    slots, peers = target_ref.shape

    @pl.loop(0, peers)
    def _(i):
        for c in range(slots):
            total[target_ref[c, i]] += recv_ref[i, c].astype(jnp.float32)

    for t in range(out_ref.shape[0]):
        residual = (incident_ref[t].astype(jnp.float32) - total[t].T).astype(jnp.bfloat16)
        out_ref[t] = jnp.dot(
            inverse_ref[t], residual, preferred_element_type=jnp.float32
        ).astype(out_ref.dtype)


def update(target, near, recv, inverse, incident):
    return pl.pallas_call(
        update_kernel,
        out_shape=jax.ShapeDtypeStruct(incident.shape, jnp.bfloat16),
        in_specs=[SMEM, HBM] + [VMEM] * 3,
        out_specs=VMEM,
        scratch_shapes=[pltpu.VMEM(near.shape, jnp.float32), pltpu.SemaphoreType.DMA],
        compiler_params=pltpu.CompilerParams(vmem_limit_bytes=32 * MIB),
    )(target, near, recv, inverse, incident)


def swap(value, bit, peers):
    return lax.ppermute(value, "grp", [(i, i ^ bit) for i in range(peers)])


def upper(value, peers):
    masks, held = [0], [value]
    bit = 8
    while bit < peers:
        masks += [mask ^ bit for mask in masks]
        held += [swap(value, bit, peers) for value in held]
        bit *= 2
    return masks, held


def with_other_core(found, peers):
    return found + [(mask ^ 1, first, swap(v, 1, peers)) for mask, first, v in found]


def per_device(
    weights,
    history,
    send_patch,
    send_lag,
    send_class,
    recv_target,
    local_src,
    local_lag,
    local_class,
    local_target,
    inverse_blocks,
    incident,
):
    classes, rows, panels = weights.shape
    peers, slots = send_patch.shape
    height = rows // peers
    group = lax.axis_index("grp")
    lane = lax.axis_index("lag")
    lanes = lax.axis_size("lag")
    order = list(range(0, lanes, 2)) + list(range(1, lanes, 2))[::-1]
    ring = [(order[(i + 1) % lanes], order[i]) for i in range(lanes)]

    def ahead(step):
        number = lane
        for at, to in [(i, order[(order.index(i) + step) % lanes]) for i in range(lanes)]:
            number = jnp.where(lane == at, to, number)
        return number
    served = (send_patch.T, send_lag.T, send_class.T)
    local = (local_src, local_lag, local_class, local_target)

    hist_t = jnp.swapaxes(history, 1, 2)
    half = height // 2

    def part(index):
        return lax.dynamic_slice(weights, (0, index * height, 0), (classes, height, panels))

    def add_shards(first, end, served, local, sums, **options):
        numbers = [ahead(step) for step in range(first, end)]
        shards = rounds[first - 1 : end - 1]
        return window_sums(
            numbers, group, served, local, hist_t, shards, [sums], rows, **options
        )[0]

    own = part(group)

    def neighbours(value):
        masks, held = upper(value, peers)
        return (
            [(m, 0, v) for m, v in zip(masks, held)],
            [(m ^ 2, 0, swap(v, 2, peers)) for m, v in zip(masks, held)],
            [(m ^ 4, 0, swap(v, 4, peers)) for m, v in zip(masks, held)],
        )

    def tie(*values):
        leaves, tree = jax.tree.flatten(values)
        arrays = lax.optimization_barrier([v for v in leaves if not isinstance(v, int)])
        return jax.tree.unflatten(
            tree, [v if isinstance(v, int) else arrays.pop(0) for v in leaves]
        )

    def corners(value):
        masks, held = upper(value, peers)
        return [(m ^ 6, 0, v) for m, v in zip(masks, held)]

    own = lax.ppermute(own, "lag", ring)
    own, hist_t, opposite = tie(own, hist_t, group ^ 6)
    corner = part(opposite)
    trio = neighbours(own)
    own = lax.ppermute(own, "lag", ring)
    served_sums, near = window_sums(
        [lane], group * 0, served, local, hist_t, [[(0, 0, weights)]], None, rows
    )
    trio, own, corner, served_sums, near = tie(trio, own, corner, served_sums, near)
    held, across, along = trio
    found, across = tie(with_other_core(held, peers), across)
    found += with_other_core(across, peers)
    more = with_other_core(along, peers)
    held, across, along = neighbours(own)
    more, held = tie(more, held)
    found += more
    diagonal = lax.ppermute(corner, "lag", ring)
    held = with_other_core(held, peers)
    across, along, own, diagonal, found, held = tie(across, along, own, diagonal, found, held)
    diagonal = with_other_core(corners(diagonal), peers)
    rounds = [found + diagonal]
    for step in range(2, lanes - 1):
        own = lax.ppermute(own, "lag", ring)
        if step == 2:
            rounds[0], across, along = tie(rounds[0], across, along)
        turned = [(m ^ 2, 0, swap(v[:, :half], 2, peers)) for m, _, v in along]
        turned += [(m ^ 4, half, swap(v[:, half:], 4, peers)) for m, _, v in across]
        found = held + with_other_core(across + along, peers)
        near = add_shards(step - 1, step, (), local, near)
        own, turned, near, corner, found = tie(own, turned, near, corner, found)
        held, across, along = neighbours(own)
        found, held = tie(found + with_other_core(turned, peers), held)
        rounds.append(found)
        held = with_other_core(held, peers)
        if step < lanes - 2:
            across, along, own = tie(across, along, own)
    diagonal = lax.ppermute(corner, "lag", [(j, i) for i, j in ring])
    served_sums = add_shards(1, lanes - 1, served, (), served_sums)
    across, along, diagonal, served_sums = tie(across, along, diagonal, served_sums)
    rounds.append(held + with_other_core(across + along + corners(diagonal), peers))
    contribution = add_shards(lanes - 1, lanes, served, (), served_sums, narrow=True)
    recv = lax.all_to_all(
        contribution.reshape(peers, slots, *contribution.shape[1:]),
        "grp",
        split_axis=0,
        concat_axis=0,
        tiled=True,
    )
    near = add_shards(lanes - 2, lanes, (), local, near)
    return update(recv_target.T, near, recv, inverse_blocks, incident)


def solution(mesh):
    both = ("grp", "lag")
    return jax.shard_map(
        per_device,
        mesh=mesh,
        in_specs=(
            P(None, "lag", None),
            P(both, None, None),
            P(both, None),
            P(both, None),
            P(both, None),
            P(both, None),
            P(both),
            P(both),
            P(both),
            P(both),
            P(both, None, None),
            P(both, None, None),
        ),
        out_specs=P(both, None, None),
        check_vma=False,
    )
```

```python
import functools

import jax
import jax.numpy as jnp
from jax import lax
from jax.experimental import pallas as pl
from jax.experimental.pallas import tpu as pltpu
from jax.sharding import PartitionSpec as P

SMEM = pl.BlockSpec(memory_space=pltpu.SMEM)
VMEM = pl.BlockSpec(memory_space=pltpu.VMEM)
HBM = pl.BlockSpec(memory_space=pltpu.HBM)
MIB = 1 << 20
HALF_BITS, SOURCE_BITS, CLASS_BITS, LAG_BITS = 1, 8, 4, 8
FIELDS = (HALF_BITS, SOURCE_BITS, CLASS_BITS, LAG_BITS)
UNROLL = 2


def pack(half, source, klass, lag, place):
    packed = place
    for value, bits in ((lag, LAG_BITS), (klass, CLASS_BITS), (source, SOURCE_BITS), (half, HALF_BITS)):
        packed = (packed << bits) | value
    return packed


def list_task(bases, span, steps, pair, tasks, counts):
    source, klass, lag, place = pair
    half = steps // 2
    number = 2 * klass
    touched = None
    for slot, base in enumerate(bases):
        first = lag - base
        whole = (first > -half) & (first < span - half)
        lower = (first >= span - half) & (first < span)
        higher = (first > -steps) & (first <= -half)
        second = jnp.where(higher, 1, 0)
        row = slot * (span + half - 1) + half - 1
        at = counts[number]
        tasks[number, at] = pack(0, source, klass, jnp.maximum(row + first, 0), place)
        counts[number] = at + jnp.where(whole, 1, 0)
        at = counts[number + 1]
        begin = jnp.maximum(row + first + half * second, 0)
        tasks[number + 1, at] = pack(second, source, klass, begin, place)
        counts[number + 1] = at + jnp.where(lower | higher, 1, 0)
        active = whole | lower | higher
        touched = active if touched is None else touched | active
    return touched


def run_list(number, width, tasks, counts, hist, table, acc):
    panels = table.shape[2]

    def run(n):
        packed = tasks[number, n]
        fields = []
        for bits in FIELDS:
            fields.append(packed & ((1 << bits) - 1))
            packed = packed >> bits
        half, source, klass, lag = fields
        columns = pl.multiple_of(half * (width * panels), width * panels)
        rows = pl.multiple_of(lag * panels, panels)
        acc[packed] += jnp.dot(
            hist[source, :, pl.ds(columns, width * panels)],
            table[klass, pl.ds(rows, width * panels), :],
            preferred_element_type=jnp.float32,
        )

    count = counts[number]

    @pl.loop(0, count // UNROLL)
    def _(j):
        for n in range(UNROLL):
            run(j * UNROLL + n)

    @pl.loop(count // UNROLL * UNROLL, count)
    def _(j):
        run(j)


def window_kernel(config, *refs):
    served, local, begun, narrow, places, shards, rows, height, owned = config
    refs = list(refs)
    where = refs.pop(0)
    served_refs = [refs.pop(0) for _ in range(3 if served else 0)]
    local_refs = [refs.pop(0) for _ in range(4 if local else 0)]
    hist_ref = refs.pop(0)
    pieces = [refs.pop(0) for _ in places]
    before = [refs.pop(0) for _ in range((bool(served) + bool(local)) if begun else 0)]
    outs = [refs.pop(0) for _ in range(bool(served) + bool(local))]
    table, hist, acc, prior, tasks, counts, used, sems, ends, served_sems = refs
    group = where[0]
    bases = [where[1 + n] for n in range(shards)]
    classes, _, panels = table.shape
    steps = hist.shape[2] // panels
    margin = (steps // 2 - 1) * panels
    span = rows // panels

    pltpu.make_async_copy(hist_ref, hist, ends.at[0]).start()
    near = acc.at[pl.ds(served, owned)] if local else None
    if local and begun:
        pltpu.make_async_copy(before[-1], near, ends.at[1]).start()
    for k in range(classes):
        for (slot, mask, first), piece in zip(places, pieces):
            start = margin + slot * (rows + margin) + (group ^ mask) * height + first
            start = pl.multiple_of(start, 16)
            pltpu.make_async_copy(
                piece.at[k], table.at[k, pl.ds(start, piece.shape[1]), :], sems.at[k]
            ).start()
    if not begun or narrow:
        acc[...] = jnp.zeros_like(acc)
    ends_of_table = jnp.zeros((margin, panels), table.dtype)
    for k in range(classes):
        counts[2 * k] = 0
        counts[2 * k + 1] = 0
        for n in range(shards + 1):
            table[k, pl.ds(n * (rows + margin), margin), :] = ends_of_table

    def served_copy(i, back):
        ends_of = (acc.at[i], outs[0].at[i]) if back else (before[0].at[i], acc.at[i])
        return pltpu.make_async_copy(*ends_of, served_sems.at[i])

    prior_copy = pltpu.make_async_copy(before[0], prior, ends.at[1]) if narrow else None
    if narrow:
        prior_copy.start()

    if served:
        slots, peers = served_refs[0].shape

        @pl.loop(0, peers)
        def _(i):
            for c in range(slots):
                source, lag, klass = (ref[c, i] for ref in served_refs)
                place = i * slots + c
                pair = (source, klass, lag, place)
                touched = list_task(bases, span, steps, pair, tasks, counts)
                used[place] = jnp.where(touched, 1, 0)
                if begun and not narrow:
                    @pl.when(touched)
                    def _():
                        served_copy(place, False).start()

    if local:
        @pl.loop(0, local_refs[0].shape[0])
        def _(i):
            source, lag, klass, target = (ref[i] for ref in local_refs)
            pair = (source, klass, lag, target + served)
            list_task(bases, span, steps, pair, tasks, counts)

    pltpu.make_async_copy(hist_ref, hist, ends.at[0]).wait()
    if local and begun:
        pltpu.make_async_copy(before[-1], near, ends.at[1]).wait()
    if served and begun and not narrow:
        @pl.loop(0, served)
        def _(i):
            @pl.when(used[i] != 0)
            def _():
                served_copy(i, False).wait()

    def wait_class(k):
        inner = table.at[k, pl.ds(margin, shards * rows), :]
        pltpu.make_async_copy(inner, inner, sems.at[k]).wait()

    def run_lists(number):
        run_list(number, steps, tasks, counts, hist, table, acc)
        run_list(number + 1, steps // 2, tasks, counts, hist, table, acc)

    @pl.loop(0, classes)
    def _(k):
        wait_class(k)
        run_lists(2 * k)

    if narrow:
        prior_copy.wait()
        outs[0][...] = (prior[...] + acc[pl.ds(0, served)]).astype(outs[0].dtype)
        return
    if local:
        pltpu.make_async_copy(near, outs[-1], ends.at[1]).start()
    if served:
        for wait in (False, True):
            @pl.loop(0, served)
            def _(i):
                @pl.when((used[i] != 0) | (not begun))
                def _():
                    copy = served_copy(i, True)
                    copy.wait() if wait else copy.start()
    if local:
        pltpu.make_async_copy(near, outs[-1], ends.at[1]).wait()


def window_sums(numbers, group, served, local, hist_t, shards, sums, rows, narrow=False):
    owned, excite, depth = hist_t.shape
    pieces = [(slot, *piece) for slot, found in enumerate(shards) for piece in found]
    classes, _, panels = pieces[0][3].shape
    places = served[0].size if served else 0
    targets = owned if local else 0
    pairs = places + (local[0].size if local else 0)
    steps = depth // panels
    config = (
        places,
        bool(local),
        sums is not None,
        narrow,
        tuple(piece[:3] for piece in pieces),
        len(shards),
        rows,
        max(first + value.shape[1] for _, _, first, value in pieces),
        targets,
    )
    bases = [number * (rows // panels) for number in numbers]
    operands = [jnp.stack([group, *bases]).astype(jnp.int32), *served, *local]
    wide = [hist_t, *[piece[3] for piece in pieces]]
    before = list(sums) if sums is not None else []
    outs = [
        jax.ShapeDtypeStruct((n, excite, panels), jnp.bfloat16 if narrow else jnp.float32)
        for n in (places, targets)
        if n
    ]
    depth_of_table = len(shards) * rows + (len(shards) + 1) * (steps // 2 - 1) * panels
    return pl.pallas_call(
        functools.partial(window_kernel, config),
        out_shape=outs,
        in_specs=[SMEM] * len(operands) + [HBM] * (len(wide) + len(before)),
        out_specs=[VMEM if narrow else HBM] * len(outs),
        scratch_shapes=[
            pltpu.VMEM((classes, depth_of_table, panels), jnp.bfloat16),
            pltpu.VMEM(hist_t.shape, hist_t.dtype),
            pltpu.VMEM((places + targets, excite, panels), jnp.float32),
            pltpu.VMEM((places if narrow else 1, excite, panels), jnp.float32),
            pltpu.SMEM((2 * classes, 2 * pairs + 1), jnp.int32),
            pltpu.SMEM((2 * classes,), jnp.int32),
            pltpu.SMEM((max(places, 1),), jnp.int32),
            pltpu.SemaphoreType.DMA((classes,)),
            pltpu.SemaphoreType.DMA((2,)),
            pltpu.SemaphoreType.DMA((max(places, 1),)),
        ],
        input_output_aliases={} if narrow else {
            len(operands) + len(wide) + n: n for n in range(len(before))
        },
        compiler_params=pltpu.CompilerParams(vmem_limit_bytes=58 * MIB),
        cost_estimate=pl.CostEstimate(
            flops=2 * pairs * panels * depth * excite,
            bytes_accessed=2 * classes * len(shards) * rows * panels + 2 * hist_t.size,
            transcendentals=0,
        ),
    )(*operands, *wide, *before)


def update_kernel(target_ref, near_ref, recv_ref, inverse_ref, incident_ref, out_ref, total, sem):
    copy = pltpu.make_async_copy(near_ref, total, sem)
    copy.start()
    copy.wait()
    slots, peers = target_ref.shape

    @pl.loop(0, peers)
    def _(i):
        for c in range(slots):
            total[target_ref[c, i]] += recv_ref[i, c].astype(jnp.float32)

    for t in range(out_ref.shape[0]):
        residual = (incident_ref[t].astype(jnp.float32) - total[t].T).astype(jnp.bfloat16)
        out_ref[t] = jnp.dot(
            inverse_ref[t], residual, preferred_element_type=jnp.float32
        ).astype(out_ref.dtype)


def update(target, near, recv, inverse, incident):
    return pl.pallas_call(
        update_kernel,
        out_shape=jax.ShapeDtypeStruct(incident.shape, jnp.bfloat16),
        in_specs=[SMEM, HBM] + [VMEM] * 3,
        out_specs=VMEM,
        scratch_shapes=[pltpu.VMEM(near.shape, jnp.float32), pltpu.SemaphoreType.DMA],
        compiler_params=pltpu.CompilerParams(vmem_limit_bytes=32 * MIB),
    )(target, near, recv, inverse, incident)


def swap(value, bit, peers):
    return lax.ppermute(value, "grp", [(i, i ^ bit) for i in range(peers)])


def upper(value, peers):
    masks, held = [0], [value]
    bit = 8
    while bit < peers:
        masks += [mask ^ bit for mask in masks]
        held += [swap(value, bit, peers) for value in held]
        bit *= 2
    return masks, held


def with_other_core(found, peers):
    return found + [(mask ^ 1, first, swap(v, 1, peers)) for mask, first, v in found]


def per_device(
    weights,
    history,
    send_patch,
    send_lag,
    send_class,
    recv_target,
    local_src,
    local_lag,
    local_class,
    local_target,
    inverse_blocks,
    incident,
):
    classes, rows, panels = weights.shape
    peers, slots = send_patch.shape
    height = rows // peers
    group = lax.axis_index("grp")
    lane = lax.axis_index("lag")
    lanes = lax.axis_size("lag")
    order = list(range(0, lanes, 2)) + list(range(1, lanes, 2))[::-1]
    ring = [(order[(i + 1) % lanes], order[i]) for i in range(lanes)]

    def ahead(step):
        number = lane
        for at, to in [(i, order[(order.index(i) + step) % lanes]) for i in range(lanes)]:
            number = jnp.where(lane == at, to, number)
        return number
    served = (send_patch.T, send_lag.T, send_class.T)
    local = (local_src, local_lag, local_class, local_target)

    hist_t = jnp.swapaxes(history, 1, 2)
    half = height // 2

    def part(index):
        return lax.dynamic_slice(weights, (0, index * height, 0), (classes, height, panels))

    def add_shards(first, end, served, local, sums, **options):
        numbers = [ahead(step) for step in range(first, end)]
        shards = rounds[first - 1 : end - 1]
        return window_sums(
            numbers, group, served, local, hist_t, shards, [sums], rows, **options
        )[0]

    own = part(group)

    def neighbours(value):
        masks, held = upper(value, peers)
        return (
            [(m, 0, v) for m, v in zip(masks, held)],
            [(m ^ 2, 0, swap(v, 2, peers)) for m, v in zip(masks, held)],
            [(m ^ 4, 0, swap(v, 4, peers)) for m, v in zip(masks, held)],
        )

    def tie(*values):
        leaves, tree = jax.tree.flatten(values)
        arrays = lax.optimization_barrier([v for v in leaves if not isinstance(v, int)])
        return jax.tree.unflatten(
            tree, [v if isinstance(v, int) else arrays.pop(0) for v in leaves]
        )

    def corners(value):
        masks, held = upper(value, peers)
        return [(m ^ 6, 0, v) for m, v in zip(masks, held)]

    own = lax.ppermute(own, "lag", ring)
    own, hist_t = tie(own, hist_t)
    trio = neighbours(own)
    own = lax.ppermute(own, "lag", ring)
    served_sums, near = window_sums(
        [lane], group * 0, served, local, hist_t, [[(0, 0, weights)]], None, rows
    )
    opposite, near = tie(group ^ 6, near)
    corner = part(opposite)
    diagonal = lax.ppermute(corner, "lag", ring)
    trio, own, served_sums, near = tie(trio, own, served_sums, near)
    held, across, along = trio
    found, across = tie(with_other_core(held, peers), across)
    found += with_other_core(across, peers)
    more = with_other_core(along, peers)
    held, across, along = neighbours(own)
    more, held = tie(more, held)
    found += more
    held = with_other_core(held, peers)
    across, along, own, diagonal, found, held = tie(across, along, own, diagonal, found, held)
    diagonal = with_other_core(corners(diagonal), peers)
    rounds = [found + diagonal]
    for step in range(2, lanes - 1):
        own = lax.ppermute(own, "lag", ring)
        if step == 2:
            rounds[0], across, along = tie(rounds[0], across, along)
        turned = [(m ^ 2, 0, swap(v[:, :half], 2, peers)) for m, _, v in along]
        turned += [(m ^ 4, half, swap(v[:, half:], 4, peers)) for m, _, v in across]
        found = held + with_other_core(across + along, peers)
        near = add_shards(step - 1, step, (), local, near)
        own, turned, near, corner, found = tie(own, turned, near, corner, found)
        held, across, along = neighbours(own)
        found, held = tie(found + with_other_core(turned, peers), held)
        rounds.append(found)
        held = with_other_core(held, peers)
        if step < lanes - 2:
            across, along, own = tie(across, along, own)
    diagonal = lax.ppermute(corner, "lag", [(j, i) for i, j in ring])
    served_sums = add_shards(1, lanes - 1, served, (), served_sums)
    across, along, diagonal, served_sums = tie(across, along, diagonal, served_sums)
    rounds.append(held + with_other_core(across + along + corners(diagonal), peers))
    contribution = add_shards(lanes - 1, lanes, served, (), served_sums, narrow=True)
    recv = lax.all_to_all(
        contribution.reshape(peers, slots, *contribution.shape[1:]),
        "grp",
        split_axis=0,
        concat_axis=0,
        tiled=True,
    )
    near = add_shards(lanes - 2, lanes, (), local, near)
    return update(recv_target.T, near, recv, inverse_blocks, incident)


def solution(mesh):
    both = ("grp", "lag")
    return jax.shard_map(
        per_device,
        mesh=mesh,
        in_specs=(
            P(None, "lag", None),
            P(both, None, None),
            P(both, None),
            P(both, None),
            P(both, None),
            P(both, None),
            P(both),
            P(both),
            P(both),
            P(both),
            P(both, None, None),
            P(both, None, None),
        ),
        out_specs=P(both, None, None),
        check_vma=False,
    )
```

```python
import functools

import jax
import jax.numpy as jnp
from jax import lax
from jax.experimental import pallas as pl
from jax.experimental.pallas import tpu as pltpu
from jax.sharding import PartitionSpec as P

SMEM = pl.BlockSpec(memory_space=pltpu.SMEM)
VMEM = pl.BlockSpec(memory_space=pltpu.VMEM)
HBM = pl.BlockSpec(memory_space=pltpu.HBM)
MIB = 1 << 20
HALF_BITS, SOURCE_BITS, CLASS_BITS, LAG_BITS = 1, 8, 4, 8
FIELDS = (HALF_BITS, SOURCE_BITS, CLASS_BITS, LAG_BITS)
UNROLL = 2


def pack(half, source, klass, lag, place):
    packed = place
    for value, bits in ((lag, LAG_BITS), (klass, CLASS_BITS), (source, SOURCE_BITS), (half, HALF_BITS)):
        packed = (packed << bits) | value
    return packed


def list_task(bases, span, steps, phased, pair, tasks, counts):
    source, klass, lag, place = pair
    half = steps // 2
    number = 2 * klass if phased else 0
    touched = None
    for slot, base in enumerate(bases):
        first = lag - base
        whole = (first > -half) & (first < span - half)
        lower = (first >= span - half) & (first < span)
        higher = (first > -steps) & (first <= -half)
        second = jnp.where(higher, 1, 0)
        row = slot * (span + half - 1) + half - 1
        at = counts[number]
        tasks[number, at] = pack(0, source, klass, jnp.maximum(row + first, 0), place)
        counts[number] = at + jnp.where(whole, 1, 0)
        at = counts[number + 1]
        begin = jnp.maximum(row + first + half * second, 0)
        tasks[number + 1, at] = pack(second, source, klass, begin, place)
        counts[number + 1] = at + jnp.where(lower | higher, 1, 0)
        active = whole | lower | higher
        touched = active if touched is None else touched | active
    return touched


def run_list(number, width, tasks, counts, hist, table, acc):
    panels = table.shape[2]

    def run(n):
        packed = tasks[number, n]
        fields = []
        for bits in FIELDS:
            fields.append(packed & ((1 << bits) - 1))
            packed = packed >> bits
        half, source, klass, lag = fields
        columns = pl.multiple_of(half * (width * panels), width * panels)
        rows = pl.multiple_of(lag * panels, panels)
        acc[packed] += jnp.dot(
            hist[source, :, pl.ds(columns, width * panels)],
            table[klass, pl.ds(rows, width * panels), :],
            preferred_element_type=jnp.float32,
        )

    count = counts[number]

    @pl.loop(0, count // UNROLL)
    def _(j):
        for n in range(UNROLL):
            run(j * UNROLL + n)

    @pl.loop(count // UNROLL * UNROLL, count)
    def _(j):
        run(j)


def window_kernel(config, *refs):
    served, local, begun, narrow, places, shards, rows, height, owned = config
    refs = list(refs)
    where = refs.pop(0)
    served_refs = [refs.pop(0) for _ in range(3 if served else 0)]
    local_refs = [refs.pop(0) for _ in range(4 if local else 0)]
    hist_ref = refs.pop(0)
    pieces = [refs.pop(0) for _ in places]
    before = [refs.pop(0) for _ in range((bool(served) + bool(local)) if begun else 0)]
    outs = [refs.pop(0) for _ in range(bool(served) + bool(local))]
    table, hist, acc, prior, tasks, counts, used, sems, ends, served_sems = refs
    group = where[0]
    bases = [where[1 + n] for n in range(shards)]
    classes, _, panels = table.shape
    steps = hist.shape[2] // panels
    margin = (steps // 2 - 1) * panels
    span = rows // panels
    phased = bool(local) or shards > 1

    pltpu.make_async_copy(hist_ref, hist, ends.at[0]).start()
    near = acc.at[pl.ds(served, owned)] if local else None
    if local and begun:
        pltpu.make_async_copy(before[-1], near, ends.at[1]).start()
    for k in range(classes):
        for (slot, mask, first), piece in zip(places, pieces):
            start = margin + slot * (rows + margin) + (group ^ mask) * height + first
            start = pl.multiple_of(start, 16)
            pltpu.make_async_copy(
                piece.at[k], table.at[k, pl.ds(start, piece.shape[1]), :], sems.at[k]
            ).start()
    if not begun or narrow:
        acc[...] = jnp.zeros_like(acc)
    ends_of_table = jnp.zeros((margin, panels), table.dtype)
    for k in range(classes):
        counts[2 * k] = 0
        counts[2 * k + 1] = 0
        for n in range(shards + 1):
            table[k, pl.ds(n * (rows + margin), margin), :] = ends_of_table

    def served_copy(i, back):
        ends_of = (acc.at[i], outs[0].at[i]) if back else (before[0].at[i], acc.at[i])
        return pltpu.make_async_copy(*ends_of, served_sems.at[i])

    prior_copy = pltpu.make_async_copy(before[0], prior, ends.at[1]) if narrow else None
    if narrow:
        prior_copy.start()

    if served:
        slots, peers = served_refs[0].shape

        @pl.loop(0, peers)
        def _(i):
            for c in range(slots):
                source, lag, klass = (ref[c, i] for ref in served_refs)
                place = i * slots + c
                pair = (source, klass, lag, place)
                touched = list_task(bases, span, steps, phased, pair, tasks, counts)
                used[place] = jnp.where(touched, 1, 0)
                if begun and not narrow:
                    @pl.when(touched)
                    def _():
                        served_copy(place, False).start()

    if local:
        @pl.loop(0, local_refs[0].shape[0])
        def _(i):
            source, lag, klass, target = (ref[i] for ref in local_refs)
            pair = (source, klass, lag, target + served)
            list_task(bases, span, steps, phased, pair, tasks, counts)

    pltpu.make_async_copy(hist_ref, hist, ends.at[0]).wait()
    if local and begun:
        pltpu.make_async_copy(before[-1], near, ends.at[1]).wait()
    if served and begun and not narrow:
        @pl.loop(0, served)
        def _(i):
            @pl.when(used[i] != 0)
            def _():
                served_copy(i, False).wait()

    def wait_class(k):
        inner = table.at[k, pl.ds(margin, shards * rows), :]
        pltpu.make_async_copy(inner, inner, sems.at[k]).wait()

    def run_lists(number):
        run_list(number, steps, tasks, counts, hist, table, acc)
        run_list(number + 1, steps // 2, tasks, counts, hist, table, acc)

    if phased:
        @pl.loop(0, classes)
        def _(k):
            wait_class(k)
            run_lists(2 * k)
    else:
        for k in range(classes):
            wait_class(k)
        run_lists(0)

    if narrow:
        prior_copy.wait()
        outs[0][...] = (prior[...] + acc[pl.ds(0, served)]).astype(outs[0].dtype)
        return
    if local:
        pltpu.make_async_copy(near, outs[-1], ends.at[1]).start()
    if served:
        for wait in (False, True):
            @pl.loop(0, served)
            def _(i):
                @pl.when((used[i] != 0) | (not begun))
                def _():
                    copy = served_copy(i, True)
                    copy.wait() if wait else copy.start()
    if local:
        pltpu.make_async_copy(near, outs[-1], ends.at[1]).wait()


def window_sums(numbers, group, served, local, hist_t, shards, sums, rows, narrow=False):
    owned, excite, depth = hist_t.shape
    pieces = [(slot, *piece) for slot, found in enumerate(shards) for piece in found]
    classes, _, panels = pieces[0][3].shape
    places = served[0].size if served else 0
    targets = owned if local else 0
    pairs = places + (local[0].size if local else 0)
    steps = depth // panels
    config = (
        places,
        bool(local),
        sums is not None,
        narrow,
        tuple(piece[:3] for piece in pieces),
        len(shards),
        rows,
        max(first + value.shape[1] for _, _, first, value in pieces),
        targets,
    )
    bases = [number * (rows // panels) for number in numbers]
    operands = [jnp.stack([group, *bases]).astype(jnp.int32), *served, *local]
    wide = [hist_t, *[piece[3] for piece in pieces]]
    before = list(sums) if sums is not None else []
    outs = [
        jax.ShapeDtypeStruct((n, excite, panels), jnp.bfloat16 if narrow else jnp.float32)
        for n in (places, targets)
        if n
    ]
    depth_of_table = len(shards) * rows + (len(shards) + 1) * (steps // 2 - 1) * panels
    return pl.pallas_call(
        functools.partial(window_kernel, config),
        out_shape=outs,
        in_specs=[SMEM] * len(operands) + [HBM] * (len(wide) + len(before)),
        out_specs=[VMEM if narrow else HBM] * len(outs),
        scratch_shapes=[
            pltpu.VMEM((classes, depth_of_table, panels), jnp.bfloat16),
            pltpu.VMEM(hist_t.shape, hist_t.dtype),
            pltpu.VMEM((places + targets, excite, panels), jnp.float32),
            pltpu.VMEM((places if narrow else 1, excite, panels), jnp.float32),
            pltpu.SMEM((2 * classes, 2 * pairs + 1), jnp.int32),
            pltpu.SMEM((2 * classes,), jnp.int32),
            pltpu.SMEM((max(places, 1),), jnp.int32),
            pltpu.SemaphoreType.DMA((classes,)),
            pltpu.SemaphoreType.DMA((2,)),
            pltpu.SemaphoreType.DMA((max(places, 1),)),
        ],
        input_output_aliases={} if narrow else {
            len(operands) + len(wide) + n: n for n in range(len(before))
        },
        compiler_params=pltpu.CompilerParams(vmem_limit_bytes=58 * MIB),
        cost_estimate=pl.CostEstimate(
            flops=2 * pairs * panels * depth * excite,
            bytes_accessed=2 * classes * len(shards) * rows * panels + 2 * hist_t.size,
            transcendentals=0,
        ),
    )(*operands, *wide, *before)


def update_kernel(target_ref, near_ref, recv_ref, inverse_ref, incident_ref, out_ref, total, sem):
    copy = pltpu.make_async_copy(near_ref, total, sem)
    copy.start()
    copy.wait()
    slots, peers = target_ref.shape

    @pl.loop(0, peers)
    def _(i):
        for c in range(slots):
            total[target_ref[c, i]] += recv_ref[i, c].astype(jnp.float32)

    for t in range(out_ref.shape[0]):
        residual = (incident_ref[t].astype(jnp.float32) - total[t].T).astype(jnp.bfloat16)
        out_ref[t] = jnp.dot(
            inverse_ref[t], residual, preferred_element_type=jnp.float32
        ).astype(out_ref.dtype)


def update(target, near, recv, inverse, incident):
    return pl.pallas_call(
        update_kernel,
        out_shape=jax.ShapeDtypeStruct(incident.shape, jnp.bfloat16),
        in_specs=[SMEM, HBM] + [VMEM] * 3,
        out_specs=VMEM,
        scratch_shapes=[pltpu.VMEM(near.shape, jnp.float32), pltpu.SemaphoreType.DMA],
        compiler_params=pltpu.CompilerParams(vmem_limit_bytes=32 * MIB),
    )(target, near, recv, inverse, incident)


def swap(value, bit, peers):
    return lax.ppermute(value, "grp", [(i, i ^ bit) for i in range(peers)])


def upper(value, peers):
    masks, held = [0], [value]
    bit = 8
    while bit < peers:
        masks += [mask ^ bit for mask in masks]
        held += [swap(value, bit, peers) for value in held]
        bit *= 2
    return masks, held


def with_other_core(found, peers):
    return found + [(mask ^ 1, first, swap(v, 1, peers)) for mask, first, v in found]


def per_device(
    weights,
    history,
    send_patch,
    send_lag,
    send_class,
    recv_target,
    local_src,
    local_lag,
    local_class,
    local_target,
    inverse_blocks,
    incident,
):
    classes, rows, panels = weights.shape
    peers, slots = send_patch.shape
    height = rows // peers
    group = lax.axis_index("grp")
    lane = lax.axis_index("lag")
    lanes = lax.axis_size("lag")
    order = list(range(0, lanes, 2)) + list(range(1, lanes, 2))[::-1]
    ring = [(order[(i + 1) % lanes], order[i]) for i in range(lanes)]

    def ahead(step):
        number = lane
        for at, to in [(i, order[(order.index(i) + step) % lanes]) for i in range(lanes)]:
            number = jnp.where(lane == at, to, number)
        return number
    served = (send_patch.T, send_lag.T, send_class.T)
    local = (local_src, local_lag, local_class, local_target)

    hist_t = jnp.swapaxes(history, 1, 2)
    half = height // 2

    def part(index):
        return lax.dynamic_slice(weights, (0, index * height, 0), (classes, height, panels))

    def add_shards(first, end, served, local, sums, **options):
        numbers = [ahead(step) for step in range(first, end)]
        shards = rounds[first - 1 : end - 1]
        return window_sums(
            numbers, group, served, local, hist_t, shards, [sums], rows, **options
        )[0]

    own = part(group)

    def neighbours(value):
        masks, held = upper(value, peers)
        return (
            [(m, 0, v) for m, v in zip(masks, held)],
            [(m ^ 2, 0, swap(v, 2, peers)) for m, v in zip(masks, held)],
            [(m ^ 4, 0, swap(v, 4, peers)) for m, v in zip(masks, held)],
        )

    def tie(*values):
        leaves, tree = jax.tree.flatten(values)
        arrays = lax.optimization_barrier([v for v in leaves if not isinstance(v, int)])
        return jax.tree.unflatten(
            tree, [v if isinstance(v, int) else arrays.pop(0) for v in leaves]
        )

    def corners(value):
        masks, held = upper(value, peers)
        return [(m ^ 6, 0, v) for m, v in zip(masks, held)]

    own = lax.ppermute(own, "lag", ring)
    own, hist_t, opposite = tie(own, hist_t, group ^ 6)
    corner = part(opposite)
    trio = neighbours(own)
    own = lax.ppermute(own, "lag", ring)
    served_sums, near = window_sums(
        [lane], group * 0, served, local, hist_t, [[(0, 0, weights)]], None, rows
    )
    corner, near = tie(corner, near)
    diagonal = lax.ppermute(corner, "lag", ring)
    trio, own, served_sums, near = tie(trio, own, served_sums, near)
    held, across, along = trio
    found, across = tie(with_other_core(held, peers), across)
    found += with_other_core(across, peers)
    more = with_other_core(along, peers)
    held, across, along = neighbours(own)
    more, held = tie(more, held)
    found += more
    held = with_other_core(held, peers)
    across, along, own, diagonal, found, held = tie(across, along, own, diagonal, found, held)
    diagonal = with_other_core(corners(diagonal), peers)
    rounds = [found + diagonal]
    for step in range(2, lanes - 1):
        own = lax.ppermute(own, "lag", ring)
        if step == 2:
            rounds[0], across, along = tie(rounds[0], across, along)
        turned = [(m ^ 2, 0, swap(v[:, :half], 2, peers)) for m, _, v in along]
        turned += [(m ^ 4, half, swap(v[:, half:], 4, peers)) for m, _, v in across]
        found = held + with_other_core(across + along, peers)
        near = add_shards(step - 1, step, (), local, near)
        own, turned, near, corner, found = tie(own, turned, near, corner, found)
        held, across, along = neighbours(own)
        found, held = tie(found + with_other_core(turned, peers), held)
        rounds.append(found)
        held = with_other_core(held, peers)
        if step < lanes - 2:
            across, along, own = tie(across, along, own)
    diagonal = lax.ppermute(corner, "lag", [(j, i) for i, j in ring])
    served_sums = add_shards(1, lanes - 1, served, (), served_sums)
    across, along, diagonal, served_sums = tie(across, along, diagonal, served_sums)
    rounds.append(held + with_other_core(across + along + corners(diagonal), peers))
    contribution = add_shards(lanes - 1, lanes, served, (), served_sums, narrow=True)
    recv = lax.all_to_all(
        contribution.reshape(peers, slots, *contribution.shape[1:]),
        "grp",
        split_axis=0,
        concat_axis=0,
        tiled=True,
    )
    near = add_shards(lanes - 2, lanes, (), local, near)
    return update(recv_target.T, near, recv, inverse_blocks, incident)


def solution(mesh):
    both = ("grp", "lag")
    return jax.shard_map(
        per_device,
        mesh=mesh,
        in_specs=(
            P(None, "lag", None),
            P(both, None, None),
            P(both, None),
            P(both, None),
            P(both, None),
            P(both, None),
            P(both),
            P(both),
            P(both),
            P(both),
            P(both, None, None),
            P(both, None, None),
        ),
        out_specs=P(both, None, None),
        check_vma=False,
    )
```
